32 devices in a mesh: layer: 8 (over y, x, core), latent: 4 (over z).
Axes of the slice: x: 2, y: 2, z: 4, core: 2. Of those that a mesh axis runs over, the one named last changes fastest.
Arguments:
- layer_input: bfloat16 [8, 1024, 4096], P('layer', None, 'latent'), may hold values from -6 to 6
- enc_weight: bfloat16 [8, 4096, 512], P('layer', None, 'latent'), may hold values from -0.09375 to 0.09375
- enc_bias: float32 [8, 512], P('layer', 'latent'), may hold values from -3 to 3
- dec_weight: bfloat16 [8, 3, 512, 4096], P('layer', None, None, 'latent'), may hold values from -0.5 to 0.5
- block_lists: int32 [8, 16, 2], P('layer'), may hold values from 0 to 3, as said below
- block_counts: int32 [8, 16], P('layer'), may hold values from 1 to 2, as said below
Outputs:
- rebuilt: bfloat16 [8, 1024, 4096], P('layer', None, 'latent')
The draws below stay inside these ranges and needn't reach their ends.
Inputs may be any that keep to these rules, and one draw needn't show every extreme that they name: `block_lists`: each list holds distinct block ids of one layer. `block_counts`: some entry equals 2 in every draw.
All inputs are finite; a program needn't handle non-finite values.
Results may differ from the reference program's by a relative error of at most 0.0055.
Values may be sent and summed in bfloat16 or wider, within the bound.
No kernel may reach another device: no remote copies, remote signals or barrier semaphores. Data moves between devices by JAX's collectives and lax.ppermute only.
A program may use at most 128 MiB of HBM per device.

```python
import jax
import jax.numpy as jnp
from jax import lax

D = 4096
BLK = 128
TILE = 64
SPAN = 3
TOK = 1024
LAYERS = 8
BLOCKS = 4
LATR = 512
KMAX = 2
TILES = 16


def draw_block_lists(key, part):
    keys = jax.random.split(key, LAYERS * TILES)
    orders = jax.vmap(lambda single: jax.random.permutation(single, BLOCKS))(keys)
    return orders[:, :KMAX].reshape(LAYERS, TILES, KMAX).astype(jnp.int32)


def draw_block_counts(key, part):
    counts = jax.random.randint(key, (LAYERS * TILES,), 1, KMAX + 1)
    where_full = jax.random.randint(jax.random.fold_in(key, 7), (), 0, LAYERS * TILES)
    counts = counts.at[where_full].set(KMAX)
    return counts.reshape(LAYERS, TILES).astype(jnp.int32)


def levels(key, shape, shards, smallest, high):
    level = 1.0
    for dim, blocks in shards:
        heights = jax.random.uniform(jax.random.fold_in(jax.random.fold_in(key, 6), dim), (blocks,), jnp.float32, smallest / len(shards), high / len(shards))
        level = level * jnp.repeat(jnp.exp(heights), shape[dim] // blocks).reshape((-1,) + (1,) * (len(shape) - 1 - dim))
    return level


def gaussian(stream_key, shape, scale, reach, pieces=(), dtype=jnp.bfloat16):
    array = scale * jax.random.normal(stream_key, shape, jnp.float32)
    if pieces:
        array = array * levels(stream_key, shape, pieces, -0.22, 0.18)
    return jnp.clip(array, -reach, reach).astype(dtype)


def setup_inputs(seed: int = 0) -> dict:
    seeds = jax.random.split(jax.random.key(seed), 7)
    return {
        "layer_input": gaussian(seeds[0], (LAYERS, TOK, D), 1.0, 6.0, ((0, 8), (2, 4))),
        "enc_weight": gaussian(seeds[1], (LAYERS, D, LATR), D ** -0.5, 0.09375, ((0, 8), (2, 4))),
        "enc_bias": gaussian(seeds[2], (LAYERS, LATR), 0.5, 3.0, ((0, 8), (1, 4)), jnp.float32),
        "dec_weight": gaussian(seeds[3], (LAYERS, SPAN, LATR, D), (LATR // 4) ** -0.5, 0.5, ((0, 8), (3, 4))),
        "block_lists": draw_block_lists(jax.random.fold_in(seeds[6], 71), 0),
        "block_counts": draw_block_counts(jax.random.fold_in(seeds[6], 71), 0),
    }


def reference(layer_input, enc_weight, enc_bias, dec_weight, block_lists, block_counts):
    slot_ids = jnp.arange(KMAX)
    block_ids = jnp.arange(BLOCKS)
    rebuilt = jnp.zeros((LAYERS, TOK, D), jnp.float32)
    for source in range(LAYERS):
        preact = jnp.dot(layer_input[source], enc_weight[source], preferred_element_type=jnp.float32) + enc_bias[source][None, :]
        matched = (block_lists[source][:, :, None] == block_ids[None, None, :]) & (slot_ids[None, :, None] < block_counts[source][:, None, None])
        live = jnp.any(matched, axis=1).astype(jnp.float32)
        row_mask = jnp.repeat(jnp.repeat(live, TILE, axis=0), BLK, axis=1)
        latent_act = (jnp.maximum(preact, 0.0) * row_mask).astype(jnp.bfloat16)
        for offset in range(SPAN):
            if source + offset < LAYERS:
                term = jnp.dot(latent_act, dec_weight[source, offset], preferred_element_type=jnp.float32)
                if offset > 0:
                    term = lax.optimization_barrier(term.astype(jnp.bfloat16)).astype(jnp.float32)
                rebuilt = rebuilt.at[source + offset].add(term)
    return rebuilt.astype(jnp.bfloat16)
```

```python
import functools

import jax
import jax.numpy as jnp
from jax import lax
from jax.experimental import pallas as pl
from jax.experimental.pallas import tpu as pltpu
from jax.sharding import PartitionSpec as P

VMEM = pl.BlockSpec(memory_space=pltpu.VMEM)
SMEM = pl.BlockSpec(memory_space=pltpu.SMEM)


def rotated(value, steps):
    count = lax.axis_size("latent")
    return lax.ppermute(value, "latent", [(i, (i + steps) % count) for i in range(count)])


def passed_along(value, steps):
    count = lax.axis_size("layer")
    return lax.ppermute(value, "layer", [(i, i + steps) for i in range(count - steps)])


def encode_kernel(parts, place_ref, relative_ref, bias_ref, x_ref, *refs):
    weight_refs, refs = refs[:parts], refs[parts:]
    out_refs, (wide, partial) = refs[:parts], refs[parts:]
    width = bias_ref.shape[1]
    tiles, slots, rows, _ = out_refs[0].shape
    group_rows = tiles * rows
    for source in range(parts):
        wide[:, source * width : (source + 1) * width] = weight_refs[source][...]
    for step in range(parts):
        group = lax.rem(place_ref[0] + step, parts)
        first = pl.multiple_of(group * group_rows, group_rows)
        product = jnp.dot(x_ref[pl.ds(first, group_rows), :], wide[...], preferred_element_type=jnp.float32)
        for source in range(parts):
            block = product[:, source * width : (source + 1) * width]
            partial[source] = block + bias_ref[...] if source == 0 else block
        for tile in range(tiles):
            for slot in range(slots):
                source = relative_ref[group * tiles + tile, slot]
                kept = partial[source, tile * rows : (tile + 1) * rows, :]
                out_refs[step][tile, slot] = kept.astype(out_refs[step].dtype)


def encode(place, relative, bias, x, weights, tiles):
    parts = len(weights)
    tokens, depth = x.shape
    width = bias.shape[1]
    shape = (tiles // parts, relative.shape[1], tokens // tiles, width)
    return pl.pallas_call(
        functools.partial(encode_kernel, parts),
        out_shape=[jax.ShapeDtypeStruct(shape, jnp.bfloat16 if step else jnp.float32) for step in range(parts)],
        in_specs=[SMEM, SMEM] + [VMEM] * (2 + parts),
        out_specs=[VMEM] * parts,
        scratch_shapes=[
            pltpu.VMEM((depth, parts * width), jnp.bfloat16),
            pltpu.VMEM((parts, tokens // parts, width), jnp.float32),
        ],
        compiler_params=pltpu.CompilerParams(vmem_limit_bytes=40 << 20),
        cost_estimate=pl.CostEstimate(
            flops=2 * tokens * depth * parts * width,
            bytes_accessed=2 * (tokens * depth + depth * parts * width),
            transcendentals=0,
        ),
        name="encode",
    )(place, relative, bias, x, *weights)


def decode_kernel(parts, targets, place_ref, lists_ref, *refs):
    act_refs, refs = refs[: parts * targets], refs[parts * targets :]
    decoder_refs, (out_ref, dense) = refs[:targets], refs[targets:]
    tiles, slots, rows, width = act_refs[0].shape
    step = pl.program_id(0)
    group = lax.rem(place_ref[0] - step + parts, parts)
    dense[...] = jnp.zeros_like(dense)
    for origin in range(parts):

        @pl.when(step == origin)
        def _():
            for offset in range(targets):
                for tile in range(tiles):
                    for slot in range(slots):
                        block = lists_ref[offset, group * tiles + tile, slot]
                        lanes = pl.ds(pl.multiple_of(block * width, width), width)
                        dense[offset, tile * rows : (tile + 1) * rows, lanes] = act_refs[offset * parts + origin][tile, slot]

    total = jnp.dot(dense[0], decoder_refs[0][...], preferred_element_type=jnp.float32)
    for offset in range(1, targets):
        total = total + jnp.dot(dense[offset], decoder_refs[offset][...], preferred_element_type=jnp.float32)
    out_ref[...] = total.astype(out_ref.dtype)


def decode(place, lists, acts, decoders, tokens):
    targets, parts = len(acts), len(acts[0])
    latents, features = decoders[0].shape
    group_rows = tokens // parts
    return pl.pallas_call(
        functools.partial(decode_kernel, parts, targets),
        grid_spec=pltpu.PrefetchScalarGridSpec(
            num_scalar_prefetch=2,
            grid=(parts,),
            in_specs=[VMEM] * (targets * parts + targets),
            out_specs=pl.BlockSpec(
                (group_rows, features),
                lambda step, place_ref, lists_ref: (lax.rem(place_ref[0] - step + parts, parts), 0),
            ),
            scratch_shapes=[pltpu.VMEM((targets, group_rows, latents), jnp.bfloat16)],
        ),
        out_shape=jax.ShapeDtypeStruct((tokens, features), jnp.bfloat16),
        compiler_params=pltpu.CompilerParams(vmem_limit_bytes=40 << 20),
        cost_estimate=pl.CostEstimate(
            flops=2 * tokens * latents * features * targets,
            bytes_accessed=2 * (targets * latents * features + 2 * tokens * features),
            transcendentals=0,
        ),
        name="decode",
    )(place, lists, *[part for act in acts for part in act], *decoders)


def shards(layer_input, enc_weight, enc_bias, dec_weight, block_lists, block_counts):
    parts = lax.axis_size("latent")
    place = lax.axis_index("latent")
    x, encoder, decoder = layer_input[0], enc_weight[0], dec_weight[0]
    lists, counts = block_lists[0], block_counts[0]
    tokens, depth = x.shape
    tiles, slots = lists.shape
    targets = decoder.shape[0]

    with jax.named_scope("encoder_rows"):
        pieces = [
            lax.dynamic_slice_in_dim(encoder, lax.rem(place + step, parts) * depth, depth) for step in range(parts)
        ]
        weights = [pieces[0]] + [rotated(pieces[step], step) for step in range(1, parts)]
    with jax.named_scope("decoder_weights"):
        decoders = [decoder[0]] + [passed_along(decoder[offset], offset) for offset in range(1, targets)]
        all_lists = jnp.stack([lists] + [passed_along(lists, offset) for offset in range(1, targets)])

    with jax.named_scope("encode"):
        where = place.astype(jnp.int32)[None]
        relative = lax.rem(place - lists + parts, parts)
        partials = encode(where, relative, enc_bias, x, weights, tiles)
        arrived = [rotated(partials[step], step) for step in range(1, parts)]
    with jax.named_scope("activate"):
        preact = partials[0]
        for term in arrived:
            preact = preact + term.astype(jnp.float32)
        own_counts = lax.dynamic_slice_in_dim(counts, place * (tiles // parts), tiles // parts)
        live = (jnp.arange(slots)[None, :] < own_counts[:, None]).astype(jnp.float32)
        act = (jnp.maximum(preact, 0.0) * live[:, :, None, None]).astype(jnp.bfloat16)
    with jax.named_scope("spread"):
        acts = [[act] + [rotated(act, step) for step in range(1, parts)]]
        for offset in range(1, targets):
            acts.append([passed_along(part, offset) for part in acts[0]])
    with jax.named_scope("decode"):
        return decode(where, all_lists, acts, decoders, tokens)[None]


def solution(mesh):
    placed = (
        P("layer", None, "latent"),
        P("layer", None, "latent"),
        P("layer", "latent"),
        P("layer", None, None, "latent"),
        P("layer", None, None),
        P("layer", None),
    )
    return jax.shard_map(
        shards, mesh=mesh, in_specs=placed, out_specs=P("layer", None, "latent"), check_vma=False
    )
```

```python
import functools

import jax
import jax.numpy as jnp
from jax import lax
from jax.experimental import pallas as pl
from jax.experimental.pallas import tpu as pltpu
from jax.sharding import PartitionSpec as P

VMEM = pl.BlockSpec(memory_space=pltpu.VMEM)
SMEM = pl.BlockSpec(memory_space=pltpu.SMEM)


def rotated(value, steps):
    count = lax.axis_size("latent")
    return lax.ppermute(value, "latent", [(i, (i + steps) % count) for i in range(count)])


def passed_along(value, steps):
    count = lax.axis_size("layer")
    return lax.ppermute(value, "layer", [(i, i + steps) for i in range(count - steps)])


def encode_kernel(place_ref, lists_ref, bias_ref, x_ref, weights_ref, own_ref, sent_ref, wide, partial):
    parts, tiles, slots, rows, width = sent_ref.shape
    group_rows = tiles * rows
    for block in range(parts):
        wide[:, block * width : (block + 1) * width] = weights_ref[block]
    for group in range(parts):
        product = jnp.dot(
            x_ref[group * group_rows : (group + 1) * group_rows, :], wide[...], preferred_element_type=jnp.float32
        )
        for block in range(parts):
            here = (place_ref[0] == block).astype(jnp.float32)
            partial[block] = product[:, block * width : (block + 1) * width] + here * bias_ref[...]
        for tile in range(tiles):
            for slot in range(slots):
                block = lists_ref[group * tiles + tile, slot]
                kept = partial[block, tile * rows : (tile + 1) * rows, :]
                sent_ref[group, tile, slot] = kept.astype(sent_ref.dtype)

                @pl.when(place_ref[0] == group)
                def _():
                    own_ref[tile, slot] = kept


def encode(place, lists, bias, x, weights):
    parts, depth, width = weights.shape
    tokens = x.shape[0]
    tiles, slots = lists.shape
    shape = (tiles // parts, slots, tokens // tiles, width)
    return pl.pallas_call(
        encode_kernel,
        out_shape=[jax.ShapeDtypeStruct(shape, jnp.float32), jax.ShapeDtypeStruct((parts,) + shape, jnp.bfloat16)],
        in_specs=[SMEM, SMEM] + [VMEM] * 3,
        out_specs=[VMEM] * 2,
        scratch_shapes=[
            pltpu.VMEM((depth, parts * width), jnp.bfloat16),
            pltpu.VMEM((parts, tokens // parts, width), jnp.float32),
        ],
        compiler_params=pltpu.CompilerParams(vmem_limit_bytes=40 << 20),
        cost_estimate=pl.CostEstimate(
            flops=2 * tokens * depth * parts * width,
            bytes_accessed=2 * (tokens * depth + depth * parts * width),
            transcendentals=0,
        ),
        name="encode",
    )(place, lists, bias, x, weights)


def decode_kernel(parts, targets, place_ref, lists_ref, *refs):
    first_refs, rest_refs = refs[:targets], refs[targets : 2 * targets]
    decoder_refs, (out_ref, dense) = refs[2 * targets : 3 * targets], refs[3 * targets :]
    tiles, slots, rows, width = first_refs[0].shape
    latents = dense.shape[1] // targets
    columns = out_ref.shape[1]
    step = pl.program_id(0)

    @pl.when(step == 0)
    def _():
        dense[...] = jnp.zeros_like(dense)
        for offset in range(targets):
            for origin in range(parts):
                group = lax.rem(place_ref[0] - origin + parts, parts)
                for tile in range(tiles):
                    row = pl.multiple_of((group * tiles + tile) * rows, rows)
                    for slot in range(slots):
                        block = lists_ref[offset, group * tiles + tile, slot]
                        lane = pl.multiple_of(offset * latents + block * width, width)
                        if origin:
                            kept = rest_refs[offset][(origin - 1) * tiles + tile, slot]
                        else:
                            kept = first_refs[offset][tile, slot]
                        dense[pl.ds(row, rows), pl.ds(lane, width)] = kept

    lanes = pl.ds(pl.multiple_of(step * columns, columns), columns)
    stacked = jnp.concatenate([decoder[:latents, lanes] for decoder in decoder_refs], axis=0)
    out_ref[...] = jnp.dot(dense[...], stacked, preferred_element_type=jnp.float32).astype(out_ref.dtype)


def decode(place, lists, firsts, rests, decoders, tokens, latents):
    targets = len(firsts)
    features = decoders[0].shape[1]
    columns = features // max(features // 256, 1)
    parts = tokens // (firsts[0].shape[0] * firsts[0].shape[2])
    return pl.pallas_call(
        functools.partial(decode_kernel, parts, targets),
        grid_spec=pltpu.PrefetchScalarGridSpec(
            num_scalar_prefetch=2,
            grid=(features // columns,),
            in_specs=[VMEM] * (3 * targets),
            out_specs=pl.BlockSpec((tokens, columns), lambda step, place_ref, lists_ref: (0, step)),
            scratch_shapes=[pltpu.VMEM((tokens, targets * latents), jnp.bfloat16)],
        ),
        out_shape=jax.ShapeDtypeStruct((tokens, features), jnp.bfloat16),
        compiler_params=pltpu.CompilerParams(vmem_limit_bytes=40 << 20),
        cost_estimate=pl.CostEstimate(
            flops=2 * tokens * latents * features * targets,
            bytes_accessed=2 * (targets * latents * features + 2 * tokens * features),
            transcendentals=0,
        ),
        name="decode",
    )(place, lists, *firsts, *rests, *decoders)


def with_lists(decoder, lists):
    tiles, slots = lists.shape
    ids = jnp.pad(lists.astype(decoder.dtype), ((0, -tiles % 16), (0, decoder.shape[1] - slots)))
    return jnp.concatenate([decoder, ids], axis=0)


def shards(layer_input, enc_weight, enc_bias, dec_weight, block_lists, block_counts):
    parts = lax.axis_size("latent")
    place = lax.axis_index("latent")
    x, encoder, decoder = layer_input[0], enc_weight[0], dec_weight[0]
    lists, counts = block_lists[0], block_counts[0]
    tokens, depth = x.shape
    width = encoder.shape[1]
    tiles, slots = lists.shape
    targets, latents, _ = decoder.shape

    with jax.named_scope("encoder_rows"):
        weights = lax.all_to_all(encoder.reshape(parts, depth, width), "latent", 0, 0)
    with jax.named_scope("decoder_weights"):
        decoders, all_lists = [decoder[0]], [lists]
        for offset in range(1, targets):
            arrived = passed_along(with_lists(decoder[offset], lists), offset)
            decoders.append(arrived)
            all_lists.append(arrived[latents : latents + tiles, :slots].astype(jnp.int32))

    with jax.named_scope("encode"):
        where = place.astype(jnp.int32)[None]
        own, sent = encode(where, lists, enc_bias, x, weights)
        arrived = lax.all_to_all(sent, "latent", 0, 0)
    with jax.named_scope("activate"):
        preact = own
        for origin in range(parts):
            preact = preact + jnp.where(place == origin, 0.0, arrived[origin].astype(jnp.float32))
        own_counts = lax.dynamic_slice_in_dim(counts, place * (tiles // parts), tiles // parts)
        live = (jnp.arange(slots)[None, :] < own_counts[:, None]).astype(jnp.float32)
        act = (jnp.maximum(preact, 0.0) * live[:, :, None, None]).astype(jnp.bfloat16)
    with jax.named_scope("spread"):
        rest = jnp.concatenate([rotated(act, step) for step in range(1, parts)], axis=0)
        firsts = [act] + [passed_along(act, offset) for offset in range(1, targets)]
        rest, firsts = lax.optimization_barrier((rest, firsts))
        rests = [rest] + [passed_along(rest, offset) for offset in range(1, targets)]
    with jax.named_scope("decode"):
        return decode(where, jnp.stack(all_lists), firsts, rests, decoders, tokens, latents)[None]


def solution(mesh):
    placed = (
        P("layer", None, "latent"),
        P("layer", None, "latent"),
        P("layer", "latent"),
        P("layer", None, None, "latent"),
        P("layer", None, None),
        P("layer", None),
    )
    return jax.shard_map(
        shards, mesh=mesh, in_specs=placed, out_specs=P("layer", None, "latent"), check_vma=False
    )
```

```python
import functools

import jax
import jax.numpy as jnp
from jax import lax
from jax.experimental import pallas as pl
from jax.experimental.pallas import tpu as pltpu
from jax.sharding import PartitionSpec as P

VMEM = pl.BlockSpec(memory_space=pltpu.VMEM)
SMEM = pl.BlockSpec(memory_space=pltpu.SMEM)
ANY = pl.BlockSpec(memory_space=pl.ANY)


def swapped(value, step):
    count = lax.axis_size("latent")
    return lax.ppermute(value, "latent", [(i, i ^ step) for i in range(count)])


def passed_along(value, steps):
    count = lax.axis_size("layer")
    return lax.ppermute(value, "layer", [(i, i + steps) for i in range(count - steps)])


def across_cores(value):
    count = lax.axis_size("layer")
    return lax.ppermute(value, "layer", [(i, i ^ 1) for i in range(count)])


def doubling(parts):
    if parts & (parts - 1):
        raise ValueError("latent axis")
    steps, held = [], [0]
    while len(held) < parts:
        steps.append(parts // (2 * len(held)))
        held = held + [distance ^ steps[-1] for distance in held]
    return steps, held


def fetch_rows_kernel(place_ref, encoder_ref, *refs):
    piece_refs, sems = refs[:-1], refs[-1]
    depth = piece_refs[0].shape[0]
    copies = []
    for step in range(len(piece_refs)):
        first = pl.multiple_of(lax.bitwise_xor(place_ref[0], step) * depth, depth)
        copies.append(pltpu.make_async_copy(encoder_ref.at[pl.ds(first, depth)], piece_refs[step], sems.at[step]))
        copies[-1].start()
    for copy in copies:
        copy.wait()


def fetch_rows(place, encoder, parts):
    depth = encoder.shape[0] // parts
    return pl.pallas_call(
        fetch_rows_kernel,
        out_shape=[jax.ShapeDtypeStruct((depth, encoder.shape[1]), encoder.dtype)] * parts,
        in_specs=[SMEM, ANY],
        out_specs=[ANY] * parts,
        scratch_shapes=[pltpu.SemaphoreType.DMA((parts,))],
        compiler_params=pltpu.CompilerParams(vmem_limit_bytes=60 << 20),
        name="fetch_rows",
    )(place, encoder)


def fetch_kernel(source_ref, out_ref, sem):
    copy = pltpu.make_async_copy(source_ref, out_ref, sem)
    copy.start()
    copy.wait()


def fetch(value):
    return pl.pallas_call(
        fetch_kernel,
        out_shape=jax.ShapeDtypeStruct(value.shape, value.dtype),
        in_specs=[ANY],
        out_specs=VMEM,
        scratch_shapes=[pltpu.SemaphoreType.DMA],
        compiler_params=pltpu.CompilerParams(vmem_limit_bytes=48 << 20),
        name="fetch",
    )(value)


def with_lists(decoder, lists):
    tiles, slots = lists.shape
    ids = jnp.pad(lists.astype(decoder.dtype), ((0, -tiles % 16), (0, decoder.shape[1] - slots)))
    return jnp.concatenate([decoder, ids], axis=0)


def encode_kernel(parts, place_ref, relative_ref, bias_ref, x_ref, *refs):
    weight_refs, refs = refs[:parts], refs[parts:]
    out_refs, partial = refs[:parts], refs[parts]
    width = bias_ref.shape[1]
    tiles, slots, rows, _ = out_refs[0].shape
    pair = 1 + (parts > 1)
    for first in range(0, parts, pair):
        stacked = jnp.concatenate([ref[...] for ref in weight_refs[first : first + pair]], axis=1)
        product = jnp.dot(x_ref[...], stacked, preferred_element_type=jnp.float32)
        for source in range(first, first + pair):
            block = product[:, (source - first) * width : (source - first + 1) * width]
            partial[source] = block if source else block + bias_ref[...]
    for step in range(parts):
        group = lax.bitwise_xor(place_ref[0], step)
        for tile in range(tiles):
            first = pl.multiple_of((group * tiles + tile) * rows, rows)
            for slot in range(slots):
                source = relative_ref[group * tiles + tile, slot]
                out_refs[step][tile, slot] = partial[source, pl.ds(first, rows), :].astype(out_refs[step].dtype)


def encode(place, relative, bias, x, weights, tiles):
    parts = len(weights)
    tokens, depth = x.shape
    width = bias.shape[1]
    shape = (tiles // parts, relative.shape[1], tokens // tiles, width)
    return pl.pallas_call(
        functools.partial(encode_kernel, parts),
        out_shape=[jax.ShapeDtypeStruct(shape, jnp.bfloat16 if step else jnp.float32) for step in range(parts)],
        in_specs=[SMEM, SMEM] + [VMEM] * (2 + parts),
        out_specs=[VMEM] * parts,
        scratch_shapes=[pltpu.VMEM((parts, tokens, width), jnp.float32)],
        compiler_params=pltpu.CompilerParams(vmem_limit_bytes=24 << 20),
        cost_estimate=pl.CostEstimate(
            flops=2 * tokens * depth * parts * width,
            bytes_accessed=2 * (tokens * depth + depth * parts * width),
            transcendentals=0,
        ),
        name="encode",
    )(place, relative, bias, x, *weights)


def expand(dense, lists_ref, offset, groups_ref, first, act_ref):
    tiles_held, slots, rows, width = act_ref.shape
    tiles = lists_ref.shape[1] // groups_ref.shape[0]
    for held in range(tiles_held):
        for slot in range(slots):
            block = lists_ref[offset, groups_ref[first + held // tiles] * tiles + held % tiles, slot]
            lanes = pl.ds(pl.multiple_of(block * width, width), width)
            dense[held * rows : (held + 1) * rows, lanes] = act_ref[held, slot]


def column_tiles(features):
    columns = 256 if features % 256 == 0 else features
    return [slice(first, first + columns) for first in range(0, features, columns)]


def send_out(stage, out_ref, sems, groups_ref, first, rows, number, lanes):
    copies = []
    for held in range(stage.shape[0] // rows):
        row = pl.multiple_of(groups_ref[first + held] * rows, rows)
        copies.append(
            pltpu.make_async_copy(
                stage.at[held * rows : (held + 1) * rows, lanes],
                out_ref.at[pl.ds(row, rows), lanes],
                sems.at[number, held],
            )
        )
        copies[-1].start()
    return copies


def early_kernel(groups_ref, lists_ref, own_early, own_late, near, far, own_dec, near_dec, far_dec, *refs):
    out_ref, partial_ref, own, others, stage, sems = refs
    half, latents = others[0].shape
    rows = half * 2 // groups_ref.shape[0]
    own[...] = jnp.zeros_like(own)
    others[...] = jnp.zeros_like(others)
    held = groups_ref.shape[0] // 2
    expand(own.at[:half], lists_ref, 0, groups_ref, 0, own_early)
    expand(own.at[half:], lists_ref, 0, groups_ref, held, own_late)
    expand(others.at[0], lists_ref, 1, groups_ref, 0, near)
    expand(others.at[1], lists_ref, 2, groups_ref, 0, far)
    copies = []
    for number, lanes in enumerate(column_tiles(partial_ref.shape[1])):
        total = jnp.dot(own[...], own_dec[:latents, lanes], preferred_element_type=jnp.float32)
        partial_ref[:, lanes] = total[half:]
        total = total[:half] + jnp.dot(others[0], near_dec[:latents, lanes], preferred_element_type=jnp.float32)
        total = total + jnp.dot(others[1], far_dec[:latents, lanes], preferred_element_type=jnp.float32)
        stage[:, lanes] = total.astype(stage.dtype)
        copies += send_out(stage, out_ref, sems, groups_ref, 0, rows, number, lanes)
    for copy in copies:
        copy.wait()


def late_kernel(groups_ref, lists_ref, partial_ref, near, far, near_dec, far_dec, _, out_ref, others, stage, sems):
    half, latents = others[0].shape
    rows = half * 2 // groups_ref.shape[0]
    held = groups_ref.shape[0] // 2
    others[...] = jnp.zeros_like(others)
    expand(others.at[0], lists_ref, 1, groups_ref, held, near)
    expand(others.at[1], lists_ref, 2, groups_ref, held, far)
    copies = []
    for number, lanes in enumerate(column_tiles(partial_ref.shape[1])):
        total = partial_ref[:, lanes] + jnp.dot(others[0], near_dec[:latents, lanes], preferred_element_type=jnp.float32)
        total = total + jnp.dot(others[1], far_dec[:latents, lanes], preferred_element_type=jnp.float32)
        stage[:, lanes] = total.astype(stage.dtype)
        copies += send_out(stage, out_ref, sems, groups_ref, held, rows, number, lanes)
    for copy in copies:
        copy.wait()


def decode_scratch(half, latents, features, parts):
    return [
        pltpu.VMEM((2, half, latents), jnp.bfloat16),
        pltpu.VMEM((half, features), jnp.bfloat16),
        pltpu.SemaphoreType.DMA((len(column_tiles(features)), parts // 2)),
    ]


def decode_early(groups, lists, acts, decoders, tokens):
    latents, features = decoders[0].shape
    half = tokens // 2
    return pl.pallas_call(
        early_kernel,
        out_shape=[
            jax.ShapeDtypeStruct((tokens, features), jnp.bfloat16),
            jax.ShapeDtypeStruct((half, features), jnp.float32),
        ],
        in_specs=[SMEM, SMEM] + [VMEM] * (len(acts) + len(decoders)),
        out_specs=[ANY, VMEM],
        scratch_shapes=[pltpu.VMEM((tokens, latents), jnp.bfloat16)]
        + decode_scratch(half, latents, features, groups.shape[0]),
        compiler_params=pltpu.CompilerParams(vmem_limit_bytes=24 << 20),
        cost_estimate=pl.CostEstimate(
            flops=4 * tokens * latents * features,
            bytes_accessed=2 * (3 * latents * features + 2 * tokens * features),
            transcendentals=0,
        ),
        name="decode_early",
    )(groups, lists, *acts, *decoders)


def decode_late(groups, lists, partial, acts, decoders, rebuilt, latents):
    tokens, features = rebuilt.shape
    return pl.pallas_call(
        late_kernel,
        out_shape=jax.ShapeDtypeStruct((tokens, features), jnp.bfloat16),
        in_specs=[SMEM, SMEM] + [VMEM] * (1 + len(acts) + len(decoders)) + [ANY],
        out_specs=ANY,
        scratch_shapes=decode_scratch(tokens // 2, latents, features, groups.shape[0]),
        input_output_aliases={3 + len(acts) + len(decoders): 0},
        compiler_params=pltpu.CompilerParams(vmem_limit_bytes=24 << 20),
        cost_estimate=pl.CostEstimate(
            flops=2 * tokens * latents * features,
            bytes_accessed=2 * (2 * latents * features + 2 * tokens * features),
            transcendentals=0,
        ),
        name="decode_late",
    )(groups, lists, partial, *acts, *decoders, rebuilt)


def shards(layer_input, enc_weight, enc_bias, dec_weight, block_lists, block_counts):
    parts = lax.axis_size("latent")
    place = lax.axis_index("latent").astype(jnp.int32)
    x, encoder, decoder = layer_input[0], enc_weight[0], dec_weight[0]
    lists, counts = block_lists[0], block_counts[0]
    tokens, depth = x.shape
    tiles, slots = lists.shape
    targets, latents, _ = decoder.shape
    steps, held = doubling(parts)

    if targets != 3:
        raise ValueError("targets")

    with jax.named_scope("encoder_rows"):
        pieces = fetch_rows(place[None], encoder, parts)
        pieces, decoder = lax.optimization_barrier((pieces, decoder))
        weights = [pieces[0]] + [None] * (parts - 1)
        for step in sorted(range(1, parts), reverse=True):
            weights[step] = swapped(pieces[step], step)
    with jax.named_scope("decoder_weights"):
        decoders, all_lists = [decoder[0]], [lists]
        for offset in range(1, targets):
            decoders.append(passed_along(with_lists(decoder[offset], lists), offset))
            all_lists.append(decoders[offset][latents : latents + tiles, :slots].astype(jnp.int32))
        all_lists = jnp.stack(all_lists)

    with jax.named_scope("encode"):
        partials = encode(place[None], lax.bitwise_xor(place, lists), enc_bias, fetch(x), weights, tiles)
        arrived = [swapped(partials[step], step) for step in sorted(range(1, parts), reverse=True)]
    with jax.named_scope("activate"):
        preact = partials[0]
        for term in arrived:
            preact = preact + term.astype(jnp.float32)
        own_counts = lax.dynamic_slice_in_dim(counts, place * (tiles // parts), tiles // parts)
        live = (jnp.arange(slots)[None, :] < own_counts[:, None]).astype(jnp.float32)
        act = (jnp.maximum(preact, 0.0) * live[:, :, None, None]).astype(jnp.bfloat16)
    with jax.named_scope("spread"):
        own = act
        for step in steps[:-1]:
            own = jnp.concatenate([own, swapped(own, step)], axis=0)
        late_own = swapped(own, steps[-1])
        late_own, decoders = lax.optimization_barrier((late_own, decoders))
        even = lax.axis_index("layer") % 2 == 0
        far = passed_along(own, 2)
        late_far = passed_along(late_own, 2)
        near = across_cores(jnp.where(even, own, far))
    with jax.named_scope("decode"):
        groups = lax.bitwise_xor(place, jnp.array(held, jnp.int32))
        rebuilt, partial = decode_early(groups, all_lists, [own, late_own, near, far], decoders, tokens)
        rebuilt, partial, late_far = lax.optimization_barrier((rebuilt, partial, late_far))
        late = [across_cores(jnp.where(even, late_own, late_far)), late_far]
        return decode_late(groups, all_lists, partial, late, decoders[1:], rebuilt, latents)[None]


def solution(mesh):
    placed = (
        P("layer", None, "latent"),
        P("layer", None, "latent"),
        P("layer", "latent"),
        P("layer", None, None, "latent"),
        P("layer", None, None),
        P("layer", None),
    )
    return jax.shard_map(
        shards, mesh=mesh, in_specs=placed, out_specs=P("layer", None, "latent"), check_vma=False
    )
```

```python
import functools

import jax
import jax.numpy as jnp
from jax import lax
from jax.experimental import pallas as pl
from jax.experimental.pallas import tpu as pltpu
from jax.sharding import PartitionSpec as P

VMEM = pl.BlockSpec(memory_space=pltpu.VMEM)
SMEM = pl.BlockSpec(memory_space=pltpu.SMEM)
ANY = pl.BlockSpec(memory_space=pl.ANY)
HBM = pl.BlockSpec(memory_space=pltpu.HBM)


def swapped(value, step):
    count = lax.axis_size("latent")
    return lax.ppermute(value, "latent", [(i, i ^ step) for i in range(count)])


def passed_along(value, steps):
    count = lax.axis_size("layer")
    return lax.ppermute(value, "layer", [(i, i + steps) for i in range(count - steps)])


def across_cores(value):
    count = lax.axis_size("layer")
    return lax.ppermute(value, "layer", [(i, i ^ 1) for i in range(count)])


def doubling(parts):
    if parts & (parts - 1):
        raise ValueError("latent axis")
    steps, held = [], [0]
    while len(held) < parts:
        steps.append(parts // (2 * len(held)))
        held = held + [distance ^ steps[-1] for distance in held]
    return steps, held


def fetch_rows_kernel(place_ref, encoder_ref, *refs):
    piece_refs, sems = refs[:-1], refs[-1]
    depth = piece_refs[0].shape[0]
    copies = []
    for step in range(len(piece_refs)):
        first = pl.multiple_of(lax.bitwise_xor(place_ref[0], step) * depth, depth)
        copies.append(pltpu.make_async_copy(encoder_ref.at[pl.ds(first, depth)], piece_refs[step], sems.at[step]))
        copies[-1].start()
    for copy in copies:
        copy.wait()


def fetch_rows(place, encoder, parts):
    depth = encoder.shape[0] // parts
    return pl.pallas_call(
        fetch_rows_kernel,
        out_shape=[jax.ShapeDtypeStruct((depth, encoder.shape[1]), encoder.dtype)] * parts,
        in_specs=[SMEM, HBM],
        out_specs=[VMEM] * parts,
        scratch_shapes=[pltpu.SemaphoreType.DMA((parts,))],
        compiler_params=pltpu.CompilerParams(vmem_limit_bytes=16 << 20),
        name="fetch_rows",
    )(place, encoder)


def with_lists(decoder, lists):
    tiles, slots = lists.shape
    ids = jnp.pad(lists.astype(decoder.dtype), ((0, -tiles % 16), (0, decoder.shape[1] - slots)))
    return jnp.concatenate([decoder, ids], axis=0)


def encode_kernel(parts, place_ref, relative_ref, bias_ref, x_hbm, *refs):
    weight_refs, refs = refs[:parts], refs[parts:]
    out_refs, (x_ref, partial, sems) = refs[:parts], refs[parts:]
    width = bias_ref.shape[1]
    tiles, slots, rows, _ = out_refs[0].shape
    group_rows = tiles * rows
    copies = []
    for step in range(parts):
        group = pl.ds(pl.multiple_of(lax.bitwise_xor(place_ref[0], step) * group_rows, group_rows), group_rows)
        copies.append(pltpu.make_async_copy(x_hbm.at[group], x_ref.at[step], sems.at[step]))
    for copy in reversed(copies):
        copy.start()
    pair = 1 + (parts > 1)
    for step in reversed(range(parts)):
        copies[step].wait()
        for first in range(0, parts, pair):
            stacked = jnp.concatenate([ref[...] for ref in weight_refs[first : first + pair]], axis=1)
            product = jnp.dot(x_ref[step], stacked, preferred_element_type=jnp.float32)
            for source in range(first, first + pair):
                block = product[:, (source - first) * width : (source - first + 1) * width]
                partial[source] = block if source else block + bias_ref[...]
        group = lax.bitwise_xor(place_ref[0], step)
        for tile in range(tiles):
            for slot in range(slots):
                source = relative_ref[group * tiles + tile, slot]
                kept = partial[source, tile * rows : (tile + 1) * rows, :]
                out_refs[step][tile, slot] = kept.astype(out_refs[step].dtype)


def encode(place, relative, bias, x, weights, tiles):
    parts = len(weights)
    tokens, depth = x.shape
    width = bias.shape[1]
    shape = (tiles // parts, relative.shape[1], tokens // tiles, width)
    return pl.pallas_call(
        functools.partial(encode_kernel, parts),
        out_shape=[jax.ShapeDtypeStruct(shape, jnp.bfloat16 if step else jnp.float32) for step in range(parts)],
        in_specs=[SMEM, SMEM, VMEM, HBM] + [VMEM] * parts,
        out_specs=[VMEM] * parts,
        scratch_shapes=[
            pltpu.VMEM((parts, tokens // parts, depth), x.dtype),
            pltpu.VMEM((parts, tokens // parts, width), jnp.float32),
            pltpu.SemaphoreType.DMA((parts,)),
        ],
        compiler_params=pltpu.CompilerParams(vmem_limit_bytes=16 << 20),
        cost_estimate=pl.CostEstimate(
            flops=2 * tokens * depth * parts * width,
            bytes_accessed=2 * (tokens * depth + depth * parts * width),
            transcendentals=0,
        ),
        name="encode",
    )(place, relative, bias, x, *weights)


def expand(dense, lists_ref, offset, groups_ref, first, act_ref):
    tiles_held, slots, rows, width = act_ref.shape
    tiles = lists_ref.shape[1] // groups_ref.shape[0]
    for held in range(tiles_held):
        for slot in range(slots):
            block = lists_ref[offset, groups_ref[first + held // tiles] * tiles + held % tiles, slot]
            lanes = pl.ds(pl.multiple_of(block * width, width), width)
            dense[held * rows : (held + 1) * rows, lanes] = act_ref[held, slot]


def column_tiles(features):
    columns = 256 if features % 256 == 0 else features
    return [slice(first, first + columns) for first in range(0, features, columns)]


def send_out(stage, out_ref, sems, groups_ref, first, rows, number, lanes):
    copies = []
    for held in range(stage.shape[0] // rows):
        row = pl.multiple_of(groups_ref[first + held] * rows, rows)
        copies.append(
            pltpu.make_async_copy(
                stage.at[held * rows : (held + 1) * rows, lanes],
                out_ref.at[pl.ds(row, rows), lanes],
                sems.at[number, held],
            )
        )
        copies[-1].start()
    return copies


def early_kernel(groups_ref, lists_ref, own_early, own_late, near, far, own_dec, near_dec, far_dec, *refs):
    out_ref, partial_ref, own, others, stage, sems = refs
    half, latents = others[0].shape
    rows = half * 2 // groups_ref.shape[0]
    own[...] = jnp.zeros_like(own)
    others[...] = jnp.zeros_like(others)
    held = groups_ref.shape[0] // 2
    expand(own.at[:half], lists_ref, 0, groups_ref, 0, own_early)
    expand(own.at[half:], lists_ref, 0, groups_ref, held, own_late)
    expand(others.at[0], lists_ref, 1, groups_ref, 0, near)
    expand(others.at[1], lists_ref, 2, groups_ref, 0, far)
    copies = []
    for number, lanes in enumerate(column_tiles(partial_ref.shape[1])):
        total = jnp.dot(own[...], own_dec[:latents, lanes], preferred_element_type=jnp.float32)
        partial_ref[:, lanes] = total[half:]
        total = total[:half] + jnp.dot(others[0], near_dec[:latents, lanes], preferred_element_type=jnp.float32)
        total = total + jnp.dot(others[1], far_dec[:latents, lanes], preferred_element_type=jnp.float32)
        stage[:, lanes] = total.astype(stage.dtype)
        copies += send_out(stage, out_ref, sems, groups_ref, 0, rows, number, lanes)
    for copy in copies:
        copy.wait()


def late_kernel(groups_ref, lists_ref, partial_ref, near, far, near_dec, far_dec, _, out_ref, others, stage, sems):
    half, latents = others[0].shape
    rows = half * 2 // groups_ref.shape[0]
    held = groups_ref.shape[0] // 2
    others[...] = jnp.zeros_like(others)
    expand(others.at[0], lists_ref, 1, groups_ref, held, near)
    expand(others.at[1], lists_ref, 2, groups_ref, held, far)
    copies = []
    for number, lanes in enumerate(column_tiles(partial_ref.shape[1])):
        total = partial_ref[:, lanes] + jnp.dot(others[0], near_dec[:latents, lanes], preferred_element_type=jnp.float32)
        total = total + jnp.dot(others[1], far_dec[:latents, lanes], preferred_element_type=jnp.float32)
        stage[:, lanes] = total.astype(stage.dtype)
        copies += send_out(stage, out_ref, sems, groups_ref, held, rows, number, lanes)
    for copy in copies:
        copy.wait()


def decode_scratch(half, latents, features, parts):
    return [
        pltpu.VMEM((2, half, latents), jnp.bfloat16),
        pltpu.VMEM((half, features), jnp.bfloat16),
        pltpu.SemaphoreType.DMA((len(column_tiles(features)), parts // 2)),
    ]


def decode_early(groups, lists, acts, decoders, tokens):
    latents, features = decoders[0].shape
    half = tokens // 2
    return pl.pallas_call(
        early_kernel,
        out_shape=[
            jax.ShapeDtypeStruct((tokens, features), jnp.bfloat16),
            jax.ShapeDtypeStruct((half, features), jnp.float32),
        ],
        in_specs=[SMEM, SMEM] + [VMEM] * (len(acts) + len(decoders)),
        out_specs=[ANY, VMEM],
        scratch_shapes=[pltpu.VMEM((tokens, latents), jnp.bfloat16)]
        + decode_scratch(half, latents, features, groups.shape[0]),
        compiler_params=pltpu.CompilerParams(vmem_limit_bytes=16 << 20),
        cost_estimate=pl.CostEstimate(
            flops=4 * tokens * latents * features,
            bytes_accessed=2 * (3 * latents * features + 2 * tokens * features),
            transcendentals=0,
        ),
        name="decode_early",
    )(groups, lists, *acts, *decoders)


def decode_late(groups, lists, partial, acts, decoders, rebuilt, latents):
    tokens, features = rebuilt.shape
    return pl.pallas_call(
        late_kernel,
        out_shape=jax.ShapeDtypeStruct((tokens, features), jnp.bfloat16),
        in_specs=[SMEM, SMEM] + [VMEM] * (1 + len(acts) + len(decoders)) + [ANY],
        out_specs=ANY,
        scratch_shapes=decode_scratch(tokens // 2, latents, features, groups.shape[0]),
        input_output_aliases={3 + len(acts) + len(decoders): 0},
        compiler_params=pltpu.CompilerParams(vmem_limit_bytes=16 << 20),
        cost_estimate=pl.CostEstimate(
            flops=2 * tokens * latents * features,
            bytes_accessed=2 * (2 * latents * features + 2 * tokens * features),
            transcendentals=0,
        ),
        name="decode_late",
    )(groups, lists, partial, *acts, *decoders, rebuilt)


def shards(layer_input, enc_weight, enc_bias, dec_weight, block_lists, block_counts):
    parts = lax.axis_size("latent")
    place = lax.axis_index("latent").astype(jnp.int32)
    x, encoder, decoder = layer_input[0], enc_weight[0], dec_weight[0]
    lists, counts = block_lists[0], block_counts[0]
    tokens, depth = x.shape
    tiles, slots = lists.shape
    targets, latents, _ = decoder.shape
    steps, held = doubling(parts)

    if targets != 3:
        raise ValueError("targets")

    with jax.named_scope("encoder_rows"):
        pieces = fetch_rows(place[None], encoder, parts)
        pieces, decoder = lax.optimization_barrier((pieces, decoder))
        weights = [pieces[0]] + [None] * (parts - 1)
        for step in sorted(range(1, parts), reverse=True):
            weights[step] = swapped(pieces[step], step)
    with jax.named_scope("decoder_weights"):
        decoders, all_lists = [decoder[0]], [lists]
        for offset in range(1, targets):
            decoders.append(passed_along(with_lists(decoder[offset], lists), offset))
            all_lists.append(decoders[offset][latents : latents + tiles, :slots].astype(jnp.int32))
        all_lists = jnp.stack(all_lists)

    with jax.named_scope("encode"):
        partials = encode(place[None], lax.bitwise_xor(place, lists), enc_bias, x, weights, tiles)
        arrived = [swapped(partials[step], step) for step in sorted(range(1, parts), reverse=True)]
    with jax.named_scope("activate"):
        preact = partials[0]
        for term in arrived:
            preact = preact + term.astype(jnp.float32)
        own_counts = lax.dynamic_slice_in_dim(counts, place * (tiles // parts), tiles // parts)
        live = (jnp.arange(slots)[None, :] < own_counts[:, None]).astype(jnp.float32)
        act = (jnp.maximum(preact, 0.0) * live[:, :, None, None]).astype(jnp.bfloat16)
    with jax.named_scope("spread"):
        own = act
        for step in steps[:-1]:
            own = jnp.concatenate([own, swapped(own, step)], axis=0)
        late_own = swapped(own, steps[-1])
        late_own, decoders = lax.optimization_barrier((late_own, decoders))
        even = lax.axis_index("layer") % 2 == 0
        far = passed_along(own, 2)
        late_far = passed_along(late_own, 2)
        far, late_own = lax.optimization_barrier((far, late_own))
        near = across_cores(jnp.where(even, own, far))
    with jax.named_scope("decode"):
        groups = lax.bitwise_xor(place, jnp.array(held, jnp.int32))
        rebuilt, partial = decode_early(groups, all_lists, [own, late_own, near, far], decoders, tokens)
        rebuilt, partial, late_far = lax.optimization_barrier((rebuilt, partial, late_far))
        late = [across_cores(jnp.where(even, late_own, late_far)), late_far]
        return decode_late(groups, all_lists, partial, late, decoders[1:], rebuilt, latents)[None]


def solution(mesh):
    placed = (
        P("layer", None, "latent"),
        P("layer", None, "latent"),
        P("layer", "latent"),
        P("layer", None, None, "latent"),
        P("layer", None, None),
        P("layer", None),
    )
    return jax.shard_map(
        shards, mesh=mesh, in_specs=placed, out_specs=P("layer", None, "latent"), check_vma=False
    )
```

```python
import functools

import jax
import jax.numpy as jnp
from jax import lax
from jax.experimental import pallas as pl
from jax.experimental.pallas import tpu as pltpu
from jax.sharding import PartitionSpec as P

VMEM = pl.BlockSpec(memory_space=pltpu.VMEM)
SMEM = pl.BlockSpec(memory_space=pltpu.SMEM)
ANY = pl.BlockSpec(memory_space=pl.ANY)
HBM = pl.BlockSpec(memory_space=pltpu.HBM)


def swapped(value, step):
    count = lax.axis_size("latent")
    return lax.ppermute(value, "latent", [(i, i ^ step) for i in range(count)])


def passed_along(value, steps):
    count = lax.axis_size("layer")
    return lax.ppermute(value, "layer", [(i, i + steps) for i in range(count - steps)])


def across_cores(value):
    count = lax.axis_size("layer")
    return lax.ppermute(value, "layer", [(i, i ^ 1) for i in range(count)])


def small(name, megabytes=8):
    return dict(compiler_params=pltpu.CompilerParams(vmem_limit_bytes=megabytes << 20), name=name)


def fetch_rows_kernel(place_ref, encoder_ref, *piece_refs):
    depth = piece_refs[0].shape[0]
    for step, piece in enumerate(piece_refs):
        first = pl.multiple_of(lax.bitwise_xor(place_ref[0], step) * depth, depth)
        piece[...] = encoder_ref[pl.ds(first, depth), :]


def fetch_rows(place, encoder, parts):
    depth = encoder.shape[0] // parts
    return pl.pallas_call(
        fetch_rows_kernel,
        out_shape=[jax.ShapeDtypeStruct((depth, encoder.shape[1]), encoder.dtype)] * parts,
        in_specs=[SMEM, VMEM],
        out_specs=[VMEM] * parts,
        **small("fetch_rows"),
    )(place, encoder)


def fetch_decoders_kernel(lists_ref, decoder_ref, *refs):
    out_refs, sems = refs[:-1], refs[-1]
    latents = decoder_ref.shape[1]
    copies = []
    for number, out_ref in enumerate(out_refs):
        copies.append(
            pltpu.make_async_copy(decoder_ref.at[number + 1], out_ref.at[pl.ds(0, latents)], sems.at[number])
        )
        copies[-1].start()
    for out_ref in out_refs:
        out_ref[latents:, :] = lists_ref[...]
    for copy in copies:
        copy.wait()


def fetch_decoders(lists, decoder):
    targets, latents, features = decoder.shape
    ids = jnp.pad(lists.astype(decoder.dtype), ((0, -lists.shape[0] % 16), (0, features - lists.shape[1])))
    shape = jax.ShapeDtypeStruct((latents + ids.shape[0], features), decoder.dtype)
    return pl.pallas_call(
        fetch_decoders_kernel,
        out_shape=[shape] * (targets - 1),
        in_specs=[VMEM, ANY],
        out_specs=[VMEM] * (targets - 1),
        scratch_shapes=[pltpu.SemaphoreType.DMA((targets - 1,))],
        **small("fetch_decoders"),
    )(ids, decoder)


def encode_kernel(parts, place_ref, relative_ref, bias_ref, x_ref, *refs):
    weight_refs, (kept_ref, sent_ref, partial) = refs[:parts], refs[parts:]
    width = bias_ref.shape[1]
    held, slots, rows, _ = kept_ref.shape
    tiles = 2 * held // parts
    pair = 1 + (parts > 1)
    for first in range(0, parts, pair):
        stacked = jnp.concatenate([ref[...] for ref in weight_refs[first : first + pair]], axis=1)
        product = jnp.dot(x_ref[...], stacked, preferred_element_type=jnp.float32)
        for source in range(first, first + pair):
            block = product[:, (source - first) * width : (source - first + 1) * width]
            partial[source] = block if source else block + bias_ref[...]
    for side, out_ref in ((0, kept_ref), (1, sent_ref)):
        parity = lax.bitwise_xor(lax.bitwise_and(place_ref[0], 1), side)
        for position in range(held):
            tile = (2 * (position // tiles) + parity) * tiles + position % tiles
            first = pl.multiple_of(tile * rows, rows)
            for slot in range(slots):
                source = relative_ref[tile, slot]
                out_ref[position, slot] = partial[source, pl.ds(first, rows), :].astype(out_ref.dtype)


def encode(place, relative, bias, x, weights):
    parts = len(weights)
    tokens, depth = x.shape
    width = bias.shape[1]
    tiles, slots = relative.shape
    shape = (tiles // 2, slots, tokens // tiles, width)
    return pl.pallas_call(
        functools.partial(encode_kernel, parts),
        out_shape=[jax.ShapeDtypeStruct(shape, jnp.float32), jax.ShapeDtypeStruct(shape, jnp.bfloat16)],
        in_specs=[SMEM, SMEM] + [VMEM] * (2 + parts),
        out_specs=[VMEM] * 2,
        scratch_shapes=[pltpu.VMEM((parts, tokens, width), jnp.float32)],
        cost_estimate=pl.CostEstimate(
            flops=2 * tokens * depth * parts * width,
            bytes_accessed=2 * (tokens * depth + depth * parts * width),
            transcendentals=0,
        ),
        **small("encode", 16),
    )(place, relative, bias, x, *weights)


def merge_kernel(kept_ref, arrived_ref, total_ref, sent_ref):
    total = kept_ref[...] + arrived_ref[...].astype(jnp.float32)
    total_ref[...] = total
    sent_ref[...] = total.astype(sent_ref.dtype)


def merge(kept, arrived):
    return pl.pallas_call(
        merge_kernel,
        out_shape=[jax.ShapeDtypeStruct(kept.shape, kept.dtype), jax.ShapeDtypeStruct(kept.shape, arrived.dtype)],
        in_specs=[VMEM] * 2,
        out_specs=[VMEM] * 2,
        **small("merge"),
    )(kept, arrived)


def activate_kernel(parts, place_ref, counts_ref, kept_ref, arrived_ref, act_ref):
    held, slots, _, _ = kept_ref.shape
    tiles = 2 * held // parts
    parity = lax.bitwise_and(place_ref[0], 1)
    for position in range(held):
        tile = (2 * (position // tiles) + parity) * tiles + position % tiles
        for slot in range(slots):
            live = (slot < counts_ref[tile]).astype(jnp.float32)
            preact = kept_ref[position, slot] + arrived_ref[position, slot].astype(jnp.float32)
            act_ref[position, slot] = (jnp.maximum(preact, 0.0) * live).astype(act_ref.dtype)


def activate(place, counts, kept, arrived, parts):
    return pl.pallas_call(
        functools.partial(activate_kernel, parts),
        out_shape=jax.ShapeDtypeStruct(kept.shape, arrived.dtype),
        in_specs=[SMEM, SMEM] + [VMEM] * 2,
        out_specs=VMEM,
        **small("activate"),
    )(place, counts, kept, arrived)


def choose_kernel(even_ref, *refs):
    sources, out_ref = refs[:-1], refs[-1]
    held = sources[0].shape[0]

    @pl.when(even_ref[0] == 1)
    def _():
        out_ref[:held] = sources[0][...]
        out_ref[held:] = sources[1][...]

    @pl.when(even_ref[0] != 1)
    def _():
        out_ref[:held] = sources[2][...]
        out_ref[held:] = sources[3][...]


def choose(even, own, far):
    shape = own[0].shape
    return pl.pallas_call(
        choose_kernel,
        out_shape=jax.ShapeDtypeStruct((2 * shape[0],) + shape[1:], own[0].dtype),
        in_specs=[SMEM] + [VMEM] * 4,
        out_specs=VMEM,
        **small("choose"),
    )(even, *own, *far)


def expand(dense, lists_ref, offset, groups_ref, first, act_ref):
    tiles_held, slots, rows, width = act_ref.shape
    tiles = lists_ref.shape[1] // groups_ref.shape[0]
    for held in range(tiles_held):
        for slot in range(slots):
            block = lists_ref[offset, groups_ref[first + held // tiles] * tiles + held % tiles, slot]
            lanes = pl.ds(pl.multiple_of(block * width, width), width)
            dense[held * rows : (held + 1) * rows, lanes] = act_ref[held, slot]


def column_tiles(features):
    columns = 256 if features % 256 == 0 else features
    return [slice(first, first + columns) for first in range(0, features, columns)]


def send_out(stage, out_ref, sems, groups_ref, first, rows, number, lanes):
    copies = []
    for held in range(stage.shape[0] // rows):
        row = pl.multiple_of(groups_ref[first + held] * rows, rows)
        copies.append(
            pltpu.make_async_copy(
                stage.at[held * rows : (held + 1) * rows, lanes],
                out_ref.at[pl.ds(row, rows), lanes],
                sems.at[number, held],
            )
        )
        copies[-1].start()
    return copies


def early_kernel(groups_ref, lists_ref, own_early, own_late, far, decoder_hbm, far_dec, partial_ref, own, other, own_dec, sem):
    copy = pltpu.make_async_copy(decoder_hbm.at[0], own_dec, sem)
    copy.start()
    half, latents = other.shape
    held = groups_ref.shape[0] // 2
    own[...] = jnp.zeros_like(own)
    other[...] = jnp.zeros_like(other)
    expand(own.at[:half], lists_ref, 0, groups_ref, 0, own_early)
    expand(own.at[half:], lists_ref, 0, groups_ref, held, own_late)
    expand(other, lists_ref, 2, groups_ref, 0, far)
    copy.wait()
    for lanes in column_tiles(partial_ref.shape[1]):
        total = jnp.dot(own[...], own_dec[:, lanes], preferred_element_type=jnp.float32)
        partial_ref[half:, lanes] = total[half:]
        partial_ref[:half, lanes] = total[:half] + jnp.dot(
            other[...], far_dec[:latents, lanes], preferred_element_type=jnp.float32
        )


def late_kernel(groups_ref, lists_ref, partial_ref, near, far, near_dec, far_dec, out_ref, wide, other, stage, sems):
    half, latents = other.shape
    parts = groups_ref.shape[0]
    wide[...] = jnp.zeros_like(wide)
    other[...] = jnp.zeros_like(other)
    expand(wide, lists_ref, 1, groups_ref, 0, near)
    expand(other, lists_ref, 2, groups_ref, parts // 2, far)
    copies = []
    for number, lanes in enumerate(column_tiles(partial_ref.shape[1])):
        total = partial_ref[:, lanes] + jnp.dot(
            wide[...], near_dec[:latents, lanes], preferred_element_type=jnp.float32
        )
        stage[:half, lanes] = total[:half].astype(stage.dtype)
        total = total[half:] + jnp.dot(other[...], far_dec[:latents, lanes], preferred_element_type=jnp.float32)
        stage[half:, lanes] = total.astype(stage.dtype)
        copies += send_out(stage, out_ref, sems, groups_ref, 0, 2 * half // parts, number, lanes)
    for copy in copies:
        copy.wait()


def decode_early(groups, lists, acts, decoder, far_decoder, tokens):
    _, latents, features = decoder.shape
    return pl.pallas_call(
        early_kernel,
        out_shape=jax.ShapeDtypeStruct((tokens, features), jnp.float32),
        in_specs=[SMEM, SMEM] + [VMEM] * 3 + [ANY, VMEM],
        out_specs=VMEM,
        scratch_shapes=[
            pltpu.VMEM((tokens, latents), jnp.bfloat16),
            pltpu.VMEM((tokens // 2, latents), jnp.bfloat16),
            pltpu.VMEM((latents, features), jnp.bfloat16),
            pltpu.SemaphoreType.DMA,
        ],
        cost_estimate=pl.CostEstimate(
            flops=3 * tokens * latents * features,
            bytes_accessed=2 * (2 * latents * features + 2 * tokens * features),
            transcendentals=0,
        ),
        **small("decode_early", 16),
    )(groups, lists, *acts, decoder, far_decoder)


def decode_late(groups, lists, partial, near, far, decoders, latents):
    tokens, features = partial.shape
    parts = groups.shape[0]
    return pl.pallas_call(
        late_kernel,
        out_shape=jax.ShapeDtypeStruct((tokens, features), jnp.bfloat16),
        in_specs=[SMEM, SMEM] + [VMEM] * 5,
        out_specs=ANY,
        scratch_shapes=[
            pltpu.VMEM((tokens, latents), jnp.bfloat16),
            pltpu.VMEM((tokens // 2, latents), jnp.bfloat16),
            pltpu.VMEM((tokens, features), jnp.bfloat16),
            pltpu.SemaphoreType.DMA((len(column_tiles(features)), parts)),
        ],
        cost_estimate=pl.CostEstimate(
            flops=3 * tokens * latents * features,
            bytes_accessed=2 * (2 * latents * features + 2 * tokens * features),
            transcendentals=0,
        ),
        **small("decode_late", 16),
    )(groups, lists, partial, near, far, *decoders)


def shards(layer_input, enc_weight, enc_bias, dec_weight, block_lists, block_counts):
    parts = lax.axis_size("latent")
    index = lax.axis_index("latent").astype(jnp.int32)
    place = index[None]
    x, encoder, decoder = layer_input[0], enc_weight[0], dec_weight[0]
    lists, counts = block_lists[0], block_counts[0]
    tokens = x.shape[0]
    tiles, slots = lists.shape
    targets, latents, _ = decoder.shape
    if targets != 3 or parts < 2 or parts & (parts - 1):
        raise ValueError("mesh")

    with jax.named_scope("encoder_rows"):
        pieces = fetch_rows(place, encoder, parts)
        pieces, decoder = lax.optimization_barrier((pieces, decoder))
        weights = [pieces[0]] + [None] * (parts - 1)
        for step in sorted(range(1, parts), reverse=True):
            weights[step] = swapped(pieces[step], step)
    with jax.named_scope("decoder_weights"):
        decoders, all_lists = [], [lists]
        for number, rows in enumerate(fetch_decoders(lists, decoder)):
            decoders.append(passed_along(rows, number + 1))
            all_lists.append(decoders[-1][latents : latents + tiles, :slots].astype(jnp.int32))
        all_lists = jnp.stack(all_lists)

    with jax.named_scope("encode"):
        kept, sent = encode(place, lax.bitwise_xor(index, lists), enc_bias, x, weights)
        arrived = swapped(sent, 1)
        step = 2
        while step < parts:
            kept, sent = merge(kept, arrived)
            arrived = swapped(sent, step)
            step *= 2
        own = activate(place, counts, kept, arrived, parts)
    with jax.named_scope("spread"):
        late_own = swapped(own, 1)
        far = passed_along(own, 2)
        late_far = passed_along(late_own, 2)
    with jax.named_scope("decode"):
        order = 2 * jnp.arange(parts // 2, dtype=jnp.int32)
        parity = lax.bitwise_and(index, 1)
        groups = jnp.concatenate([order + parity, order + 1 - parity])
        partial = decode_early(groups, all_lists, [own, late_own, far], decoder, decoders[1], tokens)
        partial, late_far = lax.optimization_barrier((partial, late_far))
        even = (lax.axis_index("layer") % 2 == 0).astype(jnp.int32)[None]
        near = across_cores(choose(even, [own, late_own], [far, late_far]))
        return decode_late(groups, all_lists, partial, near, late_far, decoders, latents)[None]


def solution(mesh):
    placed = (
        P("layer", None, "latent"),
        P("layer", None, "latent"),
        P("layer", "latent"),
        P("layer", None, None, "latent"),
        P("layer", None, None),
        P("layer", None),
    )
    return jax.shard_map(
        shards, mesh=mesh, in_specs=placed, out_specs=P("layer", None, "latent"), check_vma=False
    )
```

```python
import functools

import jax
import jax.numpy as jnp
from jax import lax
from jax.experimental import pallas as pl
from jax.experimental.pallas import tpu as pltpu
from jax.sharding import PartitionSpec as P

VMEM = pl.BlockSpec(memory_space=pltpu.VMEM)
SMEM = pl.BlockSpec(memory_space=pltpu.SMEM)
ANY = pl.BlockSpec(memory_space=pl.ANY)
HBM = pl.BlockSpec(memory_space=pltpu.HBM)


def swapped(value, step):
    count = lax.axis_size("latent")
    return lax.ppermute(value, "latent", [(i, i ^ step) for i in range(count)])


def passed_along(value, steps):
    count = lax.axis_size("layer")
    return lax.ppermute(value, "layer", [(i, i + steps) for i in range(count - steps)])


def across_cores(value):
    count = lax.axis_size("layer")
    return lax.ppermute(value, "layer", [(i, i ^ 1) for i in range(count)])


def small(name, megabytes=8):
    return dict(compiler_params=pltpu.CompilerParams(vmem_limit_bytes=megabytes << 20), name=name)


def held_group(number, parts):
    half = parts // 2
    parity = lax.bitwise_and(lax.axis_index("latent"), 1)
    return 2 * (number % half) + (parity if number < half else 1 - parity)


def fetch_rows_kernel(encoder_ref, *piece_refs):
    depth = piece_refs[0].shape[0]
    for step, piece in enumerate(piece_refs):
        first = pl.multiple_of(lax.bitwise_xor(lax.axis_index("latent"), step) * depth, depth)
        piece[...] = encoder_ref[pl.ds(first, depth), :]


def fetch_rows(encoder, parts):
    depth = encoder.shape[0] // parts
    return pl.pallas_call(
        fetch_rows_kernel,
        out_shape=[jax.ShapeDtypeStruct((depth, encoder.shape[1]), encoder.dtype)] * parts,
        in_specs=[VMEM],
        out_specs=[VMEM] * parts,
        **small("fetch_rows"),
    )(encoder)


def fetch_decoders_kernel(lists_ref, decoder_ref, *refs):
    out_refs, sems = refs[:-1], refs[-1]
    latents = decoder_ref.shape[1]
    copies = []
    for number, out_ref in enumerate(out_refs):
        copies.append(
            pltpu.make_async_copy(decoder_ref.at[number + 1], out_ref.at[pl.ds(0, latents)], sems.at[number])
        )
        copies[-1].start()
    for out_ref in out_refs:
        out_ref[latents:, :] = lists_ref[...]
    for copy in copies:
        copy.wait()


def fetch_decoders(lists, decoder):
    targets, latents, features = decoder.shape
    ids = jnp.pad(lists.astype(decoder.dtype), ((0, -lists.shape[0] % 16), (0, features - lists.shape[1])))
    shape = jax.ShapeDtypeStruct((latents + ids.shape[0], features), decoder.dtype)
    return pl.pallas_call(
        fetch_decoders_kernel,
        out_shape=[shape] * (targets - 1),
        in_specs=[VMEM, ANY],
        out_specs=[VMEM] * (targets - 1),
        scratch_shapes=[pltpu.SemaphoreType.DMA((targets - 1,))],
        **small("fetch_decoders", 58),
    )(ids, decoder)


def encode_kernel(parts, lists_ref, bias_ref, x_ref, *refs):
    weight_refs, (kept_ref, sent_ref, partial) = refs[:parts], refs[parts:]
    width = bias_ref.shape[1]
    held, slots, rows, _ = kept_ref.shape
    tiles = 2 * held // parts
    for first in range(0, parts, 2):
        stacked = jnp.concatenate([ref[...] for ref in weight_refs[first : first + 2]], axis=1)
        product = jnp.dot(x_ref[...], stacked, preferred_element_type=jnp.float32)
        for source in range(first, first + 2):
            block = product[:, (source - first) * width : (source - first + 1) * width]
            partial[source] = block if source else block + bias_ref[...]
    for out_ref, first in ((kept_ref, 0), (sent_ref, parts // 2)):
        for position in range(held):
            tile = held_group(first + position // tiles, parts) * tiles + position % tiles
            row = pl.multiple_of(tile * rows, rows)
            for slot in range(slots):
                source = lax.bitwise_xor(lax.axis_index("latent"), lists_ref[slot, tile])
                out_ref[position, slot] = partial[source, pl.ds(row, rows), :].astype(out_ref.dtype)


def encode(lists, bias, x, weights):
    parts = len(weights)
    tokens, depth = x.shape
    width = bias.shape[1]
    slots, tiles = lists.shape
    shape = (tiles // 2, slots, tokens // tiles, width)
    return pl.pallas_call(
        functools.partial(encode_kernel, parts),
        out_shape=[jax.ShapeDtypeStruct(shape, jnp.float32), jax.ShapeDtypeStruct(shape, jnp.bfloat16)],
        in_specs=[SMEM] + [VMEM] * (2 + parts),
        out_specs=[VMEM] * 2,
        scratch_shapes=[pltpu.VMEM((parts, tokens, width), jnp.float32)],
        cost_estimate=pl.CostEstimate(
            flops=2 * tokens * depth * parts * width,
            bytes_accessed=2 * (tokens * depth + depth * parts * width),
            transcendentals=0,
        ),
        **small("encode", 16),
    )(lists, bias, x, *weights)


def merge_kernel(kept_ref, arrived_ref, total_ref, sent_ref):
    total = kept_ref[...] + arrived_ref[...].astype(jnp.float32)
    total_ref[...] = total
    sent_ref[...] = total.astype(sent_ref.dtype)


def merge(kept, arrived):
    return pl.pallas_call(
        merge_kernel,
        out_shape=[jax.ShapeDtypeStruct(kept.shape, kept.dtype), jax.ShapeDtypeStruct(kept.shape, arrived.dtype)],
        in_specs=[VMEM] * 2,
        out_specs=[VMEM] * 2,
        **small("merge"),
    )(kept, arrived)


def activate_kernel(parts, counts_ref, kept_ref, arrived_ref, act_ref):
    held, slots, _, _ = kept_ref.shape
    tiles = 2 * held // parts
    for position in range(held):
        tile = held_group(position // tiles, parts) * tiles + position % tiles
        for slot in range(slots):
            live = (slot < counts_ref[tile]).astype(jnp.float32)
            preact = kept_ref[position, slot] + arrived_ref[position, slot].astype(jnp.float32)
            act_ref[position, slot] = (jnp.maximum(preact, 0.0) * live).astype(act_ref.dtype)


def activate(counts, kept, arrived, parts):
    return pl.pallas_call(
        functools.partial(activate_kernel, parts),
        out_shape=jax.ShapeDtypeStruct(kept.shape, arrived.dtype),
        in_specs=[SMEM] + [VMEM] * 2,
        out_specs=VMEM,
        **small("activate"),
    )(counts, kept, arrived)


def choose_kernel(*refs):
    sources, out_ref = refs[:-1], refs[-1]
    held = sources[0].shape[0]
    odd = lax.bitwise_and(lax.axis_index("layer"), 1)

    @pl.when(odd == 0)
    def _():
        out_ref[:held] = sources[0][...]
        out_ref[held:] = sources[1][...]

    @pl.when(odd == 1)
    def _():
        out_ref[:held] = sources[2][...]
        out_ref[held:] = sources[3][...]


def choose(own, far):
    shape = own[0].shape
    return pl.pallas_call(
        choose_kernel,
        out_shape=jax.ShapeDtypeStruct((2 * shape[0],) + shape[1:], own[0].dtype),
        in_specs=[VMEM] * 4,
        out_specs=VMEM,
        **small("choose"),
    )(*own, *far)


def expand(dense, lists_ref, parts, first, act_ref):
    held, slots, rows, width = act_ref.shape
    tiles = lists_ref.shape[1] // parts
    for position in range(held):
        tile = held_group(first + position // tiles, parts) * tiles + position % tiles
        for slot in range(slots):
            lanes = pl.ds(pl.multiple_of(lists_ref[slot, tile] * width, width), width)
            dense[position * rows : (position + 1) * rows, lanes] = act_ref[position, slot]


def column_tiles(features):
    columns = 256 if features % 256 == 0 else features
    return [slice(first, first + columns) for first in range(0, features, columns)]


def early_kernel(parts, lists_ref, far_lists, own_early, own_late, far, decoder_hbm, far_dec, *refs):
    early_ref, late_ref, own, other, own_dec, sem = refs
    copy = pltpu.make_async_copy(decoder_hbm.at[0], own_dec, sem)
    copy.start()
    half, latents = other.shape
    own[...] = jnp.zeros_like(own)
    other[...] = jnp.zeros_like(other)
    expand(own.at[:half], lists_ref, parts, 0, own_early)
    expand(own.at[half:], lists_ref, parts, parts // 2, own_late)
    expand(other, far_lists, parts, 0, far)
    copy.wait()
    for lanes in column_tiles(early_ref.shape[1]):
        total = jnp.dot(own[...], own_dec[:, lanes], preferred_element_type=jnp.float32)
        late_ref[:, lanes] = total[half:]
        early_ref[:, lanes] = total[:half] + jnp.dot(
            other[...], far_dec[:latents, lanes], preferred_element_type=jnp.float32
        )


def decode_early(lists, far_lists, acts, decoder, far_decoder, parts):
    _, latents, features = decoder.shape
    half = acts[0].shape[0] * acts[0].shape[2]
    return pl.pallas_call(
        functools.partial(early_kernel, parts),
        out_shape=[jax.ShapeDtypeStruct((half, features), jnp.float32)] * 2,
        in_specs=[SMEM, SMEM] + [VMEM] * 3 + [ANY, VMEM],
        out_specs=[VMEM] * 2,
        scratch_shapes=[
            pltpu.VMEM((2 * half, latents), jnp.bfloat16),
            pltpu.VMEM((half, latents), jnp.bfloat16),
            pltpu.VMEM((latents, features), jnp.bfloat16),
            pltpu.SemaphoreType.DMA,
        ],
        cost_estimate=pl.CostEstimate(
            flops=6 * half * latents * features,
            bytes_accessed=2 * (2 * latents * features + 4 * half * features),
            transcendentals=0,
        ),
        **small("decode_early", 16),
    )(lists, far_lists, *acts, decoder, far_decoder)


def middle_kernel(parts, lists_ref, partial_ref, far, far_dec, total_ref, dense):
    latents = dense.shape[1]
    dense[...] = jnp.zeros_like(dense)
    expand(dense, lists_ref, parts, parts // 2, far)
    for lanes in column_tiles(partial_ref.shape[1]):
        total_ref[:, lanes] = partial_ref[:, lanes] + jnp.dot(
            dense[...], far_dec[:latents, lanes], preferred_element_type=jnp.float32
        )


def decode_middle(lists, partial, far, decoder, latents, parts):
    half, features = partial.shape
    return pl.pallas_call(
        functools.partial(middle_kernel, parts),
        out_shape=jax.ShapeDtypeStruct(partial.shape, partial.dtype),
        in_specs=[SMEM] + [VMEM] * 3,
        out_specs=VMEM,
        scratch_shapes=[pltpu.VMEM((half, latents), jnp.bfloat16)],
        cost_estimate=pl.CostEstimate(
            flops=2 * half * latents * features,
            bytes_accessed=2 * (latents * features + 4 * half * features),
            transcendentals=0,
        ),
        **small("decode_middle", 16),
    )(lists, partial, far, decoder)


def late_kernel(parts, lists_ref, early_ref, late_ref, near, near_dec, out_ref, dense, stage, sems):
    tokens, latents = dense.shape
    half, rows = tokens // 2, tokens // parts
    dense[...] = jnp.zeros_like(dense)
    expand(dense, lists_ref, parts, 0, near)
    copies = []
    for number, lanes in enumerate(column_tiles(early_ref.shape[1])):
        total = jnp.dot(dense[...], near_dec[:latents, lanes], preferred_element_type=jnp.float32)
        stage[:half, lanes] = (total[:half] + early_ref[:, lanes]).astype(stage.dtype)
        stage[half:, lanes] = (total[half:] + late_ref[:, lanes]).astype(stage.dtype)
        for held in range(parts):
            row = pl.multiple_of(held_group(held, parts) * rows, rows)
            copies.append(
                pltpu.make_async_copy(
                    stage.at[held * rows : (held + 1) * rows, lanes],
                    out_ref.at[pl.ds(row, rows), lanes],
                    sems.at[number, held],
                )
            )
            copies[-1].start()
    for copy in copies:
        copy.wait()


def decode_late(lists, early, late, near, decoder, latents, parts):
    half, features = early.shape
    return pl.pallas_call(
        functools.partial(late_kernel, parts),
        out_shape=jax.ShapeDtypeStruct((2 * half, features), jnp.bfloat16),
        in_specs=[SMEM] + [VMEM] * 4,
        out_specs=ANY,
        scratch_shapes=[
            pltpu.VMEM((2 * half, latents), jnp.bfloat16),
            pltpu.VMEM((2 * half, features), jnp.bfloat16),
            pltpu.SemaphoreType.DMA((len(column_tiles(features)), parts)),
        ],
        cost_estimate=pl.CostEstimate(
            flops=4 * half * latents * features,
            bytes_accessed=2 * (latents * features + 6 * half * features),
            transcendentals=0,
        ),
        **small("decode_late", 16),
    )(lists, early, late, near, decoder)


def shards(layer_input, enc_weight, enc_bias, dec_weight, block_lists, block_counts):
    parts = lax.axis_size("latent")
    x, encoder, decoder = layer_input[0], enc_weight[0], dec_weight[0]
    lists, counts = block_lists[0].T, block_counts[0]
    slots, tiles = lists.shape
    targets, latents, _ = decoder.shape
    if targets != 3 or parts < 2 or parts & (parts - 1):
        raise ValueError("mesh")

    with jax.named_scope("encoder_rows"):
        pieces = fetch_rows(encoder, parts)
        pieces, decoder = lax.optimization_barrier((pieces, decoder))
        weights = [pieces[0]] + [None] * (parts - 1)
        for step in sorted(range(1, parts), reverse=True):
            weights[step] = swapped(pieces[step], step)
    with jax.named_scope("decoder_weights"):
        near_rows, far_rows = fetch_decoders(lists, decoder)
        near_decoder, far_decoder = passed_along(near_rows, 1), passed_along(far_rows, 2)
        near_lists, far_lists = [
            rows[latents : latents + slots, :tiles].astype(jnp.int32) for rows in (near_decoder, far_decoder)
        ]

    with jax.named_scope("encode"):
        kept, sent = encode(lists, enc_bias, x, weights)
        arrived = swapped(sent, 1)
        step = 2
        while step < parts:
            kept, sent = merge(kept, arrived)
            arrived = swapped(sent, step)
            step *= 2
        own = activate(counts, kept, arrived, parts)
    with jax.named_scope("spread"):
        late_own = swapped(own, 1)
        far = passed_along(own, 2)
        late_far = passed_along(late_own, 2)
    with jax.named_scope("decode"):
        early, late = decode_early(lists, far_lists, [own, late_own, far], decoder, far_decoder, parts)
        early, late, late_far = lax.optimization_barrier((early, late, late_far))
        near = across_cores(choose([own, late_own], [far, late_far]))
        late = decode_middle(far_lists, late, late_far, far_decoder, latents, parts)
        return decode_late(near_lists, early, late, near, near_decoder, latents, parts)[None]


def solution(mesh):
    placed = (
        P("layer", None, "latent"),
        P("layer", None, "latent"),
        P("layer", "latent"),
        P("layer", None, None, "latent"),
        P("layer", None, None),
        P("layer", None),
    )
    return jax.shard_map(
        shards, mesh=mesh, in_specs=placed, out_specs=P("layer", None, "latent"), check_vma=False
    )
```

```python
import functools

import jax
import jax.numpy as jnp
from jax import lax
from jax.experimental import pallas as pl
from jax.experimental.pallas import tpu as pltpu
from jax.sharding import PartitionSpec as P

VMEM = pl.BlockSpec(memory_space=pltpu.VMEM)
SMEM = pl.BlockSpec(memory_space=pltpu.SMEM)
ANY = pl.BlockSpec(memory_space=pl.ANY)
HBM = pl.BlockSpec(memory_space=pltpu.HBM)


def swapped(value, step):
    count = lax.axis_size("latent")
    return lax.ppermute(value, "latent", [(i, i ^ step) for i in range(count)])


def rotated(value, step):
    count = lax.axis_size("latent")
    return lax.ppermute(value, "latent", [(i, (i + step) % count) for i in range(count)])


def passed_along(value, steps):
    count = lax.axis_size("layer")
    return lax.ppermute(value, "layer", [(i, i + steps) for i in range(count - steps)])


def across_cores(value):
    count = lax.axis_size("layer")
    return lax.ppermute(value, "layer", [(i, i ^ 1) for i in range(count)])


def small(name, megabytes=8):
    return dict(compiler_params=pltpu.CompilerParams(vmem_limit_bytes=megabytes << 20), name=name)


def held_group(number, parts):
    half = parts // 2
    parity = lax.bitwise_and(lax.axis_index("latent"), 1)
    return 2 * (number % half) + (parity if number < half else 1 - parity)


def fetch_rows_kernel(encoder_ref, *piece_refs):
    depth = piece_refs[0].shape[0]
    for step, piece in enumerate(piece_refs):
        first = pl.multiple_of(lax.rem(lax.axis_index("latent") + step, len(piece_refs)) * depth, depth)
        piece[...] = encoder_ref[pl.ds(first, depth), :]


def fetch_rows(encoder, parts):
    depth = encoder.shape[0] // parts
    return pl.pallas_call(
        fetch_rows_kernel,
        out_shape=[jax.ShapeDtypeStruct((depth, encoder.shape[1]), encoder.dtype)] * parts,
        in_specs=[VMEM],
        out_specs=[VMEM] * parts,
        **small("fetch_rows"),
    )(encoder)


def fetch_decoders_kernel(lists_ref, decoder_ref, *refs):
    out_refs, sems = refs[:-1], refs[-1]
    latents = decoder_ref.shape[1]
    copies = []
    for number, out_ref in enumerate(out_refs):
        copies.append(
            pltpu.make_async_copy(decoder_ref.at[number + 1], out_ref.at[pl.ds(0, latents)], sems.at[number])
        )
        copies[-1].start()
    for out_ref in out_refs:
        out_ref[latents:, :] = lists_ref[...]
    for copy in copies:
        copy.wait()


def fetch_decoders(lists, decoder):
    targets, latents, features = decoder.shape
    ids = jnp.pad(lists.astype(decoder.dtype), ((0, -lists.shape[0] % 16), (0, features - lists.shape[1])))
    shape = jax.ShapeDtypeStruct((latents + ids.shape[0], features), decoder.dtype)
    return pl.pallas_call(
        fetch_decoders_kernel,
        out_shape=[shape] * (targets - 1),
        in_specs=[VMEM, ANY],
        out_specs=[VMEM] * (targets - 1),
        scratch_shapes=[pltpu.SemaphoreType.DMA((targets - 1,))],
        **small("fetch_decoders", 58),
    )(ids, decoder)


def encode_kernel(parts, lists_ref, counts_ref, bias_ref, x_ref, *refs):
    weight_refs, (kept_ref, sent_ref, partial) = refs[:parts], refs[parts:]
    width = bias_ref.shape[1]
    held, slots, rows, _ = kept_ref.shape
    tiles = 2 * held // parts
    for first in range(0, parts, 2):
        stacked = jnp.concatenate([ref[...] for ref in weight_refs[first : first + 2]], axis=1)
        product = jnp.dot(x_ref[...], stacked, preferred_element_type=jnp.float32)
        for source in range(first, first + 2):
            block = product[:, (source - first) * width : (source - first + 1) * width]
            partial[source] = block if source else block + bias_ref[...]
    for out_ref, first in ((kept_ref, 0), (sent_ref, parts // 2)):
        for position in range(held):
            tile = held_group(first + position // tiles, parts) * tiles + position % tiles
            row = pl.multiple_of(tile * rows, rows)
            for slot in range(slots):
                source = lax.rem(lax.axis_index("latent") - lists_ref[slot, tile] + parts, parts)
                kept = partial[source, pl.ds(row, rows), :]
                if out_ref is kept_ref:
                    kept = kept + jnp.where(slot < counts_ref[tile], 0.0, -1e30)
                out_ref[position, slot] = kept.astype(out_ref.dtype)


def encode(lists, counts, bias, x, weights):
    parts = len(weights)
    tokens, depth = x.shape
    width = bias.shape[1]
    slots, tiles = lists.shape
    shape = (tiles // 2, slots, tokens // tiles, width)
    return pl.pallas_call(
        functools.partial(encode_kernel, parts),
        out_shape=[jax.ShapeDtypeStruct(shape, jnp.float32), jax.ShapeDtypeStruct(shape, jnp.bfloat16)],
        in_specs=[SMEM] * 2 + [VMEM] * (2 + parts),
        out_specs=[VMEM] * 2,
        scratch_shapes=[pltpu.VMEM((parts, tokens, width), jnp.float32)],
        cost_estimate=pl.CostEstimate(
            flops=2 * tokens * depth * parts * width,
            bytes_accessed=2 * (tokens * depth + depth * parts * width),
            transcendentals=0,
        ),
        **small("encode", 16),
    )(lists, counts, bias, x, *weights)


def merge_kernel(kept_ref, arrived_ref, total_ref, sent_ref):
    total = kept_ref[...] + arrived_ref[...].astype(jnp.float32)
    total_ref[...] = total
    sent_ref[...] = total.astype(sent_ref.dtype)


def merge(kept, arrived):
    return pl.pallas_call(
        merge_kernel,
        out_shape=[jax.ShapeDtypeStruct(kept.shape, kept.dtype), jax.ShapeDtypeStruct(kept.shape, arrived.dtype)],
        in_specs=[VMEM] * 2,
        out_specs=[VMEM] * 2,
        **small("merge"),
    )(kept, arrived)


def activate_kernel(kept_ref, arrived_ref, act_ref):
    preact = kept_ref[...] + arrived_ref[...].astype(jnp.float32)
    act_ref[...] = jnp.maximum(preact, 0.0).astype(act_ref.dtype)


def activate(kept, arrived):
    return pl.pallas_call(
        activate_kernel,
        out_shape=jax.ShapeDtypeStruct(kept.shape, arrived.dtype),
        in_specs=[VMEM] * 2,
        out_specs=VMEM,
        **small("activate"),
    )(kept, arrived)


def choose_kernel(*refs):
    sources, out_ref = refs[:-1], refs[-1]
    held = sources[0].shape[0]
    odd = lax.bitwise_and(lax.axis_index("layer"), 1)

    @pl.when(odd == 0)
    def _():
        out_ref[:held] = sources[0][...]
        out_ref[held:] = sources[1][...]

    @pl.when(odd == 1)
    def _():
        out_ref[:held] = sources[2][...]
        out_ref[held:] = sources[3][...]


def choose(own, far):
    shape = own[0].shape
    return pl.pallas_call(
        choose_kernel,
        out_shape=jax.ShapeDtypeStruct((2 * shape[0],) + shape[1:], own[0].dtype),
        in_specs=[VMEM] * 4,
        out_specs=VMEM,
        **small("choose"),
    )(*own, *far)


def expand(dense, lists_ref, parts, first, act_ref):
    held, slots, rows, width = act_ref.shape
    tiles = lists_ref.shape[1] // parts
    for position in range(held):
        tile = held_group(first + position // tiles, parts) * tiles + position % tiles
        for slot in range(slots):
            lanes = pl.ds(pl.multiple_of(lists_ref[slot, tile] * width, width), width)
            dense[position * rows : (position + 1) * rows, lanes] = act_ref[position, slot]


def column_tiles(features):
    columns = 256 if features % 256 == 0 else features
    return [slice(first, first + columns) for first in range(0, features, columns)]


def early_kernel(parts, lists_ref, far_lists, own_early, own_late, far, decoder_hbm, far_dec, *refs):
    early_ref, late_ref, own, other, own_dec, sem = refs
    copy = pltpu.make_async_copy(decoder_hbm.at[0], own_dec, sem)
    copy.start()
    half, latents = other.shape
    own[...] = jnp.zeros_like(own)
    other[...] = jnp.zeros_like(other)
    expand(own.at[:half], lists_ref, parts, 0, own_early)
    expand(own.at[half:], lists_ref, parts, parts // 2, own_late)
    expand(other, far_lists, parts, 0, far)
    copy.wait()
    for lanes in column_tiles(early_ref.shape[1]):
        total = jnp.dot(own[...], own_dec[:, lanes], preferred_element_type=jnp.float32)
        late_ref[:, lanes] = total[half:]
        early_ref[:, lanes] = total[:half] + jnp.dot(
            other[...], far_dec[:latents, lanes], preferred_element_type=jnp.float32
        )


def decode_early(lists, far_lists, acts, decoder, far_decoder, parts):
    _, latents, features = decoder.shape
    half = acts[0].shape[0] * acts[0].shape[2]
    return pl.pallas_call(
        functools.partial(early_kernel, parts),
        out_shape=[jax.ShapeDtypeStruct((half, features), jnp.float32)] * 2,
        in_specs=[SMEM, SMEM] + [VMEM] * 3 + [ANY, VMEM],
        out_specs=[VMEM] * 2,
        scratch_shapes=[
            pltpu.VMEM((2 * half, latents), jnp.bfloat16),
            pltpu.VMEM((half, latents), jnp.bfloat16),
            pltpu.VMEM((latents, features), jnp.bfloat16),
            pltpu.SemaphoreType.DMA,
        ],
        cost_estimate=pl.CostEstimate(
            flops=6 * half * latents * features,
            bytes_accessed=2 * (2 * latents * features + 4 * half * features),
            transcendentals=0,
        ),
        **small("decode_early", 16),
    )(lists, far_lists, *acts, decoder, far_decoder)


def middle_kernel(parts, lists_ref, partial_ref, far, far_dec, total_ref, dense):
    latents = dense.shape[1]
    dense[...] = jnp.zeros_like(dense)
    expand(dense, lists_ref, parts, parts // 2, far)
    for lanes in column_tiles(partial_ref.shape[1]):
        total_ref[:, lanes] = partial_ref[:, lanes] + jnp.dot(
            dense[...], far_dec[:latents, lanes], preferred_element_type=jnp.float32
        )


def decode_middle(lists, partial, far, decoder, latents, parts):
    half, features = partial.shape
    return pl.pallas_call(
        functools.partial(middle_kernel, parts),
        out_shape=jax.ShapeDtypeStruct(partial.shape, partial.dtype),
        in_specs=[SMEM] + [VMEM] * 3,
        out_specs=VMEM,
        scratch_shapes=[pltpu.VMEM((half, latents), jnp.bfloat16)],
        cost_estimate=pl.CostEstimate(
            flops=2 * half * latents * features,
            bytes_accessed=2 * (latents * features + 4 * half * features),
            transcendentals=0,
        ),
        **small("decode_middle", 16),
    )(lists, partial, far, decoder)


def late_kernel(parts, lists_ref, early_ref, late_ref, near, near_dec, out_ref, dense, stage, sems):
    tokens, latents = dense.shape
    half, rows = tokens // 2, tokens // parts
    dense[...] = jnp.zeros_like(dense)
    expand(dense, lists_ref, parts, 0, near)
    copies = []
    for number, lanes in enumerate(column_tiles(early_ref.shape[1])):
        total = jnp.dot(dense[...], near_dec[:latents, lanes], preferred_element_type=jnp.float32)
        stage[:half, lanes] = (total[:half] + early_ref[:, lanes]).astype(stage.dtype)
        stage[half:, lanes] = (total[half:] + late_ref[:, lanes]).astype(stage.dtype)
        for held in range(parts):
            row = pl.multiple_of(held_group(held, parts) * rows, rows)
            copies.append(
                pltpu.make_async_copy(
                    stage.at[held * rows : (held + 1) * rows, lanes],
                    out_ref.at[pl.ds(row, rows), lanes],
                    sems.at[number, held],
                )
            )
            copies[-1].start()
    for copy in copies:
        copy.wait()


def decode_late(lists, early, late, near, decoder, latents, parts):
    half, features = early.shape
    return pl.pallas_call(
        functools.partial(late_kernel, parts),
        out_shape=jax.ShapeDtypeStruct((2 * half, features), jnp.bfloat16),
        in_specs=[SMEM] + [VMEM] * 4,
        out_specs=ANY,
        scratch_shapes=[
            pltpu.VMEM((2 * half, latents), jnp.bfloat16),
            pltpu.VMEM((2 * half, features), jnp.bfloat16),
            pltpu.SemaphoreType.DMA((len(column_tiles(features)), parts)),
        ],
        cost_estimate=pl.CostEstimate(
            flops=4 * half * latents * features,
            bytes_accessed=2 * (latents * features + 6 * half * features),
            transcendentals=0,
        ),
        **small("decode_late", 16),
    )(lists, early, late, near, decoder)


def shards(layer_input, enc_weight, enc_bias, dec_weight, block_lists, block_counts):
    parts = lax.axis_size("latent")
    x, encoder, decoder = layer_input[0], enc_weight[0], dec_weight[0]
    lists, counts = block_lists[0].T, block_counts[0]
    slots, tiles = lists.shape
    targets, latents, _ = decoder.shape
    if targets != 3 or parts < 2 or parts & (parts - 1):
        raise ValueError("mesh")

    with jax.named_scope("encoder_rows"):
        pieces = fetch_rows(encoder, parts)
        pieces, decoder = lax.optimization_barrier((pieces, decoder))
        weights = [pieces[0]] + [None] * (parts - 1)
        for step in sorted(range(1, parts), reverse=True):
            weights[step] = rotated(pieces[step], step)
    with jax.named_scope("decoder_weights"):
        near_rows, far_rows = fetch_decoders(lists, decoder)
        near_decoder, far_decoder = passed_along(near_rows, 1), passed_along(far_rows, 2)
        near_lists, far_lists = [
            rows[latents : latents + slots, :tiles].astype(jnp.int32) for rows in (near_decoder, far_decoder)
        ]

    with jax.named_scope("encode"):
        kept, sent = encode(lists, counts, enc_bias, x, weights)
        arrived = swapped(sent, 1)
        step = 2
        while step < parts:
            kept, sent = merge(kept, arrived)
            arrived = swapped(sent, step)
            step *= 2
        own = activate(kept, arrived)
    with jax.named_scope("spread"):
        late_own = swapped(own, 1)
        far = passed_along(own, 2)
        late_far = passed_along(late_own, 2)
    with jax.named_scope("decode"):
        early, late = decode_early(lists, far_lists, [own, late_own, far], decoder, far_decoder, parts)
        early, late, late_far = lax.optimization_barrier((early, late, late_far))
        near = across_cores(choose([own, late_own], [far, late_far]))
        late = decode_middle(far_lists, late, late_far, far_decoder, latents, parts)
        return decode_late(near_lists, early, late, near, near_decoder, latents, parts)[None]


def solution(mesh):
    placed = (
        P("layer", None, "latent"),
        P("layer", None, "latent"),
        P("layer", "latent"),
        P("layer", None, None, "latent"),
        P("layer", None, None),
        P("layer", None),
    )
    return jax.shard_map(
        shards, mesh=mesh, in_specs=placed, out_specs=P("layer", None, "latent"), check_vma=False
    )
```

```python
import functools

import jax
import jax.numpy as jnp
from jax import lax
from jax.experimental import pallas as pl
from jax.experimental.pallas import tpu as pltpu
from jax.sharding import PartitionSpec as P

VMEM = pl.BlockSpec(memory_space=pltpu.VMEM)
SMEM = pl.BlockSpec(memory_space=pltpu.SMEM)
ANY = pl.BlockSpec(memory_space=pl.ANY)
HBM = pl.BlockSpec(memory_space=pltpu.HBM)


def swapped(value, step):
    count = lax.axis_size("latent")
    return lax.ppermute(value, "latent", [(i, i ^ step) for i in range(count)])


def rotated(value, step):
    count = lax.axis_size("latent")
    return lax.ppermute(value, "latent", [(i, (i + step) % count) for i in range(count)])


def passed_along(value, steps):
    count = lax.axis_size("layer")
    return lax.ppermute(value, "layer", [(i, i + steps) for i in range(count - steps)])


def across_cores(value):
    count = lax.axis_size("layer")
    return lax.ppermute(value, "layer", [(i, i ^ 1) for i in range(count)])


def small(name, megabytes=8):
    return dict(compiler_params=pltpu.CompilerParams(vmem_limit_bytes=megabytes << 20), name=name)


def held_group(number, parts):
    half = parts // 2
    parity = lax.bitwise_and(lax.axis_index("latent"), 1)
    return 2 * (number % half) + (parity if number < half else 1 - parity)


def fetch_rows_kernel(encoder_ref, *piece_refs):
    depth = piece_refs[0].shape[0]
    for step, piece in enumerate(piece_refs):
        first = pl.multiple_of(lax.rem(lax.axis_index("latent") + step, len(piece_refs)) * depth, depth)
        piece[...] = encoder_ref[pl.ds(first, depth), :]


def fetch_rows(encoder, parts):
    depth = encoder.shape[0] // parts
    return pl.pallas_call(
        fetch_rows_kernel,
        out_shape=[jax.ShapeDtypeStruct((depth, encoder.shape[1]), encoder.dtype)] * parts,
        in_specs=[VMEM],
        out_specs=[VMEM] * parts,
        **small("fetch_rows"),
    )(encoder)


def fetch_decoders_kernel(lists_ref, decoder_ref, *refs):
    out_refs, ids = refs[:-1], refs[-1]
    latents = decoder_ref.shape[1]
    slots, tiles = lists_ref.shape
    ids[...] = jnp.zeros_like(ids)
    ids[:slots, :tiles] = lists_ref[...].astype(jnp.float32)
    for number, out_ref in enumerate(out_refs):
        out_ref[:latents, :] = decoder_ref[number + 1]
        out_ref[latents:, :] = ids[...].astype(out_ref.dtype)


def fetch_decoders(lists, decoder):
    targets, latents, features = decoder.shape
    rows = lists.shape[0] + -lists.shape[0] % 16
    shape = jax.ShapeDtypeStruct((latents + rows, features), decoder.dtype)
    return pl.pallas_call(
        fetch_decoders_kernel,
        out_shape=[shape] * (targets - 1),
        in_specs=[VMEM, VMEM],
        out_specs=[VMEM] * (targets - 1),
        scratch_shapes=[pltpu.VMEM((rows, features), jnp.float32)],
        **small("fetch_decoders", 16),
    )(lists, decoder)


def encode_kernel(parts, lists_ref, counts_ref, bias_ref, x_ref, *refs):
    weight_refs, (kept_ref, sent_ref, partial) = refs[:parts], refs[parts:]
    width = bias_ref.shape[1]
    held, slots, rows, _ = kept_ref.shape
    tiles = 2 * held // parts
    for first in range(0, parts, 2):
        stacked = jnp.concatenate([ref[...] for ref in weight_refs[first : first + 2]], axis=1)
        product = jnp.dot(x_ref[...], stacked, preferred_element_type=jnp.float32)
        for source in range(first, first + 2):
            block = product[:, (source - first) * width : (source - first + 1) * width]
            partial[source] = block if source else block + bias_ref[...]
    for out_ref, first in ((kept_ref, 0), (sent_ref, parts // 2)):
        for position in range(held):
            tile = held_group(first + position // tiles, parts) * tiles + position % tiles
            row = pl.multiple_of(tile * rows, rows)
            for slot in range(slots):
                source = lax.rem(lax.axis_index("latent") - lists_ref[slot, tile] + parts, parts)
                kept = partial[source, pl.ds(row, rows), :]
                if out_ref is kept_ref:
                    kept = kept + jnp.where(slot < counts_ref[tile], 0.0, -1e30)
                out_ref[position, slot] = kept.astype(out_ref.dtype)


def encode(lists, counts, bias, x, weights):
    parts = len(weights)
    tokens, depth = x.shape
    width = bias.shape[1]
    slots, tiles = lists.shape
    shape = (tiles // 2, slots, tokens // tiles, width)
    return pl.pallas_call(
        functools.partial(encode_kernel, parts),
        out_shape=[jax.ShapeDtypeStruct(shape, jnp.float32), jax.ShapeDtypeStruct(shape, jnp.bfloat16)],
        in_specs=[SMEM] * 2 + [VMEM] * (2 + parts),
        out_specs=[VMEM] * 2,
        scratch_shapes=[pltpu.VMEM((parts, tokens, width), jnp.float32)],
        cost_estimate=pl.CostEstimate(
            flops=2 * tokens * depth * parts * width,
            bytes_accessed=2 * (tokens * depth + depth * parts * width),
            transcendentals=0,
        ),
        **small("encode", 16),
    )(lists, counts, bias, x, *weights)


def merge_kernel(kept_ref, arrived_ref, total_ref, sent_ref):
    total = kept_ref[...] + arrived_ref[...].astype(jnp.float32)
    total_ref[...] = total
    sent_ref[...] = total.astype(sent_ref.dtype)


def merge(kept, arrived):
    return pl.pallas_call(
        merge_kernel,
        out_shape=[jax.ShapeDtypeStruct(kept.shape, kept.dtype), jax.ShapeDtypeStruct(kept.shape, arrived.dtype)],
        in_specs=[VMEM] * 2,
        out_specs=[VMEM] * 2,
        **small("merge"),
    )(kept, arrived)


def activate_kernel(kept_ref, arrived_ref, act_ref):
    preact = kept_ref[...] + arrived_ref[...].astype(jnp.float32)
    act_ref[...] = jnp.maximum(preact, 0.0).astype(act_ref.dtype)


def activate(kept, arrived):
    return pl.pallas_call(
        activate_kernel,
        out_shape=jax.ShapeDtypeStruct(kept.shape, arrived.dtype),
        in_specs=[VMEM] * 2,
        out_specs=VMEM,
        **small("activate"),
    )(kept, arrived)


def choose_kernel(*refs):
    sources, out_ref = refs[:-1], refs[-1]
    held = sources[0].shape[0]
    odd = lax.bitwise_and(lax.axis_index("layer"), 1)

    @pl.when(odd == 0)
    def _():
        out_ref[:held] = sources[0][...]
        out_ref[held:] = sources[1][...]

    @pl.when(odd == 1)
    def _():
        out_ref[:held] = sources[2][...]
        out_ref[held:] = sources[3][...]


def choose(own, far):
    shape = own[0].shape
    return pl.pallas_call(
        choose_kernel,
        out_shape=jax.ShapeDtypeStruct((2 * shape[0],) + shape[1:], own[0].dtype),
        in_specs=[VMEM] * 4,
        out_specs=VMEM,
        **small("choose"),
    )(*own, *far)


def expand(dense, lists_ref, parts, first, act_ref):
    held, slots, rows, width = act_ref.shape
    tiles = lists_ref.shape[1] // parts
    for position in range(held):
        tile = held_group(first + position // tiles, parts) * tiles + position % tiles
        for slot in range(slots):
            lanes = pl.ds(pl.multiple_of(lists_ref[slot, tile] * width, width), width)
            dense[position * rows : (position + 1) * rows, lanes] = act_ref[position, slot]


def column_tiles(features):
    columns = 256 if features % 256 == 0 else features
    return [slice(first, first + columns) for first in range(0, features, columns)]


def early_kernel(parts, lists_ref, far_lists, own_early, own_late, far, decoder_hbm, far_dec, *refs):
    early_ref, late_ref, own, other, own_dec, sem = refs
    copy = pltpu.make_async_copy(decoder_hbm.at[0], own_dec, sem)
    copy.start()
    half, latents = other.shape
    own[...] = jnp.zeros_like(own)
    other[...] = jnp.zeros_like(other)
    expand(own.at[:half], lists_ref, parts, 0, own_early)
    expand(own.at[half:], lists_ref, parts, parts // 2, own_late)
    expand(other, far_lists, parts, 0, far)
    copy.wait()
    for lanes in column_tiles(early_ref.shape[1]):
        total = jnp.dot(own[...], own_dec[:, lanes], preferred_element_type=jnp.float32)
        late_ref[:, lanes] = total[half:]
        early_ref[:, lanes] = total[:half] + jnp.dot(
            other[...], far_dec[:latents, lanes], preferred_element_type=jnp.float32
        )


def decode_early(lists, far_lists, acts, decoder, far_decoder, parts):
    _, latents, features = decoder.shape
    half = acts[0].shape[0] * acts[0].shape[2]
    return pl.pallas_call(
        functools.partial(early_kernel, parts),
        out_shape=[jax.ShapeDtypeStruct((half, features), jnp.float32)] * 2,
        in_specs=[SMEM, SMEM] + [VMEM] * 3 + [ANY, VMEM],
        out_specs=[VMEM] * 2,
        scratch_shapes=[
            pltpu.VMEM((2 * half, latents), jnp.bfloat16),
            pltpu.VMEM((half, latents), jnp.bfloat16),
            pltpu.VMEM((latents, features), jnp.bfloat16),
            pltpu.SemaphoreType.DMA,
        ],
        cost_estimate=pl.CostEstimate(
            flops=6 * half * latents * features,
            bytes_accessed=2 * (2 * latents * features + 4 * half * features),
            transcendentals=0,
        ),
        **small("decode_early", 16),
    )(lists, far_lists, *acts, decoder, far_decoder)


def middle_kernel(parts, lists_ref, partial_ref, far, far_dec, total_ref, dense):
    latents = dense.shape[1]
    dense[...] = jnp.zeros_like(dense)
    expand(dense, lists_ref, parts, parts // 2, far)
    for lanes in column_tiles(partial_ref.shape[1]):
        total_ref[:, lanes] = partial_ref[:, lanes] + jnp.dot(
            dense[...], far_dec[:latents, lanes], preferred_element_type=jnp.float32
        )


def decode_middle(lists, partial, far, decoder, latents, parts):
    half, features = partial.shape
    return pl.pallas_call(
        functools.partial(middle_kernel, parts),
        out_shape=jax.ShapeDtypeStruct(partial.shape, partial.dtype),
        in_specs=[SMEM] + [VMEM] * 3,
        out_specs=VMEM,
        scratch_shapes=[pltpu.VMEM((half, latents), jnp.bfloat16)],
        cost_estimate=pl.CostEstimate(
            flops=2 * half * latents * features,
            bytes_accessed=2 * (latents * features + 4 * half * features),
            transcendentals=0,
        ),
        **small("decode_middle", 16),
    )(lists, partial, far, decoder)


def late_kernel(parts, lists_ref, early_ref, late_ref, near, near_dec, out_ref, dense, stage, sems):
    tokens, latents = dense.shape
    half, rows = tokens // 2, tokens // parts
    dense[...] = jnp.zeros_like(dense)
    expand(dense, lists_ref, parts, 0, near)
    copies = []
    for number, lanes in enumerate(column_tiles(early_ref.shape[1])):
        total = jnp.dot(dense[...], near_dec[:latents, lanes], preferred_element_type=jnp.float32)
        stage[:half, lanes] = (total[:half] + early_ref[:, lanes]).astype(stage.dtype)
        stage[half:, lanes] = (total[half:] + late_ref[:, lanes]).astype(stage.dtype)
        for held in range(parts):
            row = pl.multiple_of(held_group(held, parts) * rows, rows)
            copies.append(
                pltpu.make_async_copy(
                    stage.at[held * rows : (held + 1) * rows, lanes],
                    out_ref.at[pl.ds(row, rows), lanes],
                    sems.at[number, held],
                )
            )
            copies[-1].start()
    for copy in copies:
        copy.wait()


def decode_late(lists, early, late, near, decoder, latents, parts):
    half, features = early.shape
    return pl.pallas_call(
        functools.partial(late_kernel, parts),
        out_shape=jax.ShapeDtypeStruct((2 * half, features), jnp.bfloat16),
        in_specs=[SMEM] + [VMEM] * 4,
        out_specs=ANY,
        scratch_shapes=[
            pltpu.VMEM((2 * half, latents), jnp.bfloat16),
            pltpu.VMEM((2 * half, features), jnp.bfloat16),
            pltpu.SemaphoreType.DMA((len(column_tiles(features)), parts)),
        ],
        cost_estimate=pl.CostEstimate(
            flops=4 * half * latents * features,
            bytes_accessed=2 * (latents * features + 6 * half * features),
            transcendentals=0,
        ),
        **small("decode_late", 16),
    )(lists, early, late, near, decoder)


def shards(layer_input, enc_weight, enc_bias, dec_weight, block_lists, block_counts):
    parts = lax.axis_size("latent")
    x, encoder, decoder = layer_input[0], enc_weight[0], dec_weight[0]
    lists, counts = block_lists[0].T, block_counts[0]
    slots, tiles = lists.shape
    targets, latents, _ = decoder.shape
    if targets != 3 or parts < 2 or parts & (parts - 1):
        raise ValueError("mesh")

    with jax.named_scope("encoder_rows"):
        pieces = fetch_rows(encoder, parts)
        pieces, decoder = lax.optimization_barrier((pieces, decoder))
        weights = [pieces[0]] + [None] * (parts - 1)
        for step in sorted(range(1, parts), reverse=True):
            weights[step] = rotated(pieces[step], step)
    with jax.named_scope("decoder_weights"):
        near_rows, far_rows = fetch_decoders(lists, decoder)
        near_decoder, far_decoder = passed_along(near_rows, 1), passed_along(far_rows, 2)
        near_decoder, far_decoder = lax.optimization_barrier((near_decoder, far_decoder))
        near_lists, far_lists = [
            rows[latents : latents + slots, :tiles].astype(jnp.int32) for rows in (near_decoder, far_decoder)
        ]

    with jax.named_scope("encode"):
        kept, sent = encode(lists, counts, enc_bias, x, weights)
        arrived = swapped(sent, 1)
        step = 2
        while step < parts:
            kept, sent = merge(kept, arrived)
            arrived = swapped(sent, step)
            step *= 2
        own = activate(kept, arrived)
    with jax.named_scope("spread"):
        late_own = swapped(own, 1)
        far = passed_along(own, 2)
        late_far = passed_along(late_own, 2)
    with jax.named_scope("decode"):
        early, late = decode_early(lists, far_lists, [own, late_own, far], decoder, far_decoder, parts)
        early, late, late_far = lax.optimization_barrier((early, late, late_far))
        near = across_cores(choose([own, late_own], [far, late_far]))
        late = decode_middle(far_lists, late, late_far, far_decoder, latents, parts)
        return decode_late(near_lists, early, late, near, near_decoder, latents, parts)[None]


def solution(mesh):
    placed = (
        P("layer", None, "latent"),
        P("layer", None, "latent"),
        P("layer", "latent"),
        P("layer", None, None, "latent"),
        P("layer", None, None),
        P("layer", None),
    )
    return jax.shard_map(
        shards, mesh=mesh, in_specs=placed, out_specs=P("layer", None, "latent"), check_vma=False
    )
```

```python
import functools

import jax
import jax.numpy as jnp
from jax import lax
from jax.experimental import pallas as pl
from jax.experimental.pallas import tpu as pltpu
from jax.sharding import PartitionSpec as P

VMEM = pl.BlockSpec(memory_space=pltpu.VMEM)
SMEM = pl.BlockSpec(memory_space=pltpu.SMEM)
ANY = pl.BlockSpec(memory_space=pl.ANY)
HBM = pl.BlockSpec(memory_space=pltpu.HBM)


def swapped(value, step):
    count = lax.axis_size("latent")
    return lax.ppermute(value, "latent", [(i, i ^ step) for i in range(count)])


def passed_along(value, steps):
    count = lax.axis_size("layer")
    return lax.ppermute(value, "layer", [(i, i + steps) for i in range(count - steps)])


def across_cores(value):
    count = lax.axis_size("layer")
    return lax.ppermute(value, "layer", [(i, i ^ 1) for i in range(count)])


def small(name, megabytes=8):
    return dict(compiler_params=pltpu.CompilerParams(vmem_limit_bytes=megabytes << 20), name=name)


def held_tile(position, tiles, parts):
    each = tiles // parts
    number, half = position // each, parts // 2
    parity = lax.bitwise_and(lax.axis_index("latent"), 1)
    return (2 * (number % half) + (parity if number < half else 1 - parity)) * each + position % each


def fetch_rows_kernel(encoder_ref, *piece_refs):
    depth = piece_refs[0].shape[0]
    for step, piece in enumerate(piece_refs):
        first = pl.multiple_of(lax.bitwise_xor(lax.axis_index("latent"), step) * depth, depth)
        piece[...] = encoder_ref[pl.ds(first, depth), :]


def fetch_rows(encoder, parts):
    depth = encoder.shape[0] // parts
    return pl.pallas_call(
        fetch_rows_kernel,
        out_shape=[jax.ShapeDtypeStruct((depth, encoder.shape[1]), encoder.dtype)] * parts,
        in_specs=[VMEM],
        out_specs=[VMEM] * parts,
        **small("fetch_rows"),
    )(encoder)


def fetch_decoders_kernel(lists_ref, decoder_ref, *refs):
    out_refs, ids = refs[:-1], refs[-1]
    latents = decoder_ref.shape[1]
    slots, tiles = lists_ref.shape
    ids[...] = jnp.zeros_like(ids)
    ids[:slots, :tiles] = lists_ref[...].astype(jnp.float32)
    for number, out_ref in enumerate(out_refs):
        out_ref[:latents, :] = decoder_ref[number + 1]
        out_ref[latents:, :] = ids[...].astype(out_ref.dtype)


def fetch_decoders(lists, decoder):
    targets, latents, features = decoder.shape
    rows = lists.shape[0] + -lists.shape[0] % 16
    shape = jax.ShapeDtypeStruct((latents + rows, features), decoder.dtype)
    return pl.pallas_call(
        fetch_decoders_kernel,
        out_shape=[shape] * (targets - 1),
        in_specs=[VMEM, VMEM],
        out_specs=[VMEM] * (targets - 1),
        scratch_shapes=[pltpu.VMEM((rows, features), jnp.float32)],
        **small("fetch_decoders", 16),
    )(lists, decoder)


def encode_kernel(parts, lists_ref, counts_ref, bias_ref, x_ref, *refs):
    weight_refs, out_refs, partial = refs[:parts], refs[parts:-1], refs[-1]
    width = bias_ref.shape[1]
    count, slots, rows, _ = out_refs[0].shape
    tiles = lists_ref.shape[1]
    for first in range(0, parts, 2):
        stacked = jnp.concatenate([ref[...] for ref in weight_refs[first : first + 2]], axis=1)
        product = jnp.dot(x_ref[...], stacked, preferred_element_type=jnp.float32)
        for source in range(first, first + 2):
            block = product[:, (source - first) * width : (source - first + 1) * width]
            partial[source] = block if source else block + bias_ref[...]
    for number, out_ref in enumerate(out_refs):
        for position in range(count):
            tile = held_tile(number * count + position, tiles, parts)
            row = pl.multiple_of(tile * rows, rows)
            for slot in range(slots):
                source = lax.bitwise_xor(lax.axis_index("latent"), lists_ref[slot, tile])
                kept = partial[source, pl.ds(row, rows), :]
                if number < 2:
                    kept = kept + jnp.where(slot < counts_ref[tile], 0.0, -1e30)
                out_ref[position, slot] = kept.astype(out_ref.dtype)


def encode(lists, counts, bias, x, weights):
    parts = len(weights)
    tokens, depth = x.shape
    width = bias.shape[1]
    slots, tiles = lists.shape
    shape = (tiles // 4, slots, tokens // tiles, width)
    return pl.pallas_call(
        functools.partial(encode_kernel, parts),
        out_shape=[jax.ShapeDtypeStruct(shape, jnp.float32)] * 2 + [jax.ShapeDtypeStruct(shape, jnp.bfloat16)] * 2,
        in_specs=[SMEM] * 2 + [VMEM] * (2 + parts),
        out_specs=[VMEM] * 4,
        scratch_shapes=[pltpu.VMEM((parts, tokens, width), jnp.float32)],
        cost_estimate=pl.CostEstimate(
            flops=32 * tokens * depth * parts * width,
            bytes_accessed=2 * (tokens * depth + depth * parts * width),
            transcendentals=0,
        ),
        **small("encode", 16),
    )(lists, counts, bias, x, *weights)


def merge_kernel(kept_ref, arrived_ref, total_ref, sent_ref):
    total = kept_ref[...] + arrived_ref[...].astype(jnp.float32)
    total_ref[...] = total
    sent_ref[...] = total.astype(sent_ref.dtype)


def merge(kept, arrived):
    return pl.pallas_call(
        merge_kernel,
        out_shape=[jax.ShapeDtypeStruct(kept.shape, kept.dtype), jax.ShapeDtypeStruct(kept.shape, arrived.dtype)],
        in_specs=[VMEM] * 2,
        out_specs=[VMEM] * 2,
        **small("merge"),
    )(kept, arrived)


def activate_kernel(kept_ref, arrived_ref, act_ref):
    preact = kept_ref[...] + arrived_ref[...].astype(jnp.float32)
    act_ref[...] = jnp.maximum(preact, 0.0).astype(act_ref.dtype)


def activate(kept, arrived):
    return pl.pallas_call(
        activate_kernel,
        out_shape=jax.ShapeDtypeStruct(kept.shape, arrived.dtype),
        in_specs=[VMEM] * 2,
        out_specs=VMEM,
        **small("activate"),
    )(kept, arrived)


def choose_kernel(*refs):
    sources, out_ref = refs[:-1], refs[-1]
    count = sources[0].shape[0]
    odd = lax.bitwise_and(lax.axis_index("layer"), 1)

    @pl.when(odd == 0)
    def _():
        for number in range(4):
            out_ref[number * count : (number + 1) * count] = sources[number][...]

    @pl.when(odd == 1)
    def _():
        out_ref[:count] = sources[4][...]
        out_ref[count : 3 * count] = sources[5][...]
        out_ref[3 * count :] = sources[6][...]


def choose(own, far):
    shape = own[0].shape
    return pl.pallas_call(
        choose_kernel,
        out_shape=jax.ShapeDtypeStruct((4 * shape[0],) + shape[1:], own[0].dtype),
        in_specs=[VMEM] * 7,
        out_specs=VMEM,
        **small("choose"),
    )(*own, *far)


def join_kernel(first_ref, second_ref, out_ref):
    count = first_ref.shape[0]
    out_ref[:count] = first_ref[...]
    out_ref[count:] = second_ref[...]


def join(first, second):
    return pl.pallas_call(
        join_kernel,
        out_shape=jax.ShapeDtypeStruct((2 * first.shape[0],) + first.shape[1:], first.dtype),
        in_specs=[VMEM] * 2,
        out_specs=VMEM,
        **small("join"),
    )(first, second)


def expand(dense, lists_ref, parts, first, act_refs):
    row = 0
    for act_ref in act_refs:
        count, slots, rows, width = act_ref.shape
        for position in range(count):
            tile = held_tile(first + position, lists_ref.shape[1], parts)
            for slot in range(slots):
                lanes = pl.ds(pl.multiple_of(lists_ref[slot, tile] * width, width), width)
                dense[row : row + rows, lanes] = act_ref[position, slot]
            row += rows
        first += count


def column_tiles(features):
    columns = 256 if features % 256 == 0 else features
    return [slice(first, first + columns) for first in range(0, features, columns)]


def early_kernel(parts, lists_ref, far_lists, *refs):
    own_refs, far_refs, (decoder_hbm, far_dec), refs = refs[:4], refs[4:6], refs[6:8], refs[8:]
    early_ref, late_a, late_b, own, other, own_dec, sem = refs
    copy = pltpu.make_async_copy(decoder_hbm.at[0], own_dec, sem)
    copy.start()
    quarter, latents = late_a.shape[0], own.shape[1]
    own[...] = jnp.zeros_like(own)
    other[...] = jnp.zeros_like(other)
    expand(own, lists_ref, parts, 0, own_refs)
    expand(other, far_lists, parts, 0, far_refs)
    copy.wait()
    for lanes in column_tiles(early_ref.shape[1]):
        total = jnp.dot(own[...], own_dec[:, lanes], preferred_element_type=jnp.float32)
        late_b[:, lanes] = total[3 * quarter :]
        total = total[: 3 * quarter] + jnp.dot(
            other[...], far_dec[:latents, lanes], preferred_element_type=jnp.float32
        )
        early_ref[:, lanes] = total[: 2 * quarter]
        late_a[:, lanes] = total[2 * quarter :]


def decode_early(lists, far_lists, acts, decoder, far_decoder, parts):
    _, latents, features = decoder.shape
    quarter = acts[0].shape[0] * acts[0].shape[2]
    return pl.pallas_call(
        functools.partial(early_kernel, parts),
        out_shape=[jax.ShapeDtypeStruct((count * quarter, features), jnp.float32) for count in (2, 1, 1)],
        in_specs=[SMEM, SMEM] + [VMEM] * 6 + [ANY, VMEM],
        out_specs=[VMEM] * 3,
        scratch_shapes=[
            pltpu.VMEM((4 * quarter, latents), jnp.bfloat16),
            pltpu.VMEM((3 * quarter, latents), jnp.bfloat16),
            pltpu.VMEM((latents, features), jnp.bfloat16),
            pltpu.SemaphoreType.DMA,
        ],
        cost_estimate=pl.CostEstimate(
            flops=14 * quarter * latents * features,
            bytes_accessed=2 * (2 * latents * features + 8 * quarter * features),
            transcendentals=0,
        ),
        **small("decode_early", 16),
    )(lists, far_lists, *acts, decoder, far_decoder)


def middle_kernel(parts, lists_ref, partial_ref, far, far_dec, total_ref, dense):
    latents = dense.shape[1]
    dense[...] = jnp.zeros_like(dense)
    expand(dense, lists_ref, parts, 3 * far.shape[0], [far])
    for lanes in column_tiles(partial_ref.shape[1]):
        total_ref[:, lanes] = partial_ref[:, lanes] + jnp.dot(
            dense[...], far_dec[:latents, lanes], preferred_element_type=jnp.float32
        )


def decode_middle(lists, partial, far, decoder, latents, parts):
    quarter, features = partial.shape
    return pl.pallas_call(
        functools.partial(middle_kernel, parts),
        out_shape=jax.ShapeDtypeStruct(partial.shape, partial.dtype),
        in_specs=[SMEM] + [VMEM] * 3,
        out_specs=VMEM,
        scratch_shapes=[pltpu.VMEM((quarter, latents), jnp.bfloat16)],
        cost_estimate=pl.CostEstimate(
            flops=2 * quarter * latents * features,
            bytes_accessed=2 * (latents * features + 4 * quarter * features),
            transcendentals=0,
        ),
        **small("decode_middle", 16),
    )(lists, partial, far, decoder)


def late_kernel(parts, lists_ref, early_ref, late_a, late_b, near, near_dec, out_ref, dense, stage, sems):
    tokens, latents = dense.shape
    quarter, rows = tokens // 4, tokens // parts
    dense[...] = jnp.zeros_like(dense)
    expand(dense, lists_ref, parts, 0, [near])
    copies = []
    for number, lanes in enumerate(column_tiles(early_ref.shape[1])):
        total = jnp.dot(dense[...], near_dec[:latents, lanes], preferred_element_type=jnp.float32)
        before = ((0, early_ref), (2 * quarter, late_a), (3 * quarter, late_b))
        for first, ref in before:
            last = first + ref.shape[0]
            stage[first:last, lanes] = (total[first:last] + ref[:, lanes]).astype(stage.dtype)
        for held in range(parts):
            tiles = lists_ref.shape[1]
            row = pl.multiple_of(held_tile(held * (tiles // parts), tiles, parts) * (tokens // tiles), rows)
            copies.append(
                pltpu.make_async_copy(
                    stage.at[held * rows : (held + 1) * rows, lanes],
                    out_ref.at[pl.ds(row, rows), lanes],
                    sems.at[number, held],
                )
            )
            copies[-1].start()
    for copy in copies:
        copy.wait()


def decode_late(lists, partials, near, decoder, latents, parts):
    features = decoder.shape[1]
    tokens = near.shape[0] * near.shape[2]
    return pl.pallas_call(
        functools.partial(late_kernel, parts),
        out_shape=jax.ShapeDtypeStruct((tokens, features), jnp.bfloat16),
        in_specs=[SMEM] + [VMEM] * 5,
        out_specs=ANY,
        scratch_shapes=[
            pltpu.VMEM((tokens, latents), jnp.bfloat16),
            pltpu.VMEM((tokens, features), jnp.bfloat16),
            pltpu.SemaphoreType.DMA((len(column_tiles(features)), parts)),
        ],
        cost_estimate=pl.CostEstimate(
            flops=2 * tokens * latents * features,
            bytes_accessed=2 * (latents * features + 3 * tokens * features),
            transcendentals=0,
        ),
        **small("decode_late", 16),
    )(lists, *partials, near, decoder)


def shards(layer_input, enc_weight, enc_bias, dec_weight, block_lists, block_counts):
    parts = lax.axis_size("latent")
    x, encoder, decoder = layer_input[0], enc_weight[0], dec_weight[0]
    lists, counts = block_lists[0].T, block_counts[0]
    slots, tiles = lists.shape
    targets, latents, _ = decoder.shape
    if targets != 3 or parts < 2 or parts & (parts - 1) or tiles % 4:
        raise ValueError("mesh")

    with jax.named_scope("encoder_rows"):
        pieces = fetch_rows(encoder, parts)
        pieces, decoder = lax.optimization_barrier((pieces, decoder))
        weights = [pieces[0]] + [None] * (parts - 1)
        for step in sorted(range(1, parts), reverse=True):
            weights[step] = swapped(pieces[step], step)
    with jax.named_scope("decoder_weights"):
        near_rows, far_rows = fetch_decoders(lists, decoder)
        near_decoder, far_decoder = passed_along(near_rows, 1), passed_along(far_rows, 2)
        near_decoder, far_decoder = lax.optimization_barrier((near_decoder, far_decoder))
        near_lists, far_lists = [
            rows[latents : latents + slots, :tiles].astype(jnp.int32) for rows in (near_decoder, far_decoder)
        ]

    with jax.named_scope("encode"):
        kept_a, kept_b, sent_a, sent_b = encode(lists, counts, enc_bias, x, weights)
        arrived_a, arrived_b = swapped(sent_a, 1), swapped(sent_b, 1)
        step = 2
        while step < parts:
            kept_a, sent_a = merge(kept_a, arrived_a)
            kept_b, sent_b = merge(kept_b, arrived_b)
            arrived_a, arrived_b = swapped(sent_a, step), swapped(sent_b, step)
            step *= 2
        own_a, own_b = activate(kept_a, arrived_a), activate(kept_b, arrived_b)
    with jax.named_scope("spread"):
        late_a, late_b = swapped(own_a, 1), swapped(own_b, 1)
        own = [own_a, own_b, late_a, late_b]
        far_a = passed_along(own_a, 2)
        late_a, far_a = lax.optimization_barrier((late_a, far_a))
        far = [far_a] + [passed_along(piece, 2) for piece in (join(own_b, late_a), late_b)]
    with jax.named_scope("decode"):
        early, late_a, late_b = decode_early(lists, far_lists, own + far[:2], decoder, far_decoder, parts)
        early, late_a, late_b, far[2] = lax.optimization_barrier((early, late_a, late_b, far[2]))
        near = across_cores(choose(own, far))
        late_b = decode_middle(far_lists, late_b, far[2], far_decoder, latents, parts)
        return decode_late(near_lists, [early, late_a, late_b], near, near_decoder, latents, parts)[None]


def solution(mesh):
    placed = (
        P("layer", None, "latent"),
        P("layer", None, "latent"),
        P("layer", "latent"),
        P("layer", None, None, "latent"),
        P("layer", None, None),
        P("layer", None),
    )
    return jax.shard_map(
        shards, mesh=mesh, in_specs=placed, out_specs=P("layer", None, "latent"), check_vma=False
    )
```

```python
import functools

import jax
import jax.numpy as jnp
from jax import lax
from jax.experimental import pallas as pl
from jax.experimental.pallas import tpu as pltpu
from jax.sharding import PartitionSpec as P

VMEM = pl.BlockSpec(memory_space=pltpu.VMEM)
SMEM = pl.BlockSpec(memory_space=pltpu.SMEM)
ANY = pl.BlockSpec(memory_space=pl.ANY)
HBM = pl.BlockSpec(memory_space=pltpu.HBM)


def swapped(value, step):
    count = lax.axis_size("latent")
    return lax.ppermute(value, "latent", [(i, i ^ step) for i in range(count)])


def passed_along(value, steps):
    count = lax.axis_size("layer")
    return lax.ppermute(value, "layer", [(i, i + steps) for i in range(count - steps)])


def across_cores(value):
    count = lax.axis_size("layer")
    return lax.ppermute(value, "layer", [(i, i ^ 1) for i in range(count)])


def small(name, megabytes=8):
    return dict(compiler_params=pltpu.CompilerParams(vmem_limit_bytes=megabytes << 20), name=name)


def held_tile(position, tiles, parts):
    each = tiles // parts
    number, half = position // each, parts // 2
    parity = lax.bitwise_and(lax.axis_index("latent"), 1)
    return (2 * (number % half) + (parity if number < half else 1 - parity)) * each + position % each


def fetch_rows_kernel(encoder_ref, *piece_refs):
    depth = piece_refs[0].shape[0]
    for step, piece in enumerate(piece_refs):
        first = pl.multiple_of(lax.bitwise_xor(lax.axis_index("latent"), step) * depth, depth)
        piece[...] = encoder_ref[pl.ds(first, depth), :]


def fetch_rows(encoder, parts):
    depth = encoder.shape[0] // parts
    return pl.pallas_call(
        fetch_rows_kernel,
        out_shape=[jax.ShapeDtypeStruct((depth, encoder.shape[1]), encoder.dtype)] * parts,
        in_specs=[VMEM],
        out_specs=[VMEM] * parts,
        **small("fetch_rows"),
    )(encoder)


def fetch_decoders_kernel(lists_ref, decoder_ref, *refs):
    out_refs, ids = refs[:-1], refs[-1]
    latents = decoder_ref.shape[1]
    slots, tiles = lists_ref.shape
    ids[...] = jnp.zeros_like(ids)
    ids[:slots, :tiles] = lists_ref[...].astype(jnp.float32)
    for number, out_ref in enumerate(out_refs):
        out_ref[:latents, :] = decoder_ref[number + 1]
        out_ref[latents:, :] = ids[...].astype(out_ref.dtype)


def fetch_decoders(lists, decoder):
    targets, latents, features = decoder.shape
    rows = lists.shape[0] + -lists.shape[0] % 16
    shape = jax.ShapeDtypeStruct((latents + rows, features), decoder.dtype)
    return pl.pallas_call(
        fetch_decoders_kernel,
        out_shape=[shape] * (targets - 1),
        in_specs=[VMEM, VMEM],
        out_specs=[VMEM] * (targets - 1),
        scratch_shapes=[pltpu.VMEM((rows, features), jnp.float32)],
        **small("fetch_decoders", 16),
    )(lists, decoder)


def encode_kernel(parts, lists_ref, counts_ref, bias_ref, x_ref, *refs):
    weight_refs, out_refs, partial = refs[:parts], refs[parts:-1], refs[-1]
    width = bias_ref.shape[1]
    count, slots, rows, _ = out_refs[0].shape
    tiles = lists_ref.shape[1]
    for first in range(0, parts, 2):
        stacked = jnp.concatenate([ref[...] for ref in weight_refs[first : first + 2]], axis=1)
        product = jnp.dot(x_ref[...], stacked, preferred_element_type=jnp.float32)
        for source in range(first, first + 2):
            block = product[:, (source - first) * width : (source - first + 1) * width]
            partial[source] = block if source else block + bias_ref[...]
    for number, out_ref in enumerate(out_refs):
        for position in range(count):
            tile = held_tile(number * count + position, tiles, parts)
            row = pl.multiple_of(tile * rows, rows)
            for slot in range(slots):
                source = lax.bitwise_xor(lax.axis_index("latent"), lists_ref[slot, tile])
                kept = partial[source, pl.ds(row, rows), :]
                if number < 2:
                    kept = kept + jnp.where(slot < counts_ref[tile], 0.0, -1e30)
                out_ref[position, slot] = kept.astype(out_ref.dtype)


def encode(lists, counts, bias, x, weights):
    parts = len(weights)
    tokens, depth = x.shape
    width = bias.shape[1]
    slots, tiles = lists.shape
    shape = (tiles // 4, slots, tokens // tiles, width)
    return pl.pallas_call(
        functools.partial(encode_kernel, parts),
        out_shape=[jax.ShapeDtypeStruct(shape, jnp.float32)] * 2 + [jax.ShapeDtypeStruct(shape, jnp.bfloat16)] * 2,
        in_specs=[SMEM] * 2 + [VMEM] * (2 + parts),
        out_specs=[VMEM] * 4,
        scratch_shapes=[pltpu.VMEM((parts, tokens, width), jnp.float32)],
        cost_estimate=pl.CostEstimate(
            flops=32 * tokens * depth * parts * width,
            bytes_accessed=2 * (tokens * depth + depth * parts * width),
            transcendentals=0,
        ),
        **small("encode", 16),
    )(lists, counts, bias, x, *weights)


def merge_kernel(kept_ref, arrived_ref, total_ref, sent_ref):
    total = kept_ref[...] + arrived_ref[...].astype(jnp.float32)
    total_ref[...] = total
    sent_ref[...] = total.astype(sent_ref.dtype)


def merge(kept, arrived):
    return pl.pallas_call(
        merge_kernel,
        out_shape=[jax.ShapeDtypeStruct(kept.shape, kept.dtype), jax.ShapeDtypeStruct(kept.shape, arrived.dtype)],
        in_specs=[VMEM] * 2,
        out_specs=[VMEM] * 2,
        **small("merge"),
    )(kept, arrived)


def activate_kernel(kept_ref, arrived_ref, act_ref):
    preact = kept_ref[...] + arrived_ref[...].astype(jnp.float32)
    act_ref[...] = jnp.maximum(preact, 0.0).astype(act_ref.dtype)


def activate(kept, arrived):
    return pl.pallas_call(
        activate_kernel,
        out_shape=jax.ShapeDtypeStruct(kept.shape, arrived.dtype),
        in_specs=[VMEM] * 2,
        out_specs=VMEM,
        **small("activate"),
    )(kept, arrived)


def choose_kernel(*refs):
    sources, out_ref = refs[:-1], refs[-1]
    count = sources[0].shape[0]
    odd = lax.bitwise_and(lax.axis_index("layer"), 1)

    @pl.when(odd == 0)
    def _():
        for number in range(4):
            out_ref[number * count : (number + 1) * count] = sources[number][...]

    @pl.when(odd == 1)
    def _():
        out_ref[:count] = sources[4][...]
        out_ref[count : 3 * count] = sources[5][...]
        out_ref[3 * count :] = sources[6][...]


def choose(own, far):
    shape = own[0].shape
    return pl.pallas_call(
        choose_kernel,
        out_shape=jax.ShapeDtypeStruct((4 * shape[0],) + shape[1:], own[0].dtype),
        in_specs=[VMEM] * 7,
        out_specs=VMEM,
        **small("choose"),
    )(*own, *far)


def join_kernel(first_ref, second_ref, out_ref):
    count = first_ref.shape[0]
    out_ref[:count] = first_ref[...]
    out_ref[count:] = second_ref[...]


def join(first, second):
    return pl.pallas_call(
        join_kernel,
        out_shape=jax.ShapeDtypeStruct((2 * first.shape[0],) + first.shape[1:], first.dtype),
        in_specs=[VMEM] * 2,
        out_specs=VMEM,
        **small("join"),
    )(first, second)


def expand(dense, lists_ref, parts, first, act_refs):
    row = 0
    for act_ref in act_refs:
        count, slots, rows, width = act_ref.shape
        for position in range(count):
            tile = held_tile(first + position, lists_ref.shape[1], parts)
            for slot in range(slots):
                lanes = pl.ds(pl.multiple_of(lists_ref[slot, tile] * width, width), width)
                dense[row : row + rows, lanes] = act_ref[position, slot]
            row += rows
        first += count


def column_tiles(features):
    columns = 256 if features % 256 == 0 else features
    return [slice(first, first + columns) for first in range(0, features, columns)]


def early_kernel(parts, lists_ref, far_lists, *refs):
    own_refs, far_refs, (decoder_hbm, far_dec), refs = refs[:4], refs[4:6], refs[6:8], refs[8:]
    early_ref, late_a, late_b, own, other, own_dec, sem = refs
    copy = pltpu.make_async_copy(decoder_hbm.at[0], own_dec, sem)
    copy.start()
    quarter, latents = late_a.shape[0], own.shape[1]
    own[...] = jnp.zeros_like(own)
    other[...] = jnp.zeros_like(other)
    expand(own, lists_ref, parts, 0, own_refs)
    expand(other, far_lists, parts, 0, far_refs)
    copy.wait()
    for lanes in column_tiles(early_ref.shape[1]):
        total = jnp.dot(own[...], own_dec[:, lanes], preferred_element_type=jnp.float32)
        late_b[:, lanes] = total[3 * quarter :]
        total = total[: 3 * quarter] + jnp.dot(
            other[...], far_dec[:latents, lanes], preferred_element_type=jnp.float32
        )
        early_ref[:, lanes] = total[: 2 * quarter]
        late_a[:, lanes] = total[2 * quarter :]


def decode_early(lists, far_lists, acts, decoder, far_decoder, parts):
    _, latents, features = decoder.shape
    quarter = acts[0].shape[0] * acts[0].shape[2]
    return pl.pallas_call(
        functools.partial(early_kernel, parts),
        out_shape=[jax.ShapeDtypeStruct((count * quarter, features), jnp.float32) for count in (2, 1, 1)],
        in_specs=[SMEM, SMEM] + [VMEM] * 6 + [ANY, VMEM],
        out_specs=[VMEM] * 3,
        scratch_shapes=[
            pltpu.VMEM((4 * quarter, latents), jnp.bfloat16),
            pltpu.VMEM((3 * quarter, latents), jnp.bfloat16),
            pltpu.VMEM((latents, features), jnp.bfloat16),
            pltpu.SemaphoreType.DMA,
        ],
        cost_estimate=pl.CostEstimate(
            flops=14 * quarter * latents * features,
            bytes_accessed=2 * (2 * latents * features + 8 * quarter * features),
            transcendentals=0,
        ),
        **small("decode_early", 16),
    )(lists, far_lists, *acts, decoder, far_decoder)


def middle_kernel(parts, lists_ref, partial_ref, far, far_dec, total_ref, dense):
    latents = dense.shape[1]
    dense[...] = jnp.zeros_like(dense)
    expand(dense, lists_ref, parts, 3 * far.shape[0], [far])
    for lanes in column_tiles(partial_ref.shape[1]):
        total_ref[:, lanes] = partial_ref[:, lanes] + jnp.dot(
            dense[...], far_dec[:latents, lanes], preferred_element_type=jnp.float32
        )


def decode_middle(lists, partial, far, decoder, latents, parts):
    quarter, features = partial.shape
    return pl.pallas_call(
        functools.partial(middle_kernel, parts),
        out_shape=jax.ShapeDtypeStruct(partial.shape, partial.dtype),
        in_specs=[SMEM] + [VMEM] * 3,
        out_specs=VMEM,
        scratch_shapes=[pltpu.VMEM((quarter, latents), jnp.bfloat16)],
        cost_estimate=pl.CostEstimate(
            flops=2 * quarter * latents * features,
            bytes_accessed=2 * (latents * features + 4 * quarter * features),
            transcendentals=0,
        ),
        **small("decode_middle", 16),
    )(lists, partial, far, decoder)


def late_kernel(parts, lists_ref, early_ref, late_a, late_b, near, near_dec, out_ref, dense, stage, sems):
    tokens, latents = dense.shape
    quarter, rows = tokens // 4, tokens // parts
    dense[...] = jnp.zeros_like(dense)
    expand(dense, lists_ref, parts, 0, [near])
    copies = []
    for number, lanes in enumerate(column_tiles(early_ref.shape[1])):
        total = jnp.dot(dense[...], near_dec[:latents, lanes], preferred_element_type=jnp.float32)
        before = ((0, early_ref), (2 * quarter, late_a), (3 * quarter, late_b))
        for first, ref in before:
            last = first + ref.shape[0]
            stage[first:last, lanes] = (total[first:last] + ref[:, lanes]).astype(stage.dtype)
        for held in range(parts):
            tiles = lists_ref.shape[1]
            row = pl.multiple_of(held_tile(held * (tiles // parts), tiles, parts) * (tokens // tiles), rows)
            copies.append(
                pltpu.make_async_copy(
                    stage.at[held * rows : (held + 1) * rows, lanes],
                    out_ref.at[pl.ds(row, rows), lanes],
                    sems.at[number, held],
                )
            )
            copies[-1].start()
    for copy in copies:
        copy.wait()


def decode_late(lists, partials, near, decoder, latents, parts):
    features = decoder.shape[1]
    tokens = near.shape[0] * near.shape[2]
    return pl.pallas_call(
        functools.partial(late_kernel, parts),
        out_shape=jax.ShapeDtypeStruct((tokens, features), jnp.bfloat16),
        in_specs=[SMEM] + [VMEM] * 5,
        out_specs=ANY,
        scratch_shapes=[
            pltpu.VMEM((tokens, latents), jnp.bfloat16),
            pltpu.VMEM((tokens, features), jnp.bfloat16),
            pltpu.SemaphoreType.DMA((len(column_tiles(features)), parts)),
        ],
        cost_estimate=pl.CostEstimate(
            flops=2 * tokens * latents * features,
            bytes_accessed=2 * (latents * features + 3 * tokens * features),
            transcendentals=0,
        ),
        **small("decode_late", 16),
    )(lists, *partials, near, decoder)


def shards(layer_input, enc_weight, enc_bias, dec_weight, block_lists, block_counts):
    parts = lax.axis_size("latent")
    x, encoder, decoder = layer_input[0], enc_weight[0], dec_weight[0]
    lists, counts = block_lists[0].T, block_counts[0]
    slots, tiles = lists.shape
    targets, latents, _ = decoder.shape
    if targets != 3 or parts < 2 or parts & (parts - 1) or tiles % 4:
        raise ValueError("mesh")

    with jax.named_scope("encoder_rows"):
        pieces = fetch_rows(encoder, parts)
        pieces, decoder = lax.optimization_barrier((pieces, decoder))
        weights = [pieces[0]] + [None] * (parts - 1)
        for step in sorted(range(1, parts), reverse=True):
            weights[step] = swapped(pieces[step], step)
    with jax.named_scope("decoder_weights"):
        near_rows, far_rows = fetch_decoders(lists, decoder)
        near_decoder, far_decoder = passed_along(near_rows, 1), passed_along(far_rows, 2)
        near_decoder, far_decoder = lax.optimization_barrier((near_decoder, far_decoder))
        near_lists, far_lists = [
            rows[latents : latents + slots, :tiles].astype(jnp.int32) for rows in (near_decoder, far_decoder)
        ]

    with jax.named_scope("encode"):
        kept_a, kept_b, sent_a, sent_b = encode(lists, counts, enc_bias, x, weights)
        arrived_a, arrived_b = swapped(sent_a, 1), swapped(sent_b, 1)
        step = 2
        while step < parts:
            kept_a, sent_a = merge(kept_a, arrived_a)
            kept_b, sent_b = merge(kept_b, arrived_b)
            arrived_a = swapped(sent_a, step)
            arrived_a, sent_b = lax.optimization_barrier((arrived_a, sent_b))
            arrived_b = swapped(sent_b, step)
            step *= 2
        own_a, own_b = activate(kept_a, arrived_a), activate(kept_b, arrived_b)
    with jax.named_scope("spread"):
        late_a = swapped(own_a, 1)
        far_a = passed_along(own_a, 2)
        late_b = swapped(own_b, 1)
        joined = join(own_b, late_a)
        late_b, far_a = lax.optimization_barrier((late_b, far_a))
        own = [own_a, own_b, late_a, late_b]
        far = [far_a] + [passed_along(piece, 2) for piece in (joined, late_b)]
    with jax.named_scope("decode"):
        early, late_a, late_b = decode_early(lists, far_lists, own + far[:2], decoder, far_decoder, parts)
        early, late_a, late_b, far[2] = lax.optimization_barrier((early, late_a, late_b, far[2]))
        near = across_cores(choose(own, far))
        late_b = decode_middle(far_lists, late_b, far[2], far_decoder, latents, parts)
        return decode_late(near_lists, [early, late_a, late_b], near, near_decoder, latents, parts)[None]


def solution(mesh):
    placed = (
        P("layer", None, "latent"),
        P("layer", None, "latent"),
        P("layer", "latent"),
        P("layer", None, None, "latent"),
        P("layer", None, None),
        P("layer", None),
    )
    return jax.shard_map(
        shards, mesh=mesh, in_specs=placed, out_specs=P("layer", None, "latent"), check_vma=False
    )
```

```python
import functools

import jax
import jax.numpy as jnp
from jax import lax
from jax.experimental import pallas as pl
from jax.experimental.pallas import tpu as pltpu
from jax.sharding import PartitionSpec as P

VMEM = pl.BlockSpec(memory_space=pltpu.VMEM)
SMEM = pl.BlockSpec(memory_space=pltpu.SMEM)
ANY = pl.BlockSpec(memory_space=pl.ANY)
HBM = pl.BlockSpec(memory_space=pltpu.HBM)


def swapped(value, step):
    count = lax.axis_size("latent")
    return lax.ppermute(value, "latent", [(i, i ^ step) for i in range(count)])


def passed_along(value, steps):
    count = lax.axis_size("layer")
    return lax.ppermute(value, "layer", [(i, i + steps) for i in range(count - steps)])


def across_cores(value):
    count = lax.axis_size("layer")
    return lax.ppermute(value, "layer", [(i, i ^ 1) for i in range(count)])


def small(name, megabytes=8):
    return dict(compiler_params=pltpu.CompilerParams(vmem_limit_bytes=megabytes << 20), name=name)


def held_tile(position, tiles, parts):
    each = tiles // parts
    number, half = position // each, parts // 2
    parity = lax.bitwise_and(lax.axis_index("latent"), 1)
    return (2 * (number % half) + (parity if number < half else 1 - parity)) * each + position % each


def fetch_rows_kernel(encoder_ref, *piece_refs):
    depth = piece_refs[0].shape[0]
    for step, piece in enumerate(piece_refs):
        first = pl.multiple_of(lax.bitwise_xor(lax.axis_index("latent"), step) * depth, depth)
        piece[...] = encoder_ref[pl.ds(first, depth), :]


def fetch_rows(encoder, parts):
    depth = encoder.shape[0] // parts
    return pl.pallas_call(
        fetch_rows_kernel,
        out_shape=[jax.ShapeDtypeStruct((depth, encoder.shape[1]), encoder.dtype)] * parts,
        in_specs=[VMEM],
        out_specs=[VMEM] * parts,
        **small("fetch_rows"),
    )(encoder)


def fetch_decoders_kernel(lists_ref, decoder_ref, *refs):
    out_refs, ids = refs[:-1], refs[-1]
    latents = decoder_ref.shape[1]
    slots, tiles = lists_ref.shape
    ids[...] = jnp.zeros_like(ids)
    ids[:slots, :tiles] = lists_ref[...].astype(jnp.float32)
    for number, out_ref in enumerate(out_refs):
        out_ref[:latents, :] = decoder_ref[number + 1]
        out_ref[latents:, :] = ids[...].astype(out_ref.dtype)


def fetch_decoders(lists, decoder):
    targets, latents, features = decoder.shape
    rows = lists.shape[0] + -lists.shape[0] % 16
    shape = jax.ShapeDtypeStruct((latents + rows, features), decoder.dtype)
    return pl.pallas_call(
        fetch_decoders_kernel,
        out_shape=[shape] * (targets - 1),
        in_specs=[VMEM, VMEM],
        out_specs=[VMEM] * (targets - 1),
        scratch_shapes=[pltpu.VMEM((rows, features), jnp.float32)],
        **small("fetch_decoders", 16),
    )(lists, decoder)


def encode_kernel(parts, lists_ref, counts_ref, bias_ref, x_ref, *refs):
    weight_refs, out_refs, partial = refs[:parts], refs[parts:-1], refs[-1]
    width = bias_ref.shape[1]
    count, slots, rows, _ = out_refs[0].shape
    tiles = lists_ref.shape[1]
    for first in range(0, parts, 2):
        stacked = jnp.concatenate([ref[...] for ref in weight_refs[first : first + 2]], axis=1)
        product = jnp.dot(x_ref[...], stacked, preferred_element_type=jnp.float32)
        for source in range(first, first + 2):
            block = product[:, (source - first) * width : (source - first + 1) * width]
            partial[source] = block if source else block + bias_ref[...]
    for number, out_ref in enumerate(out_refs):
        for position in range(count):
            tile = held_tile(number * count + position, tiles, parts)
            row = pl.multiple_of(tile * rows, rows)
            for slot in range(slots):
                source = lax.bitwise_xor(lax.axis_index("latent"), lists_ref[slot, tile])
                kept = partial[source, pl.ds(row, rows), :]
                if number < 2:
                    kept = kept + jnp.where(slot < counts_ref[tile], 0.0, -1e30)
                out_ref[position, slot] = kept.astype(out_ref.dtype)


def encode(lists, counts, bias, x, weights):
    parts = len(weights)
    tokens, depth = x.shape
    width = bias.shape[1]
    slots, tiles = lists.shape
    shape = (tiles // 4, slots, tokens // tiles, width)
    return pl.pallas_call(
        functools.partial(encode_kernel, parts),
        out_shape=[jax.ShapeDtypeStruct(shape, jnp.float32)] * 2 + [jax.ShapeDtypeStruct(shape, jnp.bfloat16)] * 2,
        in_specs=[SMEM] * 2 + [VMEM] * (2 + parts),
        out_specs=[VMEM] * 4,
        scratch_shapes=[pltpu.VMEM((parts, tokens, width), jnp.float32)],
        cost_estimate=pl.CostEstimate(
            flops=32 * tokens * depth * parts * width,
            bytes_accessed=2 * (tokens * depth + depth * parts * width),
            transcendentals=0,
        ),
        **small("encode", 16),
    )(lists, counts, bias, x, *weights)


def merge_kernel(kept_ref, arrived_ref, total_ref, sent_ref):
    total = kept_ref[...] + arrived_ref[...].astype(jnp.float32)
    total_ref[...] = total
    sent_ref[...] = total.astype(sent_ref.dtype)


def merge(kept, arrived):
    return pl.pallas_call(
        merge_kernel,
        out_shape=[jax.ShapeDtypeStruct(kept.shape, kept.dtype), jax.ShapeDtypeStruct(kept.shape, arrived.dtype)],
        in_specs=[VMEM] * 2,
        out_specs=[VMEM] * 2,
        **small("merge"),
    )(kept, arrived)


def activate_kernel(kept_ref, arrived_ref, act_ref):
    preact = kept_ref[...] + arrived_ref[...].astype(jnp.float32)
    act_ref[...] = jnp.maximum(preact, 0.0).astype(act_ref.dtype)


def activate(kept, arrived):
    return pl.pallas_call(
        activate_kernel,
        out_shape=jax.ShapeDtypeStruct(kept.shape, arrived.dtype),
        in_specs=[VMEM] * 2,
        out_specs=VMEM,
        **small("activate"),
    )(kept, arrived)


def choose_kernel(*refs):
    sources, out_ref = refs[:-1], refs[-1]
    count = sources[0].shape[0]
    odd = lax.bitwise_and(lax.axis_index("layer"), 1)

    @pl.when(odd == 0)
    def _():
        for number in range(4):
            out_ref[number * count : (number + 1) * count] = sources[number][...]

    @pl.when(odd == 1)
    def _():
        out_ref[:count] = sources[4][...]
        out_ref[count : 3 * count] = sources[5][...]
        out_ref[3 * count :] = sources[6][...]


def choose(own, far):
    shape = own[0].shape
    return pl.pallas_call(
        choose_kernel,
        out_shape=jax.ShapeDtypeStruct((4 * shape[0],) + shape[1:], own[0].dtype),
        in_specs=[VMEM] * 7,
        out_specs=VMEM,
        **small("choose"),
    )(*own, *far)


def join_kernel(first_ref, second_ref, out_ref):
    count = first_ref.shape[0]
    out_ref[:count] = first_ref[...]
    out_ref[count:] = second_ref[...]


def join(first, second):
    return pl.pallas_call(
        join_kernel,
        out_shape=jax.ShapeDtypeStruct((2 * first.shape[0],) + first.shape[1:], first.dtype),
        in_specs=[VMEM] * 2,
        out_specs=VMEM,
        **small("join"),
    )(first, second)


def expand(dense, lists_ref, parts, first, act_refs):
    row = 0
    for act_ref in act_refs:
        count, slots, rows, width = act_ref.shape
        for position in range(count):
            tile = held_tile(first + position, lists_ref.shape[1], parts)
            for slot in range(slots):
                lanes = pl.ds(pl.multiple_of(lists_ref[slot, tile] * width, width), width)
                dense[row : row + rows, lanes] = act_ref[position, slot]
            row += rows
        first += count


def column_tiles(features):
    columns = 256 if features % 256 == 0 else features
    return [slice(first, first + columns) for first in range(0, features, columns)]


def early_kernel(parts, lists_ref, far_lists, *refs):
    own_refs, far_ref, (decoder_hbm, far_dec), refs = refs[:4], refs[4], refs[5:7], refs[7:]
    first_ref, rest_ref, own, other, own_dec, sem = refs
    copy = pltpu.make_async_copy(decoder_hbm.at[0], own_dec, sem)
    copy.start()
    quarter, latents = other.shape
    own[...] = jnp.zeros_like(own)
    other[...] = jnp.zeros_like(other)
    expand(own, lists_ref, parts, 0, own_refs)
    expand(other, far_lists, parts, 0, [far_ref])
    copy.wait()
    for lanes in column_tiles(first_ref.shape[1]):
        total = jnp.dot(own[...], own_dec[:, lanes], preferred_element_type=jnp.float32)
        rest_ref[:, lanes] = total[quarter:]
        first_ref[:, lanes] = total[:quarter] + jnp.dot(
            other[...], far_dec[:latents, lanes], preferred_element_type=jnp.float32
        )


def decode_early(lists, far_lists, acts, decoder, far_decoder, parts):
    _, latents, features = decoder.shape
    quarter = acts[0].shape[0] * acts[0].shape[2]
    return pl.pallas_call(
        functools.partial(early_kernel, parts),
        out_shape=[jax.ShapeDtypeStruct((count * quarter, features), jnp.float32) for count in (1, 3)],
        in_specs=[SMEM, SMEM] + [VMEM] * 5 + [ANY, VMEM],
        out_specs=[VMEM] * 2,
        scratch_shapes=[
            pltpu.VMEM((4 * quarter, latents), jnp.bfloat16),
            pltpu.VMEM((quarter, latents), jnp.bfloat16),
            pltpu.VMEM((latents, features), jnp.bfloat16),
            pltpu.SemaphoreType.DMA,
        ],
        cost_estimate=pl.CostEstimate(
            flops=10 * quarter * latents * features,
            bytes_accessed=2 * (2 * latents * features + 8 * quarter * features),
            transcendentals=0,
        ),
        **small("decode_early", 16),
    )(lists, far_lists, *acts, decoder, far_decoder)


def middle_kernel(parts, lists_ref, rest_ref, second, third, far_dec, total_ref, dense):
    latents = dense.shape[1]
    dense[...] = jnp.zeros_like(dense)
    expand(dense, lists_ref, parts, third.shape[0], [second, third])
    for lanes in column_tiles(rest_ref.shape[1]):
        total_ref[:, lanes] = rest_ref[:, lanes] + jnp.dot(
            dense[...], far_dec[:latents, lanes], preferred_element_type=jnp.float32
        )


def decode_middle(lists, rest, far, decoder, latents, parts):
    rows, features = rest.shape
    return pl.pallas_call(
        functools.partial(middle_kernel, parts),
        out_shape=jax.ShapeDtypeStruct(rest.shape, rest.dtype),
        in_specs=[SMEM] + [VMEM] * 4,
        out_specs=VMEM,
        scratch_shapes=[pltpu.VMEM((rows, latents), jnp.bfloat16)],
        cost_estimate=pl.CostEstimate(
            flops=2 * rows * latents * features,
            bytes_accessed=2 * (latents * features + 4 * rows * features),
            transcendentals=0,
        ),
        **small("decode_middle", 16),
    )(lists, rest, *far, decoder)


def late_kernel(parts, lists_ref, first_ref, rest_ref, near, near_dec, out_ref, dense, stage, sems):
    tokens, latents = dense.shape
    quarter, rows = tokens // 4, tokens // parts
    dense[...] = jnp.zeros_like(dense)
    expand(dense, lists_ref, parts, 0, [near])
    copies = []
    for number, lanes in enumerate(column_tiles(first_ref.shape[1])):
        total = jnp.dot(dense[...], near_dec[:latents, lanes], preferred_element_type=jnp.float32)
        stage[:quarter, lanes] = (total[:quarter] + first_ref[:, lanes]).astype(stage.dtype)
        stage[quarter:, lanes] = (total[quarter:] + rest_ref[:, lanes]).astype(stage.dtype)
        for held in range(parts):
            tiles = lists_ref.shape[1]
            row = pl.multiple_of(held_tile(held * (tiles // parts), tiles, parts) * (tokens // tiles), rows)
            copies.append(
                pltpu.make_async_copy(
                    stage.at[held * rows : (held + 1) * rows, lanes],
                    out_ref.at[pl.ds(row, rows), lanes],
                    sems.at[number, held],
                )
            )
            copies[-1].start()
    for copy in copies:
        copy.wait()


def decode_late(lists, partials, near, decoder, latents, parts):
    features = decoder.shape[1]
    tokens = near.shape[0] * near.shape[2]
    return pl.pallas_call(
        functools.partial(late_kernel, parts),
        out_shape=jax.ShapeDtypeStruct((tokens, features), jnp.bfloat16),
        in_specs=[SMEM] + [VMEM] * 4,
        out_specs=ANY,
        scratch_shapes=[
            pltpu.VMEM((tokens, latents), jnp.bfloat16),
            pltpu.VMEM((tokens, features), jnp.bfloat16),
            pltpu.SemaphoreType.DMA((len(column_tiles(features)), parts)),
        ],
        cost_estimate=pl.CostEstimate(
            flops=2 * tokens * latents * features,
            bytes_accessed=2 * (latents * features + 3 * tokens * features),
            transcendentals=0,
        ),
        **small("decode_late", 16),
    )(lists, *partials, near, decoder)


def shards(layer_input, enc_weight, enc_bias, dec_weight, block_lists, block_counts):
    parts = lax.axis_size("latent")
    x, encoder, decoder = layer_input[0], enc_weight[0], dec_weight[0]
    lists, counts = block_lists[0].T, block_counts[0]
    slots, tiles = lists.shape
    targets, latents, _ = decoder.shape
    if targets != 3 or parts < 2 or parts & (parts - 1) or tiles % 4:
        raise ValueError("mesh")

    with jax.named_scope("encoder_rows"):
        pieces = fetch_rows(encoder, parts)
        pieces, decoder = lax.optimization_barrier((pieces, decoder))
        weights = [pieces[0]] + [None] * (parts - 1)
        for step in sorted(range(1, parts), reverse=True):
            weights[step] = swapped(pieces[step], step)
    with jax.named_scope("decoder_weights"):
        near_rows, far_rows = fetch_decoders(lists, decoder)
        near_decoder, far_decoder = passed_along(near_rows, 1), passed_along(far_rows, 2)
        near_decoder, far_decoder = lax.optimization_barrier((near_decoder, far_decoder))
        near_lists, far_lists = [
            rows[latents : latents + slots, :tiles].astype(jnp.int32) for rows in (near_decoder, far_decoder)
        ]

    with jax.named_scope("encode"):
        kept_a, kept_b, sent_a, sent_b = encode(lists, counts, enc_bias, x, weights)
        arrived_a, arrived_b = swapped(sent_a, 1), swapped(sent_b, 1)
        step = 2
        while step < parts:
            kept_a, sent_a = merge(kept_a, arrived_a)
            kept_b, sent_b = merge(kept_b, arrived_b)
            arrived_a = swapped(sent_a, step)
            arrived_a, sent_b = lax.optimization_barrier((arrived_a, sent_b))
            arrived_b = swapped(sent_b, step)
            step *= 2
        own_a, own_b = activate(kept_a, arrived_a), activate(kept_b, arrived_b)
    with jax.named_scope("spread"):
        late_a = swapped(own_a, 1)
        far_a = passed_along(own_a, 2)
        late_b = swapped(own_b, 1)
        joined = join(own_b, late_a)
        late_b, far_a = lax.optimization_barrier((late_b, far_a))
        own = [own_a, own_b, late_a, late_b]
        far = [far_a] + [passed_along(piece, 2) for piece in (joined, late_b)]
    with jax.named_scope("decode"):
        first, rest = decode_early(lists, far_lists, own + far[:1], decoder, far_decoder, parts)
        first, rest, far[2] = lax.optimization_barrier((first, rest, far[2]))
        near = across_cores(choose(own, far))
        rest = decode_middle(far_lists, rest, far[1:], far_decoder, latents, parts)
        return decode_late(near_lists, [first, rest], near, near_decoder, latents, parts)[None]


def solution(mesh):
    placed = (
        P("layer", None, "latent"),
        P("layer", None, "latent"),
        P("layer", "latent"),
        P("layer", None, None, "latent"),
        P("layer", None, None),
        P("layer", None),
    )
    return jax.shard_map(
        shards, mesh=mesh, in_specs=placed, out_specs=P("layer", None, "latent"), check_vma=False
    )
```

```python
import functools

import jax
import jax.numpy as jnp
from jax import lax
from jax.experimental import pallas as pl
from jax.experimental.pallas import tpu as pltpu
from jax.sharding import PartitionSpec as P

VMEM = pl.BlockSpec(memory_space=pltpu.VMEM)
SMEM = pl.BlockSpec(memory_space=pltpu.SMEM)
ANY = pl.BlockSpec(memory_space=pl.ANY)
HBM = pl.BlockSpec(memory_space=pltpu.HBM)


def swapped(value, step):
    count = lax.axis_size("latent")
    return lax.ppermute(value, "latent", [(i, i ^ step) for i in range(count)])


def interleaved(parts):
    across = list(range(parts - 1, parts // 2 - 1, -1))
    within = list(range(parts // 2 - 1, 0, -1))
    return [step for pair in zip(across, within + [None]) for step in pair if step]


def passed_along(value, steps):
    count = lax.axis_size("layer")
    return lax.ppermute(value, "layer", [(i, i + steps) for i in range(count - steps)])


def across_cores(value):
    count = lax.axis_size("layer")
    return lax.ppermute(value, "layer", [(i, i ^ 1) for i in range(count)])


def small(name, megabytes=8):
    return dict(compiler_params=pltpu.CompilerParams(vmem_limit_bytes=megabytes << 20), name=name)


def held_tile(position, tiles, parts):
    each = tiles // parts
    number, half = position // each, parts // 2
    parity = lax.bitwise_and(lax.axis_index("latent"), 1)
    return (2 * (number % half) + (parity if number < half else 1 - parity)) * each + position % each


def fetch_rows_kernel(encoder_ref, *piece_refs):
    depth = piece_refs[0].shape[0]
    for step, piece in enumerate(piece_refs):
        first = pl.multiple_of(lax.bitwise_xor(lax.axis_index("latent"), step) * depth, depth)
        piece[...] = encoder_ref[pl.ds(first, depth), :]


def fetch_rows(encoder, parts):
    depth = encoder.shape[0] // parts
    return pl.pallas_call(
        fetch_rows_kernel,
        out_shape=[jax.ShapeDtypeStruct((depth, encoder.shape[1]), encoder.dtype)] * parts,
        in_specs=[VMEM],
        out_specs=[VMEM] * parts,
        **small("fetch_rows"),
    )(encoder)


def fetch_decoders_kernel(lists_ref, decoder_ref, *refs):
    out_refs, ids = refs[:-1], refs[-1]
    latents = decoder_ref.shape[1]
    slots, tiles = lists_ref.shape
    ids[...] = jnp.zeros_like(ids)
    ids[:slots, :tiles] = lists_ref[...].astype(jnp.float32)
    for number, out_ref in enumerate(out_refs):
        out_ref[:latents, :] = decoder_ref[number + 1]
        out_ref[latents:, :] = ids[...].astype(out_ref.dtype)


def fetch_decoders(lists, decoder):
    targets, latents, features = decoder.shape
    rows = lists.shape[0] + -lists.shape[0] % 16
    shape = jax.ShapeDtypeStruct((latents + rows, features), decoder.dtype)
    return pl.pallas_call(
        fetch_decoders_kernel,
        out_shape=[shape] * (targets - 1),
        in_specs=[VMEM, VMEM],
        out_specs=[VMEM] * (targets - 1),
        scratch_shapes=[pltpu.VMEM((rows, features), jnp.float32)],
        **small("fetch_decoders", 16),
    )(lists, decoder)


def encode_kernel(parts, lists_ref, counts_ref, bias_ref, x_ref, *refs):
    weight_refs, out_refs, partial = refs[:parts], refs[parts:-1], refs[-1]
    width = bias_ref.shape[1]
    count, slots, rows, _ = out_refs[0].shape
    tiles = lists_ref.shape[1]
    sources = [0] + interleaved(parts)
    for first in range(0, parts, 2):
        stacked = jnp.concatenate([ref[...] for ref in weight_refs[first : first + 2]], axis=1)
        product = jnp.dot(x_ref[...], stacked, preferred_element_type=jnp.float32)
        for number in range(2):
            block = product[:, number * width : (number + 1) * width]
            partial[sources[first + number]] = block if first + number else block + bias_ref[...]
    for number, out_ref in enumerate(out_refs):
        for position in range(count):
            tile = held_tile(number * count + position, tiles, parts)
            row = pl.multiple_of(tile * rows, rows)
            for slot in range(slots):
                source = lax.bitwise_xor(lax.axis_index("latent"), lists_ref[slot, tile])
                kept = partial[source, pl.ds(row, rows), :]
                if number < 2:
                    kept = kept + jnp.where(slot < counts_ref[tile], 0.0, -1e30)
                out_ref[position, slot] = kept.astype(out_ref.dtype)


def encode(lists, counts, bias, x, weights):
    parts = len(weights)
    tokens, depth = x.shape
    width = bias.shape[1]
    slots, tiles = lists.shape
    shape = (tiles // 4, slots, tokens // tiles, width)
    return pl.pallas_call(
        functools.partial(encode_kernel, parts),
        out_shape=[jax.ShapeDtypeStruct(shape, jnp.float32)] * 2 + [jax.ShapeDtypeStruct(shape, jnp.bfloat16)] * 2,
        in_specs=[SMEM] * 2 + [VMEM] * (2 + parts),
        out_specs=[VMEM] * 4,
        scratch_shapes=[pltpu.VMEM((parts, tokens, width), jnp.float32)],
        cost_estimate=pl.CostEstimate(
            flops=32 * tokens * depth * parts * width,
            bytes_accessed=2 * (tokens * depth + depth * parts * width),
            transcendentals=0,
        ),
        **small("encode", 16),
    )(lists, counts, bias, x, *weights)


def merge_kernel(kept_ref, arrived_ref, total_ref, sent_ref):
    total = kept_ref[...] + arrived_ref[...].astype(jnp.float32)
    total_ref[...] = total
    sent_ref[...] = total.astype(sent_ref.dtype)


def merge(kept, arrived):
    return pl.pallas_call(
        merge_kernel,
        out_shape=[jax.ShapeDtypeStruct(kept.shape, kept.dtype), jax.ShapeDtypeStruct(kept.shape, arrived.dtype)],
        in_specs=[VMEM] * 2,
        out_specs=[VMEM] * 2,
        **small("merge"),
    )(kept, arrived)


def activate_kernel(kept_ref, arrived_ref, act_ref):
    preact = kept_ref[...] + arrived_ref[...].astype(jnp.float32)
    act_ref[...] = jnp.maximum(preact, 0.0).astype(act_ref.dtype)


def activate(kept, arrived):
    return pl.pallas_call(
        activate_kernel,
        out_shape=jax.ShapeDtypeStruct(kept.shape, arrived.dtype),
        in_specs=[VMEM] * 2,
        out_specs=VMEM,
        **small("activate"),
    )(kept, arrived)


def choose_kernel(*refs):
    sources, out_ref = refs[:-1], refs[-1]
    count = sources[0].shape[0]
    odd = lax.bitwise_and(lax.axis_index("layer"), 1)

    @pl.when(odd == 0)
    def _():
        for number in range(4):
            out_ref[number * count : (number + 1) * count] = sources[number][...]

    @pl.when(odd == 1)
    def _():
        out_ref[:count] = sources[4][...]
        out_ref[count : 3 * count] = sources[5][...]
        out_ref[3 * count :] = sources[6][...]


def choose(own, far):
    shape = own[0].shape
    return pl.pallas_call(
        choose_kernel,
        out_shape=jax.ShapeDtypeStruct((4 * shape[0],) + shape[1:], own[0].dtype),
        in_specs=[VMEM] * 7,
        out_specs=VMEM,
        **small("choose"),
    )(*own, *far)


def join_kernel(first_ref, second_ref, out_ref):
    count = first_ref.shape[0]
    out_ref[:count] = first_ref[...]
    out_ref[count:] = second_ref[...]


def join(first, second):
    return pl.pallas_call(
        join_kernel,
        out_shape=jax.ShapeDtypeStruct((2 * first.shape[0],) + first.shape[1:], first.dtype),
        in_specs=[VMEM] * 2,
        out_specs=VMEM,
        **small("join"),
    )(first, second)


def expand(dense, lists_ref, parts, first, act_refs):
    row = 0
    for act_ref in act_refs:
        count, slots, rows, width = act_ref.shape
        for position in range(count):
            tile = held_tile(first + position, lists_ref.shape[1], parts)
            for slot in range(slots):
                lanes = pl.ds(pl.multiple_of(lists_ref[slot, tile] * width, width), width)
                dense[row : row + rows, lanes] = act_ref[position, slot]
            row += rows
        first += count


def column_tiles(features):
    columns = 256 if features % 256 == 0 else features
    return [slice(first, first + columns) for first in range(0, features, columns)]


def early_kernel(parts, lists_ref, far_lists, *refs):
    own_refs, far_ref, (decoder_hbm, far_dec), refs = refs[:4], refs[4], refs[5:7], refs[7:]
    first_ref, rest_ref, own, other, own_dec, sem = refs
    copy = pltpu.make_async_copy(decoder_hbm.at[0], own_dec, sem)
    copy.start()
    quarter, latents = other.shape
    own[...] = jnp.zeros_like(own)
    other[...] = jnp.zeros_like(other)
    expand(own, lists_ref, parts, 0, own_refs)
    expand(other, far_lists, parts, 0, [far_ref])
    copy.wait()
    for lanes in column_tiles(first_ref.shape[1]):
        total = jnp.dot(own[...], own_dec[:, lanes], preferred_element_type=jnp.float32)
        rest_ref[:, lanes] = total[quarter:]
        first_ref[:, lanes] = total[:quarter] + jnp.dot(
            other[...], far_dec[:latents, lanes], preferred_element_type=jnp.float32
        )


def decode_early(lists, far_lists, acts, decoder, far_decoder, parts):
    _, latents, features = decoder.shape
    quarter = acts[0].shape[0] * acts[0].shape[2]
    return pl.pallas_call(
        functools.partial(early_kernel, parts),
        out_shape=[jax.ShapeDtypeStruct((count * quarter, features), jnp.float32) for count in (1, 3)],
        in_specs=[SMEM, SMEM] + [VMEM] * 5 + [ANY, VMEM],
        out_specs=[VMEM] * 2,
        scratch_shapes=[
            pltpu.VMEM((4 * quarter, latents), jnp.bfloat16),
            pltpu.VMEM((quarter, latents), jnp.bfloat16),
            pltpu.VMEM((latents, features), jnp.bfloat16),
            pltpu.SemaphoreType.DMA,
        ],
        cost_estimate=pl.CostEstimate(
            flops=10 * quarter * latents * features,
            bytes_accessed=2 * (2 * latents * features + 8 * quarter * features),
            transcendentals=0,
        ),
        **small("decode_early", 16),
    )(lists, far_lists, *acts, decoder, far_decoder)


def middle_kernel(parts, lists_ref, rest_ref, second, third, far_dec, total_ref, dense):
    latents = dense.shape[1]
    dense[...] = jnp.zeros_like(dense)
    expand(dense, lists_ref, parts, third.shape[0], [second, third])
    for lanes in column_tiles(rest_ref.shape[1]):
        total_ref[:, lanes] = rest_ref[:, lanes] + jnp.dot(
            dense[...], far_dec[:latents, lanes], preferred_element_type=jnp.float32
        )


def decode_middle(lists, rest, far, decoder, latents, parts):
    rows, features = rest.shape
    return pl.pallas_call(
        functools.partial(middle_kernel, parts),
        out_shape=jax.ShapeDtypeStruct(rest.shape, rest.dtype),
        in_specs=[SMEM] + [VMEM] * 4,
        out_specs=VMEM,
        scratch_shapes=[pltpu.VMEM((rows, latents), jnp.bfloat16)],
        cost_estimate=pl.CostEstimate(
            flops=2 * rows * latents * features,
            bytes_accessed=2 * (latents * features + 4 * rows * features),
            transcendentals=0,
        ),
        **small("decode_middle", 16),
    )(lists, rest, *far, decoder)


def late_kernel(parts, lists_ref, first_ref, rest_ref, near, near_dec, out_ref, dense, stage, sems):
    tokens, latents = dense.shape
    quarter, rows = tokens // 4, tokens // parts
    dense[...] = jnp.zeros_like(dense)
    expand(dense, lists_ref, parts, 0, [near])
    copies = []
    for number, lanes in enumerate(column_tiles(first_ref.shape[1])):
        total = jnp.dot(dense[...], near_dec[:latents, lanes], preferred_element_type=jnp.float32)
        stage[:quarter, lanes] = (total[:quarter] + first_ref[:, lanes]).astype(stage.dtype)
        stage[quarter:, lanes] = (total[quarter:] + rest_ref[:, lanes]).astype(stage.dtype)
        for held in range(parts):
            tiles = lists_ref.shape[1]
            row = pl.multiple_of(held_tile(held * (tiles // parts), tiles, parts) * (tokens // tiles), rows)
            copies.append(
                pltpu.make_async_copy(
                    stage.at[held * rows : (held + 1) * rows, lanes],
                    out_ref.at[pl.ds(row, rows), lanes],
                    sems.at[number, held],
                )
            )
            copies[-1].start()
    for copy in copies:
        copy.wait()


def decode_late(lists, partials, near, decoder, latents, parts):
    features = decoder.shape[1]
    tokens = near.shape[0] * near.shape[2]
    return pl.pallas_call(
        functools.partial(late_kernel, parts),
        out_shape=jax.ShapeDtypeStruct((tokens, features), jnp.bfloat16),
        in_specs=[SMEM] + [VMEM] * 4,
        out_specs=ANY,
        scratch_shapes=[
            pltpu.VMEM((tokens, latents), jnp.bfloat16),
            pltpu.VMEM((tokens, features), jnp.bfloat16),
            pltpu.SemaphoreType.DMA((len(column_tiles(features)), parts)),
        ],
        cost_estimate=pl.CostEstimate(
            flops=2 * tokens * latents * features,
            bytes_accessed=2 * (latents * features + 3 * tokens * features),
            transcendentals=0,
        ),
        **small("decode_late", 16),
    )(lists, *partials, near, decoder)


def shards(layer_input, enc_weight, enc_bias, dec_weight, block_lists, block_counts):
    parts = lax.axis_size("latent")
    x, encoder, decoder = layer_input[0], enc_weight[0], dec_weight[0]
    lists, counts = block_lists[0].T, block_counts[0]
    slots, tiles = lists.shape
    targets, latents, _ = decoder.shape
    if targets != 3 or parts < 2 or parts & (parts - 1) or tiles % 4:
        raise ValueError("mesh")

    with jax.named_scope("encoder_rows"):
        pieces = fetch_rows(encoder, parts)
        pieces, decoder = lax.optimization_barrier((pieces, decoder))
        weights = [pieces[0]] + [swapped(pieces[step], step) for step in interleaved(parts)]
    with jax.named_scope("decoder_weights"):
        near_rows, far_rows = fetch_decoders(lists, decoder)
        near_decoder, far_decoder = passed_along(near_rows, 1), passed_along(far_rows, 2)
        near_decoder, far_decoder = lax.optimization_barrier((near_decoder, far_decoder))
        near_lists, far_lists = [
            rows[latents : latents + slots, :tiles].astype(jnp.int32) for rows in (near_decoder, far_decoder)
        ]

    with jax.named_scope("encode"):
        kept_a, kept_b, sent_a, sent_b = encode(lists, counts, enc_bias, x, weights)
        arrived_a, arrived_b = swapped(sent_a, 1), swapped(sent_b, 1)
        step = 2
        while step < parts:
            kept_a, sent_a = merge(kept_a, arrived_a)
            kept_b, sent_b = merge(kept_b, arrived_b)
            arrived_a = swapped(sent_a, step)
            arrived_a, sent_b = lax.optimization_barrier((arrived_a, sent_b))
            arrived_b = swapped(sent_b, step)
            step *= 2
        own_a, own_b = activate(kept_a, arrived_a), activate(kept_b, arrived_b)
    with jax.named_scope("spread"):
        late_a = swapped(own_a, 1)
        far_a = passed_along(own_a, 2)
        late_b = swapped(own_b, 1)
        joined = join(own_b, late_a)
        late_b, far_a = lax.optimization_barrier((late_b, far_a))
        own = [own_a, own_b, late_a, late_b]
        far = [far_a] + [passed_along(piece, 2) for piece in (joined, late_b)]
    with jax.named_scope("decode"):
        first, rest = decode_early(lists, far_lists, own + far[:1], decoder, far_decoder, parts)
        first, rest, far[2] = lax.optimization_barrier((first, rest, far[2]))
        near = across_cores(choose(own, far))
        rest = decode_middle(far_lists, rest, far[1:], far_decoder, latents, parts)
        return decode_late(near_lists, [first, rest], near, near_decoder, latents, parts)[None]


def solution(mesh):
    placed = (
        P("layer", None, "latent"),
        P("layer", None, "latent"),
        P("layer", "latent"),
        P("layer", None, None, "latent"),
        P("layer", None, None),
        P("layer", None),
    )
    return jax.shard_map(
        shards, mesh=mesh, in_specs=placed, out_specs=P("layer", None, "latent"), check_vma=False
    )
```

```python
import functools

import jax
import jax.numpy as jnp
from jax import lax
from jax.experimental import pallas as pl
from jax.experimental.pallas import tpu as pltpu
from jax.sharding import PartitionSpec as P

VMEM = pl.BlockSpec(memory_space=pltpu.VMEM)
SMEM = pl.BlockSpec(memory_space=pltpu.SMEM)
ANY = pl.BlockSpec(memory_space=pl.ANY)
HBM = pl.BlockSpec(memory_space=pltpu.HBM)


def swapped(value, step):
    count = lax.axis_size("latent")
    return lax.ppermute(value, "latent", [(i, i ^ step) for i in range(count)])


def passed_along(value, steps):
    count = lax.axis_size("layer")
    return lax.ppermute(value, "layer", [(i, i + steps) for i in range(count - steps)])


def across_cores(value):
    count = lax.axis_size("layer")
    return lax.ppermute(value, "layer", [(i, i ^ 1) for i in range(count)])


def small(name, megabytes=8):
    return dict(compiler_params=pltpu.CompilerParams(vmem_limit_bytes=megabytes << 20), name=name)


def held_tile(position, tiles, parts):
    each = tiles // parts
    number, half = position // each, parts // 2
    parity = lax.bitwise_and(lax.axis_index("latent"), 1)
    return (2 * (number % half) + (parity if number < half else 1 - parity)) * each + position % each


def fetch_rows_kernel(encoder_ref, *piece_refs):
    depth = piece_refs[0].shape[0]
    for step, piece in enumerate(piece_refs):
        first = pl.multiple_of(lax.bitwise_xor(lax.axis_index("latent"), step) * depth, depth)
        piece[...] = encoder_ref[pl.ds(first, depth), :]


def fetch_rows(encoder, parts):
    depth = encoder.shape[0] // parts
    return pl.pallas_call(
        fetch_rows_kernel,
        out_shape=[jax.ShapeDtypeStruct((depth, encoder.shape[1]), encoder.dtype)] * parts,
        in_specs=[VMEM],
        out_specs=[VMEM] * parts,
        **small("fetch_rows"),
    )(encoder)


def fetch_decoders_kernel(lists_ref, decoder_ref, *refs):
    out_refs, ids = refs[:-1], refs[-1]
    latents = decoder_ref.shape[1]
    slots, tiles = lists_ref.shape
    ids[...] = jnp.zeros_like(ids)
    ids[:slots, :tiles] = lists_ref[...].astype(jnp.float32)
    for number, out_ref in enumerate(out_refs):
        out_ref[:latents, :] = decoder_ref[number + 1]
        out_ref[latents:, :] = ids[...].astype(out_ref.dtype)


def fetch_decoders(lists, decoder):
    targets, latents, features = decoder.shape
    rows = lists.shape[0] + -lists.shape[0] % 16
    shape = jax.ShapeDtypeStruct((latents + rows, features), decoder.dtype)
    return pl.pallas_call(
        fetch_decoders_kernel,
        out_shape=[shape] * (targets - 1),
        in_specs=[VMEM, VMEM],
        out_specs=[VMEM] * (targets - 1),
        scratch_shapes=[pltpu.VMEM((rows, features), jnp.float32)],
        **small("fetch_decoders", 16),
    )(lists, decoder)


def encode_kernel(parts, lists_ref, counts_ref, bias_ref, x_ref, *refs):
    weight_refs, out_refs, partial = refs[:parts], refs[parts:-1], refs[-1]
    width = bias_ref.shape[1]
    count, slots, rows, _ = out_refs[0].shape
    tiles = lists_ref.shape[1]
    for first in range(0, parts, 2):
        stacked = jnp.concatenate([ref[...] for ref in weight_refs[first : first + 2]], axis=1)
        product = jnp.dot(x_ref[...], stacked, preferred_element_type=jnp.float32)
        for source in range(first, first + 2):
            block = product[:, (source - first) * width : (source - first + 1) * width]
            partial[source] = block if source else block + bias_ref[...]
    for number, out_ref in enumerate(out_refs):
        for position in range(count):
            tile = held_tile(number * count + position, tiles, parts)
            row = pl.multiple_of(tile * rows, rows)
            for slot in range(slots):
                source = lax.bitwise_xor(lax.axis_index("latent"), lists_ref[slot, tile])
                kept = partial[source, pl.ds(row, rows), :]
                if number < 2:
                    kept = kept + jnp.where(slot < counts_ref[tile], 0.0, -1e30)
                out_ref[position, slot] = kept.astype(out_ref.dtype)


def encode(lists, counts, bias, x, weights):
    parts = len(weights)
    tokens, depth = x.shape
    width = bias.shape[1]
    slots, tiles = lists.shape
    shape = (tiles // 4, slots, tokens // tiles, width)
    return pl.pallas_call(
        functools.partial(encode_kernel, parts),
        out_shape=[jax.ShapeDtypeStruct(shape, jnp.float32)] * 2 + [jax.ShapeDtypeStruct(shape, jnp.bfloat16)] * 2,
        in_specs=[SMEM] * 2 + [VMEM] * (2 + parts),
        out_specs=[VMEM] * 4,
        scratch_shapes=[pltpu.VMEM((parts, tokens, width), jnp.float32)],
        cost_estimate=pl.CostEstimate(
            flops=32 * tokens * depth * parts * width,
            bytes_accessed=2 * (tokens * depth + depth * parts * width),
            transcendentals=0,
        ),
        **small("encode", 16),
    )(lists, counts, bias, x, *weights)


def merge_kernel(kept_ref, arrived_ref, total_ref, sent_ref):
    total = kept_ref[...] + arrived_ref[...].astype(jnp.float32)
    total_ref[...] = total
    sent_ref[...] = total.astype(sent_ref.dtype)


def merge(kept, arrived):
    return pl.pallas_call(
        merge_kernel,
        out_shape=[jax.ShapeDtypeStruct(kept.shape, kept.dtype), jax.ShapeDtypeStruct(kept.shape, arrived.dtype)],
        in_specs=[VMEM] * 2,
        out_specs=[VMEM] * 2,
        **small("merge"),
    )(kept, arrived)


def activate_kernel(kept_ref, arrived_ref, act_ref):
    preact = kept_ref[...] + arrived_ref[...].astype(jnp.float32)
    act_ref[...] = jnp.maximum(preact, 0.0).astype(act_ref.dtype)


def activate(kept, arrived):
    return pl.pallas_call(
        activate_kernel,
        out_shape=jax.ShapeDtypeStruct(kept.shape, arrived.dtype),
        in_specs=[VMEM] * 2,
        out_specs=VMEM,
        **small("activate"),
    )(kept, arrived)


def choose_kernel(*refs):
    sources, out_ref = refs[:-1], refs[-1]
    count = sources[0].shape[0]
    odd = lax.bitwise_and(lax.axis_index("layer"), 1)
    for parity in range(2):

        @pl.when(odd == parity)
        def _():
            for number in range(4):
                out_ref[number * count : (number + 1) * count] = sources[4 * parity + number][...]


def choose(own, far):
    shape = own[0].shape
    return pl.pallas_call(
        choose_kernel,
        out_shape=jax.ShapeDtypeStruct((4 * shape[0],) + shape[1:], own[0].dtype),
        in_specs=[VMEM] * 8,
        out_specs=VMEM,
        **small("choose"),
    )(*own, *far)


def expand(dense, lists_ref, parts, first, act_refs):
    row = 0
    for act_ref in act_refs:
        count, slots, rows, width = act_ref.shape
        for position in range(count):
            tile = held_tile(first + position, lists_ref.shape[1], parts)
            for slot in range(slots):
                lanes = pl.ds(pl.multiple_of(lists_ref[slot, tile] * width, width), width)
                dense[row : row + rows, lanes] = act_ref[position, slot]
            row += rows
        first += count


def column_tiles(features):
    columns = 256 if features % 256 == 0 else features
    return [slice(first, first + columns) for first in range(0, features, columns)]


def early_kernel(parts, lists_ref, far_lists, *refs):
    own_refs, far_ref, (decoder_hbm, far_dec), refs = refs[:4], refs[4], refs[5:7], refs[7:]
    first_ref, rest_ref, own, other, own_dec, sem = refs
    copy = pltpu.make_async_copy(decoder_hbm.at[0], own_dec, sem)
    copy.start()
    quarter, latents = other.shape
    own[...] = jnp.zeros_like(own)
    other[...] = jnp.zeros_like(other)
    expand(own, lists_ref, parts, 0, own_refs)
    expand(other, far_lists, parts, 0, [far_ref])
    copy.wait()
    for lanes in column_tiles(first_ref.shape[1]):
        total = jnp.dot(own[...], own_dec[:, lanes], preferred_element_type=jnp.float32)
        rest_ref[:, lanes] = total[quarter:]
        first_ref[:, lanes] = total[:quarter] + jnp.dot(
            other[...], far_dec[:latents, lanes], preferred_element_type=jnp.float32
        )


def decode_early(lists, far_lists, acts, decoder, far_decoder, parts):
    _, latents, features = decoder.shape
    quarter = acts[0].shape[0] * acts[0].shape[2]
    return pl.pallas_call(
        functools.partial(early_kernel, parts),
        out_shape=[jax.ShapeDtypeStruct((count * quarter, features), jnp.float32) for count in (1, 3)],
        in_specs=[SMEM, SMEM] + [VMEM] * 5 + [ANY, VMEM],
        out_specs=[VMEM] * 2,
        scratch_shapes=[
            pltpu.VMEM((4 * quarter, latents), jnp.bfloat16),
            pltpu.VMEM((quarter, latents), jnp.bfloat16),
            pltpu.VMEM((latents, features), jnp.bfloat16),
            pltpu.SemaphoreType.DMA,
        ],
        cost_estimate=pl.CostEstimate(
            flops=10 * quarter * latents * features,
            bytes_accessed=2 * (2 * latents * features + 8 * quarter * features),
            transcendentals=0,
        ),
        **small("decode_early", 16),
    )(lists, far_lists, *acts, decoder, far_decoder)


def middle_kernel(parts, lists_ref, rest_ref, *refs):
    far_refs, (far_dec, total_ref, dense) = refs[:3], refs[3:]
    latents = dense.shape[1]
    dense[...] = jnp.zeros_like(dense)
    expand(dense, lists_ref, parts, far_refs[0].shape[0], far_refs)
    for lanes in column_tiles(rest_ref.shape[1]):
        total_ref[:, lanes] = rest_ref[:, lanes] + jnp.dot(
            dense[...], far_dec[:latents, lanes], preferred_element_type=jnp.float32
        )


def decode_middle(lists, rest, far, decoder, latents, parts):
    rows, features = rest.shape
    return pl.pallas_call(
        functools.partial(middle_kernel, parts),
        out_shape=jax.ShapeDtypeStruct(rest.shape, rest.dtype),
        in_specs=[SMEM] + [VMEM] * 5,
        out_specs=VMEM,
        scratch_shapes=[pltpu.VMEM((rows, latents), jnp.bfloat16)],
        cost_estimate=pl.CostEstimate(
            flops=2 * rows * latents * features,
            bytes_accessed=2 * (latents * features + 4 * rows * features),
            transcendentals=0,
        ),
        **small("decode_middle", 16),
    )(lists, rest, *far, decoder)


def late_kernel(parts, lists_ref, first_ref, rest_ref, near, near_dec, out_ref, dense, stage, sems):
    tokens, latents = dense.shape
    quarter, rows = tokens // 4, tokens // parts
    dense[...] = jnp.zeros_like(dense)
    expand(dense, lists_ref, parts, 0, [near])
    copies = []
    for number, lanes in enumerate(column_tiles(first_ref.shape[1])):
        total = jnp.dot(dense[...], near_dec[:latents, lanes], preferred_element_type=jnp.float32)
        stage[:quarter, lanes] = (total[:quarter] + first_ref[:, lanes]).astype(stage.dtype)
        stage[quarter:, lanes] = (total[quarter:] + rest_ref[:, lanes]).astype(stage.dtype)
        for held in range(parts):
            tiles = lists_ref.shape[1]
            row = pl.multiple_of(held_tile(held * (tiles // parts), tiles, parts) * (tokens // tiles), rows)
            copies.append(
                pltpu.make_async_copy(
                    stage.at[held * rows : (held + 1) * rows, lanes],
                    out_ref.at[pl.ds(row, rows), lanes],
                    sems.at[number, held],
                )
            )
            copies[-1].start()
    for copy in copies:
        copy.wait()


def decode_late(lists, partials, near, decoder, latents, parts):
    features = decoder.shape[1]
    tokens = near.shape[0] * near.shape[2]
    return pl.pallas_call(
        functools.partial(late_kernel, parts),
        out_shape=jax.ShapeDtypeStruct((tokens, features), jnp.bfloat16),
        in_specs=[SMEM] + [VMEM] * 4,
        out_specs=ANY,
        scratch_shapes=[
            pltpu.VMEM((tokens, latents), jnp.bfloat16),
            pltpu.VMEM((tokens, features), jnp.bfloat16),
            pltpu.SemaphoreType.DMA((len(column_tiles(features)), parts)),
        ],
        cost_estimate=pl.CostEstimate(
            flops=2 * tokens * latents * features,
            bytes_accessed=2 * (latents * features + 3 * tokens * features),
            transcendentals=0,
        ),
        **small("decode_late", 16),
    )(lists, *partials, near, decoder)


def shards(layer_input, enc_weight, enc_bias, dec_weight, block_lists, block_counts):
    parts = lax.axis_size("latent")
    x, encoder, decoder = layer_input[0], enc_weight[0], dec_weight[0]
    lists, counts = block_lists[0].T, block_counts[0]
    slots, tiles = lists.shape
    targets, latents, _ = decoder.shape
    if targets != 3 or parts < 2 or parts & (parts - 1) or tiles % 4:
        raise ValueError("mesh")

    with jax.named_scope("encoder_rows"):
        pieces = fetch_rows(encoder, parts)
        pieces, decoder = lax.optimization_barrier((pieces, decoder))
        weights = [pieces[0]] + [None] * (parts - 1)
        for step in sorted(range(1, parts), reverse=True):
            weights[step] = swapped(pieces[step], step)
    with jax.named_scope("decoder_weights"):
        near_rows, far_rows = fetch_decoders(lists, decoder)
        near_decoder, far_decoder = passed_along(near_rows, 1), passed_along(far_rows, 2)
        near_decoder, far_decoder = lax.optimization_barrier((near_decoder, far_decoder))
        near_lists, far_lists = [
            rows[latents : latents + slots, :tiles].astype(jnp.int32) for rows in (near_decoder, far_decoder)
        ]

    with jax.named_scope("encode"):
        kept_a, kept_b, sent_a, sent_b = encode(lists, counts, enc_bias, x, weights)
        arrived_a, arrived_b = swapped(sent_a, 1), swapped(sent_b, 1)
        step = 2
        while step < parts:
            kept_a, sent_a = merge(kept_a, arrived_a)
            kept_b, sent_b = merge(kept_b, arrived_b)
            arrived_a = swapped(sent_a, step)
            arrived_a, sent_b = lax.optimization_barrier((arrived_a, sent_b))
            arrived_b = swapped(sent_b, step)
            step *= 2
        own_a, own_b = activate(kept_a, arrived_a), activate(kept_b, arrived_b)
    with jax.named_scope("spread"):
        late_a = swapped(own_a, 1)
        late_a, own_b = lax.optimization_barrier((late_a, own_b))
        far_a = passed_along(own_a, 2)
        late_b, far_b = swapped(own_b, 1), passed_along(own_b, 2)
        late_b, far_b = lax.optimization_barrier((late_b, far_b))
        late_far_a, late_far_b = swapped(far_a, 1), swapped(far_b, 1)
        own = [own_a, own_b, late_a, late_b]
    with jax.named_scope("decode"):
        first, rest = decode_early(lists, far_lists, own + [far_a], decoder, far_decoder, parts)
        first, rest, late_far_b = lax.optimization_barrier((first, rest, late_far_b))
        far = [far_a, far_b, late_far_a, late_far_b]
        near = across_cores(choose(own, far))
        rest = decode_middle(far_lists, rest, far[1:], far_decoder, latents, parts)
        return decode_late(near_lists, [first, rest], near, near_decoder, latents, parts)[None]


def solution(mesh):
    placed = (
        P("layer", None, "latent"),
        P("layer", None, "latent"),
        P("layer", "latent"),
        P("layer", None, None, "latent"),
        P("layer", None, None),
        P("layer", None),
    )
    return jax.shard_map(
        shards, mesh=mesh, in_specs=placed, out_specs=P("layer", None, "latent"), check_vma=False
    )
```

```python
import functools

import jax
import jax.numpy as jnp
from jax import lax
from jax.experimental import pallas as pl
from jax.experimental.pallas import tpu as pltpu
from jax.sharding import PartitionSpec as P

VMEM = pl.BlockSpec(memory_space=pltpu.VMEM)
SMEM = pl.BlockSpec(memory_space=pltpu.SMEM)
ANY = pl.BlockSpec(memory_space=pl.ANY)
HBM = pl.BlockSpec(memory_space=pltpu.HBM)


def swapped(value, step):
    count = lax.axis_size("latent")
    return lax.ppermute(value, "latent", [(i, i ^ step) for i in range(count)])


def passed_along(value, steps):
    count = lax.axis_size("layer")
    return lax.ppermute(value, "layer", [(i, i + steps) for i in range(count - steps)])


def across_cores(value):
    count = lax.axis_size("layer")
    return lax.ppermute(value, "layer", [(i, i ^ 1) for i in range(count)])


def small(name, megabytes=8):
    return dict(compiler_params=pltpu.CompilerParams(vmem_limit_bytes=megabytes << 20), name=name)


def held_tile(position, tiles, parts):
    each = tiles // parts
    number, half = position // each, parts // 2
    parity = lax.bitwise_and(lax.axis_index("latent"), 1)
    return (2 * (number % half) + (parity if number < half else 1 - parity)) * each + position % each


def fetch_rows_kernel(encoder_ref, *piece_refs):
    depth = piece_refs[0].shape[0]
    for step, piece in enumerate(piece_refs):
        first = pl.multiple_of(lax.bitwise_xor(lax.axis_index("latent"), step) * depth, depth)
        piece[...] = encoder_ref[pl.ds(first, depth), :]


def fetch_rows(encoder, parts):
    depth = encoder.shape[0] // parts
    return pl.pallas_call(
        fetch_rows_kernel,
        out_shape=[jax.ShapeDtypeStruct((depth, encoder.shape[1]), encoder.dtype)] * parts,
        in_specs=[VMEM],
        out_specs=[VMEM] * parts,
        **small("fetch_rows"),
    )(encoder)


def fetch_decoders_kernel(lists_ref, decoder_ref, *refs):
    out_refs, ids = refs[:-1], refs[-1]
    latents = decoder_ref.shape[1]
    slots, tiles = lists_ref.shape
    ids[...] = jnp.zeros_like(ids)
    ids[:slots, :tiles] = lists_ref[...].astype(jnp.float32)
    for number, out_ref in enumerate(out_refs):
        out_ref[:latents, :] = decoder_ref[number + 1]
        out_ref[latents:, :] = ids[...].astype(out_ref.dtype)


def fetch_decoders(lists, decoder):
    targets, latents, features = decoder.shape
    rows = lists.shape[0] + -lists.shape[0] % 16
    shape = jax.ShapeDtypeStruct((latents + rows, features), decoder.dtype)
    return pl.pallas_call(
        fetch_decoders_kernel,
        out_shape=[shape] * (targets - 1),
        in_specs=[VMEM, VMEM],
        out_specs=[VMEM] * (targets - 1),
        scratch_shapes=[pltpu.VMEM((rows, features), jnp.float32)],
        **small("fetch_decoders", 16),
    )(lists, decoder)


def encode_kernel(parts, starts, lists_ref, counts_ref, bias_ref, x_ref, *refs):
    weight_refs, out_refs, partial = refs[:parts], refs[parts:-1], refs[-1]
    width = bias_ref.shape[1]
    count, slots, rows, _ = out_refs[0].shape
    tiles = lists_ref.shape[1]
    held = [[held_tile(start + position, tiles, parts) for position in range(count)] for start in starts]
    taken = [x_ref[pl.ds(pl.multiple_of(tile * rows, rows), rows), :] for group in held for tile in group]
    taken = jnp.concatenate(taken, axis=0)
    for first in range(0, parts, 2):
        stacked = jnp.concatenate([ref[...] for ref in weight_refs[first : first + 2]], axis=1)
        product = jnp.dot(taken, stacked, preferred_element_type=jnp.float32)
        for source in range(first, first + 2):
            block = product[:, (source - first) * width : (source - first + 1) * width]
            partial[source] = block if source else block + bias_ref[...]
    row = 0
    for start, group, out_ref in zip(starts, held, out_refs):
        for position, tile in enumerate(group):
            for slot in range(slots):
                source = lax.bitwise_xor(lax.axis_index("latent"), lists_ref[slot, tile])
                kept = partial[source, row : row + rows, :]
                if start < tiles // 2:
                    kept = kept + jnp.where(slot < counts_ref[tile], 0.0, -1e30)
                out_ref[position, slot] = kept.astype(out_ref.dtype)
            row += rows


def encode(starts, lists, counts, bias, x, weights, weight):
    parts = len(weights)
    tokens, depth = x.shape
    width = bias.shape[1]
    slots, tiles = lists.shape
    shape = (tiles // 4, slots, tokens // tiles, width)
    dtypes = [jnp.float32 if start < tiles // 2 else jnp.bfloat16 for start in starts]
    taken = tokens // 4 * len(starts)
    return pl.pallas_call(
        functools.partial(encode_kernel, parts, starts),
        out_shape=[jax.ShapeDtypeStruct(shape, dtype) for dtype in dtypes],
        in_specs=[SMEM] * 2 + [VMEM] * (2 + parts),
        out_specs=[VMEM] * len(starts),
        scratch_shapes=[pltpu.VMEM((parts, taken, width), jnp.float32)],
        cost_estimate=pl.CostEstimate(
            flops=weight * 2 * taken * depth * parts * width,
            bytes_accessed=2 * (tokens * depth + depth * parts * width),
            transcendentals=0,
        ),
        **small("encode", 16),
    )(lists, counts, bias, x, *weights)


def merge_kernel(kept_ref, arrived_ref, total_ref, sent_ref):
    total = kept_ref[...] + arrived_ref[...].astype(jnp.float32)
    total_ref[...] = total
    sent_ref[...] = total.astype(sent_ref.dtype)


def merge(kept, arrived):
    return pl.pallas_call(
        merge_kernel,
        out_shape=[jax.ShapeDtypeStruct(kept.shape, kept.dtype), jax.ShapeDtypeStruct(kept.shape, arrived.dtype)],
        in_specs=[VMEM] * 2,
        out_specs=[VMEM] * 2,
        **small("merge"),
    )(kept, arrived)


def activate_kernel(kept_ref, arrived_ref, act_ref):
    preact = kept_ref[...] + arrived_ref[...].astype(jnp.float32)
    act_ref[...] = jnp.maximum(preact, 0.0).astype(act_ref.dtype)


def activate(kept, arrived):
    return pl.pallas_call(
        activate_kernel,
        out_shape=jax.ShapeDtypeStruct(kept.shape, arrived.dtype),
        in_specs=[VMEM] * 2,
        out_specs=VMEM,
        **small("activate"),
    )(kept, arrived)


def choose_kernel(*refs):
    sources, out_ref = refs[:-1], refs[-1]
    count = sources[0].shape[0]
    odd = lax.bitwise_and(lax.axis_index("layer"), 1)

    @pl.when(odd == 0)
    def _():
        for number in range(4):
            out_ref[number * count : (number + 1) * count] = sources[number][...]

    @pl.when(odd == 1)
    def _():
        out_ref[:count] = sources[4][...]
        out_ref[count : 3 * count] = sources[5][...]
        out_ref[3 * count :] = sources[6][...]


def choose(own, far):
    shape = own[0].shape
    return pl.pallas_call(
        choose_kernel,
        out_shape=jax.ShapeDtypeStruct((4 * shape[0],) + shape[1:], own[0].dtype),
        in_specs=[VMEM] * 7,
        out_specs=VMEM,
        **small("choose"),
    )(*own, *far)


def join_kernel(first_ref, second_ref, out_ref):
    count = first_ref.shape[0]
    out_ref[:count] = first_ref[...]
    out_ref[count:] = second_ref[...]


def join(first, second):
    return pl.pallas_call(
        join_kernel,
        out_shape=jax.ShapeDtypeStruct((2 * first.shape[0],) + first.shape[1:], first.dtype),
        in_specs=[VMEM] * 2,
        out_specs=VMEM,
        **small("join"),
    )(first, second)


def expand(dense, lists_ref, parts, first, act_refs):
    row = 0
    for act_ref in act_refs:
        count, slots, rows, width = act_ref.shape
        for position in range(count):
            tile = held_tile(first + position, lists_ref.shape[1], parts)
            for slot in range(slots):
                lanes = pl.ds(pl.multiple_of(lists_ref[slot, tile] * width, width), width)
                dense[row : row + rows, lanes] = act_ref[position, slot]
            row += rows
        first += count


def column_tiles(features):
    columns = 256 if features % 256 == 0 else features
    return [slice(first, first + columns) for first in range(0, features, columns)]


def early_kernel(parts, lists_ref, far_lists, *refs):
    own_refs, far_ref, (decoder_hbm, far_dec), refs = refs[:4], refs[4], refs[5:7], refs[7:]
    first_ref, rest_ref, own, other, own_dec, sem = refs
    copy = pltpu.make_async_copy(decoder_hbm.at[0], own_dec, sem)
    copy.start()
    quarter, latents = other.shape
    own[...] = jnp.zeros_like(own)
    other[...] = jnp.zeros_like(other)
    expand(own, lists_ref, parts, 0, own_refs)
    expand(other, far_lists, parts, 0, [far_ref])
    copy.wait()
    for lanes in column_tiles(first_ref.shape[1]):
        total = jnp.dot(own[...], own_dec[:, lanes], preferred_element_type=jnp.float32)
        rest_ref[:, lanes] = total[quarter:]
        first_ref[:, lanes] = total[:quarter] + jnp.dot(
            other[...], far_dec[:latents, lanes], preferred_element_type=jnp.float32
        )


def decode_early(lists, far_lists, acts, decoder, far_decoder, parts):
    _, latents, features = decoder.shape
    quarter = acts[0].shape[0] * acts[0].shape[2]
    return pl.pallas_call(
        functools.partial(early_kernel, parts),
        out_shape=[jax.ShapeDtypeStruct((count * quarter, features), jnp.float32) for count in (1, 3)],
        in_specs=[SMEM, SMEM] + [VMEM] * 5 + [ANY, VMEM],
        out_specs=[VMEM] * 2,
        scratch_shapes=[
            pltpu.VMEM((4 * quarter, latents), jnp.bfloat16),
            pltpu.VMEM((quarter, latents), jnp.bfloat16),
            pltpu.VMEM((latents, features), jnp.bfloat16),
            pltpu.SemaphoreType.DMA,
        ],
        cost_estimate=pl.CostEstimate(
            flops=10 * quarter * latents * features,
            bytes_accessed=2 * (2 * latents * features + 8 * quarter * features),
            transcendentals=0,
        ),
        **small("decode_early", 16),
    )(lists, far_lists, *acts, decoder, far_decoder)


def middle_kernel(parts, lists_ref, rest_ref, second, third, far_dec, total_ref, dense):
    latents = dense.shape[1]
    dense[...] = jnp.zeros_like(dense)
    expand(dense, lists_ref, parts, third.shape[0], [second, third])
    for lanes in column_tiles(rest_ref.shape[1]):
        total_ref[:, lanes] = rest_ref[:, lanes] + jnp.dot(
            dense[...], far_dec[:latents, lanes], preferred_element_type=jnp.float32
        )


def decode_middle(lists, rest, far, decoder, latents, parts):
    rows, features = rest.shape
    return pl.pallas_call(
        functools.partial(middle_kernel, parts),
        out_shape=jax.ShapeDtypeStruct(rest.shape, rest.dtype),
        in_specs=[SMEM] + [VMEM] * 4,
        out_specs=VMEM,
        scratch_shapes=[pltpu.VMEM((rows, latents), jnp.bfloat16)],
        cost_estimate=pl.CostEstimate(
            flops=2 * rows * latents * features,
            bytes_accessed=2 * (latents * features + 4 * rows * features),
            transcendentals=0,
        ),
        **small("decode_middle", 16),
    )(lists, rest, *far, decoder)


def late_kernel(parts, lists_ref, first_ref, rest_ref, near, near_dec, out_ref, dense, stage, sems):
    tokens, latents = dense.shape
    quarter, rows = tokens // 4, tokens // parts
    dense[...] = jnp.zeros_like(dense)
    expand(dense, lists_ref, parts, 0, [near])
    copies = []
    for number, lanes in enumerate(column_tiles(first_ref.shape[1])):
        total = jnp.dot(dense[...], near_dec[:latents, lanes], preferred_element_type=jnp.float32)
        stage[:quarter, lanes] = (total[:quarter] + first_ref[:, lanes]).astype(stage.dtype)
        stage[quarter:, lanes] = (total[quarter:] + rest_ref[:, lanes]).astype(stage.dtype)
        for held in range(parts):
            tiles = lists_ref.shape[1]
            row = pl.multiple_of(held_tile(held * (tiles // parts), tiles, parts) * (tokens // tiles), rows)
            copies.append(
                pltpu.make_async_copy(
                    stage.at[held * rows : (held + 1) * rows, lanes],
                    out_ref.at[pl.ds(row, rows), lanes],
                    sems.at[number, held],
                )
            )
            copies[-1].start()
    for copy in copies:
        copy.wait()


def decode_late(lists, partials, near, decoder, latents, parts):
    features = decoder.shape[1]
    tokens = near.shape[0] * near.shape[2]
    return pl.pallas_call(
        functools.partial(late_kernel, parts),
        out_shape=jax.ShapeDtypeStruct((tokens, features), jnp.bfloat16),
        in_specs=[SMEM] + [VMEM] * 4,
        out_specs=ANY,
        scratch_shapes=[
            pltpu.VMEM((tokens, latents), jnp.bfloat16),
            pltpu.VMEM((tokens, features), jnp.bfloat16),
            pltpu.SemaphoreType.DMA((len(column_tiles(features)), parts)),
        ],
        cost_estimate=pl.CostEstimate(
            flops=2 * tokens * latents * features,
            bytes_accessed=2 * (latents * features + 3 * tokens * features),
            transcendentals=0,
        ),
        **small("decode_late", 16),
    )(lists, *partials, near, decoder)


def shards(layer_input, enc_weight, enc_bias, dec_weight, block_lists, block_counts):
    parts = lax.axis_size("latent")
    x, encoder, decoder = layer_input[0], enc_weight[0], dec_weight[0]
    lists, counts = block_lists[0].T, block_counts[0]
    slots, tiles = lists.shape
    targets, latents, _ = decoder.shape
    if targets != 3 or parts < 2 or parts & (parts - 1) or tiles % 4:
        raise ValueError("mesh")

    with jax.named_scope("encoder_rows"):
        pieces = fetch_rows(encoder, parts)
        pieces, decoder = lax.optimization_barrier((pieces, decoder))
        weights = [pieces[0]] + [None] * (parts - 1)
        for step in sorted(range(1, parts), reverse=True):
            weights[step] = swapped(pieces[step], step)
    with jax.named_scope("decoder_weights"):
        near_rows, far_rows = fetch_decoders(lists, decoder)
        near_decoder, far_decoder = passed_along(near_rows, 1), passed_along(far_rows, 2)
        near_decoder, far_decoder = lax.optimization_barrier((near_decoder, far_decoder))
        near_lists, far_lists = [
            rows[latents : latents + slots, :tiles].astype(jnp.int32) for rows in (near_decoder, far_decoder)
        ]

    with jax.named_scope("encode"):
        quarter = tiles // 4
        (sent_a,) = encode([2 * quarter], lists, counts, enc_bias, x, weights, 64)
        arrived_a = swapped(sent_a, 1)
        starts = [3 * quarter, 0, quarter]
        sent_b, kept_a, kept_b = encode(starts, lists, counts, enc_bias, x, weights, 1)
        arrived_b = swapped(sent_b, 1)
        step = 2
        while step < parts:
            kept_a, sent_a = merge(kept_a, arrived_a)
            kept_b, sent_b = merge(kept_b, arrived_b)
            arrived_a = swapped(sent_a, step)
            arrived_a, sent_b = lax.optimization_barrier((arrived_a, sent_b))
            arrived_b = swapped(sent_b, step)
            step *= 2
        own_a, own_b = activate(kept_a, arrived_a), activate(kept_b, arrived_b)
    with jax.named_scope("spread"):
        late_a = swapped(own_a, 1)
        far_a = passed_along(own_a, 2)
        late_b = swapped(own_b, 1)
        joined = join(own_b, late_a)
        late_b, far_a = lax.optimization_barrier((late_b, far_a))
        own = [own_a, own_b, late_a, late_b]
        far = [far_a] + [passed_along(piece, 2) for piece in (joined, late_b)]
    with jax.named_scope("decode"):
        first, rest = decode_early(lists, far_lists, own + far[:1], decoder, far_decoder, parts)
        first, rest, far[2] = lax.optimization_barrier((first, rest, far[2]))
        near = across_cores(choose(own, far))
        rest = decode_middle(far_lists, rest, far[1:], far_decoder, latents, parts)
        return decode_late(near_lists, [first, rest], near, near_decoder, latents, parts)[None]


def solution(mesh):
    placed = (
        P("layer", None, "latent"),
        P("layer", None, "latent"),
        P("layer", "latent"),
        P("layer", None, None, "latent"),
        P("layer", None, None),
        P("layer", None),
    )
    return jax.shard_map(
        shards, mesh=mesh, in_specs=placed, out_specs=P("layer", None, "latent"), check_vma=False
    )
```

```python
import functools

import jax
import jax.numpy as jnp
from jax import lax
from jax.experimental import pallas as pl
from jax.experimental.pallas import tpu as pltpu
from jax.sharding import PartitionSpec as P

VMEM = pl.BlockSpec(memory_space=pltpu.VMEM)
SMEM = pl.BlockSpec(memory_space=pltpu.SMEM)
ANY = pl.BlockSpec(memory_space=pl.ANY)
HBM = pl.BlockSpec(memory_space=pltpu.HBM)


def swapped(value, step):
    count = lax.axis_size("latent")
    return lax.ppermute(value, "latent", [(i, i ^ step) for i in range(count)])


def passed_along(value, steps):
    count = lax.axis_size("layer")
    return lax.ppermute(value, "layer", [(i, i + steps) for i in range(count - steps)])


def across_cores(value):
    count = lax.axis_size("layer")
    return lax.ppermute(value, "layer", [(i, i ^ 1) for i in range(count)])


def small(name, megabytes=8):
    return dict(compiler_params=pltpu.CompilerParams(vmem_limit_bytes=megabytes << 20), name=name)


def held_tile(position, tiles, parts):
    each = tiles // parts
    number, half = position // each, parts // 2
    parity = lax.bitwise_and(lax.axis_index("latent"), 1)
    return (2 * (number % half) + (parity if number < half else 1 - parity)) * each + position % each


def fetch_rows_kernel(encoder_ref, *piece_refs):
    depth = piece_refs[0].shape[0]
    for step, piece in enumerate(piece_refs):
        first = pl.multiple_of(lax.bitwise_xor(lax.axis_index("latent"), step) * depth, depth)
        piece[...] = encoder_ref[pl.ds(first, depth), :]


def fetch_rows(encoder, parts):
    depth = encoder.shape[0] // parts
    return pl.pallas_call(
        fetch_rows_kernel,
        out_shape=[jax.ShapeDtypeStruct((depth, encoder.shape[1]), encoder.dtype)] * parts,
        in_specs=[VMEM],
        out_specs=[VMEM] * parts,
        **small("fetch_rows"),
    )(encoder)


def id_place(slot, tiles, features, width):
    each = features // width
    return slot // each * tiles, slice(slot % each * width, (slot % each + 1) * width)


def fetch_decoders_kernel(parts, width, lists_ref, counts_ref, decoder_ref, *refs):
    out_refs, ids = refs[:-1], refs[-1]
    _, latents, features = decoder_ref.shape
    slots, tiles = lists_ref.shape
    ids[...] = jnp.zeros_like(ids)
    for slot in range(slots):
        first, lanes = id_place(slot, tiles, features, width)
        for position in range(tiles):
            tile = held_tile(position, tiles, parts)
            block = jnp.where(slot < counts_ref[tile], lists_ref[slot, tile], -1).astype(jnp.float32)
            ids[first + position : first + position + 1, lanes] = jnp.full((1, width), block, jnp.float32)
    for number, out_ref in enumerate(out_refs):
        out_ref[:latents, :] = decoder_ref[number + 1]
        out_ref[latents:, :] = ids[...].astype(out_ref.dtype)


def fetch_decoders(lists, counts, decoder, width, parts):
    targets, latents, features = decoder.shape
    slots, tiles = lists.shape
    rows = -(-slots // (features // width)) * tiles
    rows += -rows % 16
    shape = jax.ShapeDtypeStruct((latents + rows, features), decoder.dtype)
    return pl.pallas_call(
        functools.partial(fetch_decoders_kernel, parts, width),
        out_shape=[shape] * (targets - 1) + [jax.ShapeDtypeStruct((rows, features), jnp.float32)],
        in_specs=[SMEM, SMEM, VMEM],
        out_specs=[VMEM] * targets,
        **small("fetch_decoders", 16),
    )(lists, counts, decoder)


def encode_kernel(parts, starts, tiles, ids_ref, bias_ref, x_ref, *refs):
    weight_refs, out_refs, partial = refs[:parts], refs[parts:-1], refs[-1]
    width = bias_ref.shape[1]
    count, slots, rows, _ = out_refs[0].shape
    held = [[held_tile(start + position, tiles, parts) for position in range(count)] for start in starts]
    taken = [x_ref[pl.ds(pl.multiple_of(tile * rows, rows), rows), :] for group in held for tile in group]
    taken = jnp.concatenate(taken, axis=0)
    for first in range(0, parts, 2):
        stacked = jnp.concatenate([ref[...] for ref in weight_refs[first : first + 2]], axis=1)
        product = jnp.dot(taken, stacked, preferred_element_type=jnp.float32)
        for source in range(first, first + 2):
            block = product[:, (source - first) * width : (source - first + 1) * width]
            partial[source] = block if source else block + bias_ref[...]
    blocks = [lax.bitwise_xor(lax.axis_index("latent"), source).astype(jnp.float32) for source in range(parts)]
    row = 0
    for start, out_ref in zip(starts, out_refs):
        for position in range(count):
            for slot in range(slots):
                first, lanes = id_place(slot, tiles, ids_ref.shape[1], width)
                first += start + position
                wanted = ids_ref[first : first + 1, lanes]
                kept = jnp.zeros((rows, width), jnp.float32)
                for source in range(parts):
                    kept = kept + jnp.where(wanted == blocks[source], 1.0, 0.0) * partial[source, row : row + rows, :]
                out_ref[position, slot] = kept.astype(out_ref.dtype)
            row += rows


def encode(starts, ids, bias, x, weights, slots, tiles, weight):
    parts = len(weights)
    tokens, depth = x.shape
    width = bias.shape[1]
    shape = (tiles // 4, slots, tokens // tiles, width)
    dtypes = [jnp.float32 if start < tiles // 2 else jnp.bfloat16 for start in starts]
    taken = tokens // 4 * len(starts)
    return pl.pallas_call(
        functools.partial(encode_kernel, parts, starts, tiles),
        out_shape=[jax.ShapeDtypeStruct(shape, dtype) for dtype in dtypes],
        in_specs=[VMEM] * (3 + parts),
        out_specs=[VMEM] * len(starts),
        scratch_shapes=[pltpu.VMEM((parts, taken, width), jnp.float32)],
        cost_estimate=pl.CostEstimate(
            flops=weight * 2 * taken * depth * parts * width,
            bytes_accessed=2 * (tokens * depth + depth * parts * width),
            transcendentals=0,
        ),
        **small("encode", 16),
    )(ids, bias, x, *weights)


def merge_kernel(kept_ref, arrived_ref, total_ref, sent_ref):
    total = kept_ref[...] + arrived_ref[...].astype(jnp.float32)
    total_ref[...] = total
    sent_ref[...] = total.astype(sent_ref.dtype)


def merge(kept, arrived):
    return pl.pallas_call(
        merge_kernel,
        out_shape=[jax.ShapeDtypeStruct(kept.shape, kept.dtype), jax.ShapeDtypeStruct(kept.shape, arrived.dtype)],
        in_specs=[VMEM] * 2,
        out_specs=[VMEM] * 2,
        **small("merge"),
    )(kept, arrived)


def activate_kernel(kept_ref, arrived_ref, act_ref):
    preact = kept_ref[...] + arrived_ref[...].astype(jnp.float32)
    act_ref[...] = jnp.maximum(preact, 0.0).astype(act_ref.dtype)


def activate(kept, arrived):
    return pl.pallas_call(
        activate_kernel,
        out_shape=jax.ShapeDtypeStruct(kept.shape, arrived.dtype),
        in_specs=[VMEM] * 2,
        out_specs=VMEM,
        **small("activate"),
    )(kept, arrived)


def choose_kernel(*refs):
    sources, out_ref = refs[:-1], refs[-1]
    count = sources[0].shape[0]
    odd = lax.bitwise_and(lax.axis_index("layer"), 1)

    @pl.when(odd == 0)
    def _():
        for number in range(4):
            out_ref[number * count : (number + 1) * count] = sources[number][...]

    @pl.when(odd == 1)
    def _():
        out_ref[:count] = sources[4][...]
        out_ref[count : 3 * count] = sources[5][...]
        out_ref[3 * count :] = sources[6][...]


def choose(own, far):
    shape = own[0].shape
    return pl.pallas_call(
        choose_kernel,
        out_shape=jax.ShapeDtypeStruct((4 * shape[0],) + shape[1:], own[0].dtype),
        in_specs=[VMEM] * 7,
        out_specs=VMEM,
        **small("choose"),
    )(*own, *far)


def join_kernel(first_ref, second_ref, out_ref):
    count = first_ref.shape[0]
    out_ref[:count] = first_ref[...]
    out_ref[count:] = second_ref[...]


def join(first, second):
    return pl.pallas_call(
        join_kernel,
        out_shape=jax.ShapeDtypeStruct((2 * first.shape[0],) + first.shape[1:], first.dtype),
        in_specs=[VMEM] * 2,
        out_specs=VMEM,
        **small("join"),
    )(first, second)


def expand(dense, ids_ref, tiles, first, act_refs):
    row = 0
    for act_ref in act_refs:
        count, slots, rows, width = act_ref.shape
        for position in range(count):
            wanted = []
            for slot in range(slots):
                start, lanes = id_place(slot, tiles, ids_ref.shape[1], width)
                start += first + position
                wanted.append(ids_ref[start : start + 1, lanes])
            for block in range(dense.shape[1] // width):
                total = None
                for slot in range(slots):
                    chosen = jnp.where(wanted[slot] == block, 1.0, 0.0).astype(dense.dtype)
                    term = act_ref[position, slot] * chosen
                    total = term if total is None else total + term
                dense[row : row + rows, block * width : (block + 1) * width] = total
            row += rows
        first += count


def column_tiles(features):
    columns = 256 if features % 256 == 0 else features
    return [slice(first, first + columns) for first in range(0, features, columns)]


def early_kernel(tiles, ids_ref, *refs):
    own_refs, far_ref, (decoder_hbm, far_dec), refs = refs[:4], refs[4], refs[5:7], refs[7:]
    first_ref, rest_ref, own, other, own_dec, far_ids, sem = refs
    copy = pltpu.make_async_copy(decoder_hbm.at[0], own_dec, sem)
    copy.start()
    quarter, latents = other.shape
    far_ids[...] = far_dec[latents:, :].astype(far_ids.dtype)
    expand(own, ids_ref, tiles, 0, own_refs)
    expand(other, far_ids, tiles, 0, [far_ref])
    copy.wait()
    for lanes in column_tiles(first_ref.shape[1]):
        total = jnp.dot(own[...], own_dec[:, lanes], preferred_element_type=jnp.float32)
        rest_ref[:, lanes] = total[quarter:]
        first_ref[:, lanes] = total[:quarter] + jnp.dot(
            other[...], far_dec[:latents, lanes], preferred_element_type=jnp.float32
        )


def decode_early(ids, acts, decoder, far_decoder, tiles):
    _, latents, features = decoder.shape
    quarter = acts[0].shape[0] * acts[0].shape[2]
    return pl.pallas_call(
        functools.partial(early_kernel, tiles),
        out_shape=[jax.ShapeDtypeStruct((count * quarter, features), jnp.float32) for count in (1, 3)],
        in_specs=[VMEM] * 6 + [ANY, VMEM],
        out_specs=[VMEM] * 2,
        scratch_shapes=[
            pltpu.VMEM((4 * quarter, latents), jnp.bfloat16),
            pltpu.VMEM((quarter, latents), jnp.bfloat16),
            pltpu.VMEM((latents, features), jnp.bfloat16),
            pltpu.VMEM(ids.shape, jnp.float32),
            pltpu.SemaphoreType.DMA,
        ],
        cost_estimate=pl.CostEstimate(
            flops=10 * quarter * latents * features,
            bytes_accessed=2 * (2 * latents * features + 8 * quarter * features),
            transcendentals=0,
        ),
        **small("decode_early", 16),
    )(ids, *acts, decoder, far_decoder)


def middle_kernel(tiles, rest_ref, second, third, far_dec, total_ref, dense, ids):
    latents = dense.shape[1]
    ids[...] = far_dec[latents:, :].astype(ids.dtype)
    expand(dense, ids, tiles, third.shape[0], [second, third])
    for lanes in column_tiles(rest_ref.shape[1]):
        total_ref[:, lanes] = rest_ref[:, lanes] + jnp.dot(
            dense[...], far_dec[:latents, lanes], preferred_element_type=jnp.float32
        )


def decode_middle(rest, far, decoder, latents, tiles):
    rows, features = rest.shape
    return pl.pallas_call(
        functools.partial(middle_kernel, tiles),
        out_shape=jax.ShapeDtypeStruct(rest.shape, rest.dtype),
        in_specs=[VMEM] * 4,
        out_specs=VMEM,
        scratch_shapes=[
            pltpu.VMEM((rows, latents), jnp.bfloat16),
            pltpu.VMEM((decoder.shape[0] - latents, features), jnp.float32),
        ],
        cost_estimate=pl.CostEstimate(
            flops=2 * rows * latents * features,
            bytes_accessed=2 * (latents * features + 4 * rows * features),
            transcendentals=0,
        ),
        **small("decode_middle", 16),
    )(rest, *far, decoder)


def late_kernel(parts, tiles, first_ref, rest_ref, near, near_dec, out_ref, dense, stage, ids, sems):
    tokens, latents = dense.shape
    quarter, rows = tokens // 4, tokens // parts
    ids[...] = near_dec[latents:, :].astype(ids.dtype)
    expand(dense, ids, tiles, 0, [near])
    copies = []
    for number, lanes in enumerate(column_tiles(first_ref.shape[1])):
        total = jnp.dot(dense[...], near_dec[:latents, lanes], preferred_element_type=jnp.float32)
        stage[:quarter, lanes] = (total[:quarter] + first_ref[:, lanes]).astype(stage.dtype)
        stage[quarter:, lanes] = (total[quarter:] + rest_ref[:, lanes]).astype(stage.dtype)
        for held in range(parts):
            row = pl.multiple_of(held_tile(held * (tiles // parts), tiles, parts) * (tokens // tiles), rows)
            copies.append(
                pltpu.make_async_copy(
                    stage.at[held * rows : (held + 1) * rows, lanes],
                    out_ref.at[pl.ds(row, rows), lanes],
                    sems.at[number, held],
                )
            )
            copies[-1].start()
    for copy in copies:
        copy.wait()


def decode_late(partials, near, decoder, latents, parts):
    features = decoder.shape[1]
    tokens = near.shape[0] * near.shape[2]
    return pl.pallas_call(
        functools.partial(late_kernel, parts, near.shape[0]),
        out_shape=jax.ShapeDtypeStruct((tokens, features), jnp.bfloat16),
        in_specs=[VMEM] * 4,
        out_specs=ANY,
        scratch_shapes=[
            pltpu.VMEM((tokens, latents), jnp.bfloat16),
            pltpu.VMEM((tokens, features), jnp.bfloat16),
            pltpu.VMEM((decoder.shape[0] - latents, features), jnp.float32),
            pltpu.SemaphoreType.DMA((len(column_tiles(features)), parts)),
        ],
        cost_estimate=pl.CostEstimate(
            flops=2 * tokens * latents * features,
            bytes_accessed=2 * (latents * features + 3 * tokens * features),
            transcendentals=0,
        ),
        **small("decode_late", 16),
    )(*partials, near, decoder)


def shards(layer_input, enc_weight, enc_bias, dec_weight, block_lists, block_counts):
    parts = lax.axis_size("latent")
    x, encoder, decoder = layer_input[0], enc_weight[0], dec_weight[0]
    lists, counts = block_lists[0].T, block_counts[0]
    slots, tiles = lists.shape
    targets, latents, _ = decoder.shape
    if targets != 3 or parts < 2 or parts & (parts - 1) or tiles % 4:
        raise ValueError("mesh")

    with jax.named_scope("encoder_rows"):
        pieces = fetch_rows(encoder, parts)
        pieces, decoder = lax.optimization_barrier((pieces, decoder))
        weights = [pieces[0]] + [None] * (parts - 1)
        for step in sorted(range(1, parts), reverse=True):
            weights[step] = swapped(pieces[step], step)
    with jax.named_scope("decoder_weights"):
        near_rows, far_rows, ids = fetch_decoders(lists, counts, decoder, encoder.shape[1], parts)
        near_decoder, far_decoder = passed_along(near_rows, 1), passed_along(far_rows, 2)
        near_decoder, far_decoder = lax.optimization_barrier((near_decoder, far_decoder))

    with jax.named_scope("encode"):
        quarter = tiles // 4
        (sent_a,) = encode([2 * quarter], ids, enc_bias, x, weights, slots, tiles, 64)
        arrived_a = swapped(sent_a, 1)
        starts = [3 * quarter, 0, quarter]
        sent_b, kept_a, kept_b = encode(starts, ids, enc_bias, x, weights, slots, tiles, 1)
        arrived_b = swapped(sent_b, 1)
        step = 2
        while step < parts:
            kept_a, sent_a = merge(kept_a, arrived_a)
            kept_b, sent_b = merge(kept_b, arrived_b)
            arrived_a = swapped(sent_a, step)
            arrived_a, sent_b = lax.optimization_barrier((arrived_a, sent_b))
            arrived_b = swapped(sent_b, step)
            step *= 2
        own_a, own_b = activate(kept_a, arrived_a), activate(kept_b, arrived_b)
    with jax.named_scope("spread"):
        late_a = swapped(own_a, 1)
        far_a = passed_along(own_a, 2)
        late_b = swapped(own_b, 1)
        joined = join(own_b, late_a)
        late_b, far_a = lax.optimization_barrier((late_b, far_a))
        own = [own_a, own_b, late_a, late_b]
        far = [far_a] + [passed_along(piece, 2) for piece in (joined, late_b)]
    with jax.named_scope("decode"):
        first, rest = decode_early(ids, own + far[:1], decoder, far_decoder, tiles)
        first, rest, far[2] = lax.optimization_barrier((first, rest, far[2]))
        near = across_cores(choose(own, far))
        rest = decode_middle(rest, far[1:], far_decoder, latents, tiles)
        return decode_late([first, rest], near, near_decoder, latents, parts)[None]


def solution(mesh):
    placed = (
        P("layer", None, "latent"),
        P("layer", None, "latent"),
        P("layer", "latent"),
        P("layer", None, None, "latent"),
        P("layer", None, None),
        P("layer", None),
    )
    return jax.shard_map(
        shards, mesh=mesh, in_specs=placed, out_specs=P("layer", None, "latent"), check_vma=False
    )
```

```python
import functools

import jax
import jax.numpy as jnp
from jax import lax
from jax.experimental import pallas as pl
from jax.experimental.pallas import tpu as pltpu
from jax.sharding import PartitionSpec as P

VMEM = pl.BlockSpec(memory_space=pltpu.VMEM)
SMEM = pl.BlockSpec(memory_space=pltpu.SMEM)
ANY = pl.BlockSpec(memory_space=pl.ANY)
HBM = pl.BlockSpec(memory_space=pltpu.HBM)


def swapped(value, step):
    count = lax.axis_size("latent")
    return lax.ppermute(value, "latent", [(i, i ^ step) for i in range(count)])


def interleaved(parts):
    across = list(range(parts // 2, parts))
    within = list(range(1, parts // 2))
    return [step for pair in zip(across, within + [None]) for step in pair if step]


def passed_along(value, steps):
    count = lax.axis_size("layer")
    return lax.ppermute(value, "layer", [(i, i + steps) for i in range(count - steps)])


def across_cores(value):
    count = lax.axis_size("layer")
    return lax.ppermute(value, "layer", [(i, i ^ 1) for i in range(count)])


def small(name, megabytes=8):
    return dict(compiler_params=pltpu.CompilerParams(vmem_limit_bytes=megabytes << 20), name=name)


def held_tile(position, tiles, parts):
    each = tiles // parts
    number, half = position // each, parts // 2
    parity = lax.bitwise_and(lax.axis_index("latent"), 1)
    return (2 * (number % half) + (parity if number < half else 1 - parity)) * each + position % each


def fetch_rows_kernel(encoder_ref, *piece_refs):
    depth = piece_refs[0].shape[0]
    for step, piece in enumerate(piece_refs):
        first = pl.multiple_of(lax.bitwise_xor(lax.axis_index("latent"), step) * depth, depth)
        piece[...] = encoder_ref[pl.ds(first, depth), :]


def fetch_rows(encoder, parts):
    depth = encoder.shape[0] // parts
    return pl.pallas_call(
        fetch_rows_kernel,
        out_shape=[jax.ShapeDtypeStruct((depth, encoder.shape[1]), encoder.dtype)] * parts,
        in_specs=[VMEM],
        out_specs=[VMEM] * parts,
        **small("fetch_rows"),
    )(encoder)


def id_place(slot, tiles, features, width):
    each = features // width
    return slot // each * tiles, slice(slot % each * width, (slot % each + 1) * width)


def fetch_decoders_kernel(parts, width, lists_ref, counts_ref, decoder_ref, *refs):
    out_refs, ids = refs[:-1], refs[-1]
    _, latents, features = decoder_ref.shape
    slots, tiles = lists_ref.shape
    ids[...] = jnp.zeros_like(ids)
    for slot in range(slots):
        first, lanes = id_place(slot, tiles, features, width)
        for position in range(tiles):
            tile = held_tile(position, tiles, parts)
            block = jnp.where(slot < counts_ref[tile], lists_ref[slot, tile], -1).astype(jnp.float32)
            ids[first + position : first + position + 1, lanes] = jnp.full((1, width), block, jnp.float32)
    for number, out_ref in enumerate(out_refs):
        out_ref[:latents, :] = decoder_ref[number + 1]
        out_ref[latents:, :] = ids[...].astype(out_ref.dtype)


def fetch_decoders(lists, counts, decoder, width, parts):
    targets, latents, features = decoder.shape
    slots, tiles = lists.shape
    rows = -(-slots // (features // width)) * tiles
    rows += -rows % 16
    shape = jax.ShapeDtypeStruct((latents + rows, features), decoder.dtype)
    return pl.pallas_call(
        functools.partial(fetch_decoders_kernel, parts, width),
        out_shape=[shape] * (targets - 1) + [jax.ShapeDtypeStruct((rows, features), jnp.float32)],
        in_specs=[SMEM, SMEM, VMEM],
        out_specs=[VMEM] * targets,
        **small("fetch_decoders", 16),
    )(lists, counts, decoder)


def encode_kernel(parts, starts, tiles, ids_ref, bias_ref, x_ref, *refs):
    weight_refs, out_refs, partial = refs[:parts], refs[parts:-1], refs[-1]
    width = bias_ref.shape[1]
    count, slots, rows, _ = out_refs[0].shape
    held = [[held_tile(start + position, tiles, parts) for position in range(count)] for start in starts]
    taken = [x_ref[pl.ds(pl.multiple_of(tile * rows, rows), rows), :] for group in held for tile in group]
    taken = jnp.concatenate(taken, axis=0)
    sources = [0] + interleaved(parts)
    for first in range(0, parts, 2):
        stacked = jnp.concatenate([ref[...] for ref in weight_refs[first : first + 2]], axis=1)
        product = jnp.dot(taken, stacked, preferred_element_type=jnp.float32)
        for number in range(2):
            block = product[:, number * width : (number + 1) * width]
            partial[sources[first + number]] = block if first + number else block + bias_ref[...]
    blocks = [lax.bitwise_xor(lax.axis_index("latent"), source).astype(jnp.float32) for source in range(parts)]
    row = 0
    for start, out_ref in zip(starts, out_refs):
        for position in range(count):
            for slot in range(slots):
                first, lanes = id_place(slot, tiles, ids_ref.shape[1], width)
                first += start + position
                wanted = ids_ref[first : first + 1, lanes]
                kept = jnp.zeros((rows, width), jnp.float32)
                for source in range(parts):
                    kept = kept + jnp.where(wanted == blocks[source], 1.0, 0.0) * partial[source, row : row + rows, :]
                out_ref[position, slot] = kept.astype(out_ref.dtype)
            row += rows


def encode(starts, ids, bias, x, weights, slots, tiles, weight):
    parts = len(weights)
    tokens, depth = x.shape
    width = bias.shape[1]
    shape = (tiles // 4, slots, tokens // tiles, width)
    dtypes = [jnp.float32 if start < tiles // 2 else jnp.bfloat16 for start in starts]
    taken = tokens // 4 * len(starts)
    return pl.pallas_call(
        functools.partial(encode_kernel, parts, starts, tiles),
        out_shape=[jax.ShapeDtypeStruct(shape, dtype) for dtype in dtypes],
        in_specs=[VMEM] * (3 + parts),
        out_specs=[VMEM] * len(starts),
        scratch_shapes=[pltpu.VMEM((parts, taken, width), jnp.float32)],
        cost_estimate=pl.CostEstimate(
            flops=weight * 2 * taken * depth * parts * width,
            bytes_accessed=2 * (tokens * depth + depth * parts * width),
            transcendentals=0,
        ),
        **small("encode", 16),
    )(ids, bias, x, *weights)


def merge_kernel(kept_ref, arrived_ref, total_ref, sent_ref):
    total = kept_ref[...] + arrived_ref[...].astype(jnp.float32)
    total_ref[...] = total
    sent_ref[...] = total.astype(sent_ref.dtype)


def merge(kept, arrived):
    return pl.pallas_call(
        merge_kernel,
        out_shape=[jax.ShapeDtypeStruct(kept.shape, kept.dtype), jax.ShapeDtypeStruct(kept.shape, arrived.dtype)],
        in_specs=[VMEM] * 2,
        out_specs=[VMEM] * 2,
        **small("merge"),
    )(kept, arrived)


def activate_kernel(kept_ref, arrived_ref, act_ref):
    preact = kept_ref[...] + arrived_ref[...].astype(jnp.float32)
    act_ref[...] = jnp.maximum(preact, 0.0).astype(act_ref.dtype)


def activate(kept, arrived):
    return pl.pallas_call(
        activate_kernel,
        out_shape=jax.ShapeDtypeStruct(kept.shape, arrived.dtype),
        in_specs=[VMEM] * 2,
        out_specs=VMEM,
        **small("activate"),
    )(kept, arrived)


def choose_kernel(*refs):
    sources, out_ref = refs[:-1], refs[-1]
    count = sources[0].shape[0]
    odd = lax.bitwise_and(lax.axis_index("layer"), 1)

    @pl.when(odd == 0)
    def _():
        for number in range(4):
            out_ref[number * count : (number + 1) * count] = sources[number][...]

    @pl.when(odd == 1)
    def _():
        out_ref[:count] = sources[4][...]
        out_ref[count : 3 * count] = sources[5][...]
        out_ref[3 * count :] = sources[6][...]


def choose(own, far):
    shape = own[0].shape
    return pl.pallas_call(
        choose_kernel,
        out_shape=jax.ShapeDtypeStruct((4 * shape[0],) + shape[1:], own[0].dtype),
        in_specs=[VMEM] * 7,
        out_specs=VMEM,
        **small("choose"),
    )(*own, *far)


def join_kernel(first_ref, second_ref, out_ref):
    count = first_ref.shape[0]
    out_ref[:count] = first_ref[...]
    out_ref[count:] = second_ref[...]


def join(first, second):
    return pl.pallas_call(
        join_kernel,
        out_shape=jax.ShapeDtypeStruct((2 * first.shape[0],) + first.shape[1:], first.dtype),
        in_specs=[VMEM] * 2,
        out_specs=VMEM,
        **small("join"),
    )(first, second)


def expand(dense, ids_ref, tiles, first, act_refs):
    row = 0
    for act_ref in act_refs:
        count, slots, rows, width = act_ref.shape
        for position in range(count):
            wanted = []
            for slot in range(slots):
                start, lanes = id_place(slot, tiles, ids_ref.shape[1], width)
                start += first + position
                wanted.append(ids_ref[start : start + 1, lanes])
            for block in range(dense.shape[1] // width):
                total = None
                for slot in range(slots):
                    chosen = jnp.where(wanted[slot] == block, 1.0, 0.0).astype(dense.dtype)
                    term = act_ref[position, slot] * chosen
                    total = term if total is None else total + term
                dense[row : row + rows, block * width : (block + 1) * width] = total
            row += rows
        first += count


def column_tiles(features):
    columns = 256 if features % 256 == 0 else features
    return [slice(first, first + columns) for first in range(0, features, columns)]


def early_kernel(tiles, ids_ref, *refs):
    own_refs, far_ref, (decoder_hbm, far_dec), refs = refs[:4], refs[4], refs[5:7], refs[7:]
    first_ref, rest_ref, own, other, own_dec, far_ids, sem = refs
    copy = pltpu.make_async_copy(decoder_hbm.at[0], own_dec, sem)
    copy.start()
    quarter, latents = other.shape
    far_ids[...] = far_dec[latents:, :].astype(far_ids.dtype)
    expand(own, ids_ref, tiles, 0, own_refs)
    expand(other, far_ids, tiles, 0, [far_ref])
    copy.wait()
    for lanes in column_tiles(first_ref.shape[1]):
        total = jnp.dot(own[...], own_dec[:, lanes], preferred_element_type=jnp.float32)
        rest_ref[:, lanes] = total[quarter:]
        first_ref[:, lanes] = total[:quarter] + jnp.dot(
            other[...], far_dec[:latents, lanes], preferred_element_type=jnp.float32
        )


def decode_early(ids, acts, decoder, far_decoder, tiles):
    _, latents, features = decoder.shape
    quarter = acts[0].shape[0] * acts[0].shape[2]
    return pl.pallas_call(
        functools.partial(early_kernel, tiles),
        out_shape=[jax.ShapeDtypeStruct((count * quarter, features), jnp.float32) for count in (1, 3)],
        in_specs=[VMEM] * 6 + [ANY, VMEM],
        out_specs=[VMEM] * 2,
        scratch_shapes=[
            pltpu.VMEM((4 * quarter, latents), jnp.bfloat16),
            pltpu.VMEM((quarter, latents), jnp.bfloat16),
            pltpu.VMEM((latents, features), jnp.bfloat16),
            pltpu.VMEM(ids.shape, jnp.float32),
            pltpu.SemaphoreType.DMA,
        ],
        cost_estimate=pl.CostEstimate(
            flops=10 * quarter * latents * features,
            bytes_accessed=2 * (2 * latents * features + 8 * quarter * features),
            transcendentals=0,
        ),
        **small("decode_early", 16),
    )(ids, *acts, decoder, far_decoder)


def middle_kernel(tiles, rest_ref, second, third, far_dec, total_ref, dense, ids):
    latents = dense.shape[1]
    ids[...] = far_dec[latents:, :].astype(ids.dtype)
    expand(dense, ids, tiles, third.shape[0], [second, third])
    for lanes in column_tiles(rest_ref.shape[1]):
        total_ref[:, lanes] = rest_ref[:, lanes] + jnp.dot(
            dense[...], far_dec[:latents, lanes], preferred_element_type=jnp.float32
        )


def decode_middle(rest, far, decoder, latents, tiles):
    rows, features = rest.shape
    return pl.pallas_call(
        functools.partial(middle_kernel, tiles),
        out_shape=jax.ShapeDtypeStruct(rest.shape, rest.dtype),
        in_specs=[VMEM] * 4,
        out_specs=VMEM,
        scratch_shapes=[
            pltpu.VMEM((rows, latents), jnp.bfloat16),
            pltpu.VMEM((decoder.shape[0] - latents, features), jnp.float32),
        ],
        cost_estimate=pl.CostEstimate(
            flops=2 * rows * latents * features,
            bytes_accessed=2 * (latents * features + 4 * rows * features),
            transcendentals=0,
        ),
        **small("decode_middle", 16),
    )(rest, *far, decoder)


def late_kernel(parts, tiles, first_ref, rest_ref, near, near_dec, out_ref, dense, stage, ids, sems):
    tokens, latents = dense.shape
    quarter, rows = tokens // 4, tokens // parts
    ids[...] = near_dec[latents:, :].astype(ids.dtype)
    expand(dense, ids, tiles, 0, [near])
    copies = []
    for number, lanes in enumerate(column_tiles(first_ref.shape[1])):
        total = jnp.dot(dense[...], near_dec[:latents, lanes], preferred_element_type=jnp.float32)
        stage[:quarter, lanes] = (total[:quarter] + first_ref[:, lanes]).astype(stage.dtype)
        stage[quarter:, lanes] = (total[quarter:] + rest_ref[:, lanes]).astype(stage.dtype)
        for held in range(parts):
            row = pl.multiple_of(held_tile(held * (tiles // parts), tiles, parts) * (tokens // tiles), rows)
            copies.append(
                pltpu.make_async_copy(
                    stage.at[held * rows : (held + 1) * rows, lanes],
                    out_ref.at[pl.ds(row, rows), lanes],
                    sems.at[number, held],
                )
            )
            copies[-1].start()
    for copy in copies:
        copy.wait()


def decode_late(partials, near, decoder, latents, parts):
    features = decoder.shape[1]
    tokens = near.shape[0] * near.shape[2]
    return pl.pallas_call(
        functools.partial(late_kernel, parts, near.shape[0]),
        out_shape=jax.ShapeDtypeStruct((tokens, features), jnp.bfloat16),
        in_specs=[VMEM] * 4,
        out_specs=ANY,
        scratch_shapes=[
            pltpu.VMEM((tokens, latents), jnp.bfloat16),
            pltpu.VMEM((tokens, features), jnp.bfloat16),
            pltpu.VMEM((decoder.shape[0] - latents, features), jnp.float32),
            pltpu.SemaphoreType.DMA((len(column_tiles(features)), parts)),
        ],
        cost_estimate=pl.CostEstimate(
            flops=2 * tokens * latents * features,
            bytes_accessed=2 * (latents * features + 3 * tokens * features),
            transcendentals=0,
        ),
        **small("decode_late", 16),
    )(*partials, near, decoder)


def shards(layer_input, enc_weight, enc_bias, dec_weight, block_lists, block_counts):
    parts = lax.axis_size("latent")
    x, encoder, decoder = layer_input[0], enc_weight[0], dec_weight[0]
    lists, counts = block_lists[0].T, block_counts[0]
    slots, tiles = lists.shape
    targets, latents, _ = decoder.shape
    if targets != 3 or parts < 2 or parts & (parts - 1) or tiles % 4:
        raise ValueError("mesh")

    with jax.named_scope("encoder_rows"):
        pieces = fetch_rows(encoder, parts)
        pieces, decoder = lax.optimization_barrier((pieces, decoder))
        weights = [pieces[0]] + [swapped(pieces[step], step) for step in interleaved(parts)]
    with jax.named_scope("decoder_weights"):
        near_rows, far_rows, ids = fetch_decoders(lists, counts, decoder, encoder.shape[1], parts)
        near_decoder, far_decoder = passed_along(near_rows, 1), passed_along(far_rows, 2)
        near_decoder, far_decoder = lax.optimization_barrier((near_decoder, far_decoder))

    with jax.named_scope("encode"):
        quarter = tiles // 4
        (sent_a,) = encode([2 * quarter], ids, enc_bias, x, weights, slots, tiles, 64)
        arrived_a = swapped(sent_a, 1)
        starts = [3 * quarter, 0, quarter]
        sent_b, kept_a, kept_b = encode(starts, ids, enc_bias, x, weights, slots, tiles, 1)
        arrived_b = swapped(sent_b, 1)
        step = 2
        while step < parts:
            kept_a, sent_a = merge(kept_a, arrived_a)
            kept_b, sent_b = merge(kept_b, arrived_b)
            arrived_a = swapped(sent_a, step)
            arrived_a, sent_b = lax.optimization_barrier((arrived_a, sent_b))
            arrived_b = swapped(sent_b, step)
            step *= 2
        own_a, own_b = activate(kept_a, arrived_a), activate(kept_b, arrived_b)
    with jax.named_scope("spread"):
        late_a = swapped(own_a, 1)
        far_a = passed_along(own_a, 2)
        late_b = swapped(own_b, 1)
        joined = join(own_b, late_a)
        late_b, far_a = lax.optimization_barrier((late_b, far_a))
        own = [own_a, own_b, late_a, late_b]
        far = [far_a] + [passed_along(piece, 2) for piece in (joined, late_b)]
    with jax.named_scope("decode"):
        first, rest = decode_early(ids, own + far[:1], decoder, far_decoder, tiles)
        first, rest, far[2] = lax.optimization_barrier((first, rest, far[2]))
        near = across_cores(choose(own, far))
        rest = decode_middle(rest, far[1:], far_decoder, latents, tiles)
        return decode_late([first, rest], near, near_decoder, latents, parts)[None]


def solution(mesh):
    placed = (
        P("layer", None, "latent"),
        P("layer", None, "latent"),
        P("layer", "latent"),
        P("layer", None, None, "latent"),
        P("layer", None, None),
        P("layer", None),
    )
    return jax.shard_map(
        shards, mesh=mesh, in_specs=placed, out_specs=P("layer", None, "latent"), check_vma=False
    )
```

```python
import functools

import jax
import jax.numpy as jnp
from jax import lax
from jax.experimental import pallas as pl
from jax.experimental.pallas import tpu as pltpu
from jax.sharding import PartitionSpec as P

VMEM = pl.BlockSpec(memory_space=pltpu.VMEM)
SMEM = pl.BlockSpec(memory_space=pltpu.SMEM)
ANY = pl.BlockSpec(memory_space=pl.ANY)
HBM = pl.BlockSpec(memory_space=pltpu.HBM)


def swapped(value, step):
    count = lax.axis_size("latent")
    return lax.ppermute(value, "latent", [(i, i ^ step) for i in range(count)])


def interleaved(parts):
    across = list(range(parts // 2, parts))
    within = list(range(1, parts // 2))
    return [step for pair in zip(across, within + [None]) for step in pair if step]


def passed_along(value, steps):
    count = lax.axis_size("layer")
    return lax.ppermute(value, "layer", [(i, i + steps) for i in range(count - steps)])


def across_cores(value):
    count = lax.axis_size("layer")
    return lax.ppermute(value, "layer", [(i, i ^ 1) for i in range(count)])


def small(name, megabytes=8):
    return dict(compiler_params=pltpu.CompilerParams(vmem_limit_bytes=megabytes << 20), name=name)


def held_tile(position, tiles, parts):
    each = tiles // parts
    number, half = position // each, parts // 2
    parity = lax.bitwise_and(lax.axis_index("latent"), 1)
    return (2 * (number % half) + (parity if number < half else 1 - parity)) * each + position % each


def fetch_rows_kernel(encoder_ref, *piece_refs):
    depth = piece_refs[0].shape[0]
    for step, piece in enumerate(piece_refs):
        first = pl.multiple_of(lax.bitwise_xor(lax.axis_index("latent"), step) * depth, depth)
        piece[...] = encoder_ref[pl.ds(first, depth), :]


def fetch_rows(encoder, parts):
    depth = encoder.shape[0] // parts
    return pl.pallas_call(
        fetch_rows_kernel,
        out_shape=[jax.ShapeDtypeStruct((depth, encoder.shape[1]), encoder.dtype)] * parts,
        in_specs=[VMEM],
        out_specs=[VMEM] * parts,
        **small("fetch_rows"),
    )(encoder)


def id_place(slot, tiles, features, width):
    each = features // width
    return slot // each * tiles, slice(slot % each * width, (slot % each + 1) * width)


def fetch_decoders_kernel(parts, width, lists_ref, counts_ref, decoder_ref, *refs):
    out_refs, ids = refs[:-1], refs[-1]
    _, latents, features = decoder_ref.shape
    slots, tiles = lists_ref.shape
    ids[...] = jnp.zeros_like(ids)
    for slot in range(slots):
        first, lanes = id_place(slot, tiles, features, width)
        for position in range(tiles):
            tile = held_tile(position, tiles, parts)
            block = jnp.where(slot < counts_ref[tile], lists_ref[slot, tile], -1).astype(jnp.float32)
            ids[first + position : first + position + 1, lanes] = jnp.full((1, width), block, jnp.float32)
    for number, out_ref in enumerate(out_refs):
        out_ref[:latents, :] = decoder_ref[number + 1]
        out_ref[latents:, :] = ids[...].astype(out_ref.dtype)


def fetch_decoders(lists, counts, decoder, width, parts):
    targets, latents, features = decoder.shape
    slots, tiles = lists.shape
    rows = -(-slots // (features // width)) * tiles
    rows += -rows % 16
    shape = jax.ShapeDtypeStruct((latents + rows, features), decoder.dtype)
    return pl.pallas_call(
        functools.partial(fetch_decoders_kernel, parts, width),
        out_shape=[shape] * (targets - 1) + [jax.ShapeDtypeStruct((rows, features), jnp.float32)],
        in_specs=[SMEM, SMEM, VMEM],
        out_specs=[VMEM] * targets,
        **small("fetch_decoders", 16),
    )(lists, counts, decoder)


def encode_kernel(parts, starts, tiles, ids_ref, bias_ref, x_ref, *refs):
    weight_refs, out_refs, partial = refs[:parts], refs[parts:-1], refs[-1]
    width = bias_ref.shape[1]
    count, slots, rows, _ = out_refs[0].shape
    held = [[held_tile(start + position, tiles, parts) for position in range(count)] for start in starts]
    taken = [x_ref[pl.ds(pl.multiple_of(tile * rows, rows), rows), :] for group in held for tile in group]
    taken = jnp.concatenate(taken, axis=0)
    sources = [0] + interleaved(parts)
    for first in range(0, parts, 2):
        stacked = jnp.concatenate([ref[...] for ref in weight_refs[first : first + 2]], axis=1)
        product = jnp.dot(taken, stacked, preferred_element_type=jnp.float32)
        for number in range(2):
            block = product[:, number * width : (number + 1) * width]
            partial[sources[first + number]] = block if first + number else block + bias_ref[...]
    blocks = [lax.bitwise_xor(lax.axis_index("latent"), source).astype(jnp.float32) for source in range(parts)]
    row = 0
    for start, out_ref in zip(starts, out_refs):
        for position in range(count):
            for slot in range(slots):
                first, lanes = id_place(slot, tiles, ids_ref.shape[1], width)
                first += start + position
                wanted = ids_ref[first : first + 1, lanes]
                kept = jnp.zeros((rows, width), jnp.float32)
                for source in range(parts):
                    kept = kept + jnp.where(wanted == blocks[source], 1.0, 0.0) * partial[source, row : row + rows, :]
                out_ref[position, slot] = kept.astype(out_ref.dtype)
            row += rows


def encode(starts, ids, bias, x, weights, slots, tiles, weight):
    parts = len(weights)
    tokens, depth = x.shape
    width = bias.shape[1]
    shape = (tiles // 4, slots, tokens // tiles, width)
    dtypes = [jnp.float32 if start < tiles // 2 else jnp.bfloat16 for start in starts]
    taken = tokens // 4 * len(starts)
    return pl.pallas_call(
        functools.partial(encode_kernel, parts, starts, tiles),
        out_shape=[jax.ShapeDtypeStruct(shape, dtype) for dtype in dtypes],
        in_specs=[VMEM] * (3 + parts),
        out_specs=[VMEM] * len(starts),
        scratch_shapes=[pltpu.VMEM((parts, taken, width), jnp.float32)],
        cost_estimate=pl.CostEstimate(
            flops=weight * 2 * taken * depth * parts * width,
            bytes_accessed=2 * (tokens * depth + depth * parts * width),
            transcendentals=0,
        ),
        **small("encode", 16),
    )(ids, bias, x, *weights)


def merge_kernel(kept_ref, arrived_ref, total_ref, sent_ref):
    total = kept_ref[...] + arrived_ref[...].astype(jnp.float32)
    total_ref[...] = total
    sent_ref[...] = total.astype(sent_ref.dtype)


def merge(kept, arrived):
    return pl.pallas_call(
        merge_kernel,
        out_shape=[jax.ShapeDtypeStruct(kept.shape, kept.dtype), jax.ShapeDtypeStruct(kept.shape, arrived.dtype)],
        in_specs=[VMEM] * 2,
        out_specs=[VMEM] * 2,
        **small("merge"),
    )(kept, arrived)


def activate_kernel(kept_ref, arrived_ref, act_ref):
    preact = kept_ref[...] + arrived_ref[...].astype(jnp.float32)
    act_ref[...] = jnp.maximum(preact, 0.0).astype(act_ref.dtype)


def activate(kept, arrived):
    return pl.pallas_call(
        activate_kernel,
        out_shape=jax.ShapeDtypeStruct(kept.shape, arrived.dtype),
        in_specs=[VMEM] * 2,
        out_specs=VMEM,
        **small("activate"),
    )(kept, arrived)


def choose_kernel(*refs):
    sources, out_ref = refs[:-1], refs[-1]
    count = sources[0].shape[0]
    odd = lax.bitwise_and(lax.axis_index("layer"), 1)

    @pl.when(odd == 0)
    def _():
        for number in range(4):
            out_ref[number * count : (number + 1) * count] = sources[number][...]

    @pl.when(odd == 1)
    def _():
        out_ref[:count] = sources[4][...]
        out_ref[count : 3 * count] = sources[5][...]
        out_ref[3 * count :] = sources[6][...]


def choose(own, far):
    shape = own[0].shape
    return pl.pallas_call(
        choose_kernel,
        out_shape=jax.ShapeDtypeStruct((4 * shape[0],) + shape[1:], own[0].dtype),
        in_specs=[VMEM] * 7,
        out_specs=VMEM,
        **small("choose"),
    )(*own, *far)


def join_kernel(first_ref, second_ref, out_ref):
    count = first_ref.shape[0]
    out_ref[:count] = first_ref[...]
    out_ref[count:] = second_ref[...]


def join(first, second):
    return pl.pallas_call(
        join_kernel,
        out_shape=jax.ShapeDtypeStruct((2 * first.shape[0],) + first.shape[1:], first.dtype),
        in_specs=[VMEM] * 2,
        out_specs=VMEM,
        **small("join"),
    )(first, second)


def expand(dense, ids_ref, tiles, first, act_refs):
    row = 0
    for act_ref in act_refs:
        count, slots, rows, width = act_ref.shape
        for position in range(count):
            wanted = []
            for slot in range(slots):
                start, lanes = id_place(slot, tiles, ids_ref.shape[1], width)
                start += first + position
                wanted.append(ids_ref[start : start + 1, lanes])
            for block in range(dense.shape[1] // width):
                total = None
                for slot in range(slots):
                    chosen = jnp.where(wanted[slot] == block, 1.0, 0.0).astype(dense.dtype)
                    term = act_ref[position, slot] * chosen
                    total = term if total is None else total + term
                dense[row : row + rows, block * width : (block + 1) * width] = total
            row += rows
        first += count


def column_tiles(features):
    columns = 256 if features % 256 == 0 else features
    return [slice(first, first + columns) for first in range(0, features, columns)]


def early_kernel(tiles, ids_ref, *refs):
    own_refs, far_ref, (decoder_hbm, far_dec), refs = refs[:4], refs[4], refs[5:7], refs[7:]
    first_ref, rest_ref, own, other, own_dec, far_ids, sem = refs
    copy = pltpu.make_async_copy(decoder_hbm.at[0], own_dec, sem)
    copy.start()
    quarter, latents = other.shape
    far_ids[...] = far_dec[latents:, :].astype(far_ids.dtype)
    expand(own, ids_ref, tiles, 0, own_refs)
    expand(other, far_ids, tiles, 0, [far_ref])
    copy.wait()
    for lanes in column_tiles(first_ref.shape[1]):
        total = jnp.dot(own[...], own_dec[:, lanes], preferred_element_type=jnp.float32)
        rest_ref[:, lanes] = total[quarter:]
        first_ref[:, lanes] = total[:quarter] + jnp.dot(
            other[...], far_dec[:latents, lanes], preferred_element_type=jnp.float32
        )


def decode_early(ids, acts, decoder, far_decoder, tiles):
    _, latents, features = decoder.shape
    quarter = acts[0].shape[0] * acts[0].shape[2]
    return pl.pallas_call(
        functools.partial(early_kernel, tiles),
        out_shape=[jax.ShapeDtypeStruct((count * quarter, features), jnp.float32) for count in (1, 3)],
        in_specs=[VMEM] * 6 + [ANY, VMEM],
        out_specs=[VMEM] * 2,
        scratch_shapes=[
            pltpu.VMEM((4 * quarter, latents), jnp.bfloat16),
            pltpu.VMEM((quarter, latents), jnp.bfloat16),
            pltpu.VMEM((latents, features), jnp.bfloat16),
            pltpu.VMEM(ids.shape, jnp.float32),
            pltpu.SemaphoreType.DMA,
        ],
        cost_estimate=pl.CostEstimate(
            flops=10 * quarter * latents * features,
            bytes_accessed=2 * (2 * latents * features + 8 * quarter * features),
            transcendentals=0,
        ),
        **small("decode_early", 16),
    )(ids, *acts, decoder, far_decoder)


def middle_kernel(tiles, rest_ref, second, third, far_dec, total_ref, dense, ids):
    latents = dense.shape[1]
    ids[...] = far_dec[latents:, :].astype(ids.dtype)
    expand(dense, ids, tiles, third.shape[0], [second, third])
    for lanes in column_tiles(rest_ref.shape[1]):
        total_ref[:, lanes] = rest_ref[:, lanes] + jnp.dot(
            dense[...], far_dec[:latents, lanes], preferred_element_type=jnp.float32
        )


def decode_middle(rest, far, decoder, latents, tiles):
    rows, features = rest.shape
    return pl.pallas_call(
        functools.partial(middle_kernel, tiles),
        out_shape=jax.ShapeDtypeStruct(rest.shape, rest.dtype),
        in_specs=[VMEM] * 4,
        out_specs=VMEM,
        scratch_shapes=[
            pltpu.VMEM((rows, latents), jnp.bfloat16),
            pltpu.VMEM((decoder.shape[0] - latents, features), jnp.float32),
        ],
        cost_estimate=pl.CostEstimate(
            flops=2 * rows * latents * features,
            bytes_accessed=2 * (latents * features + 4 * rows * features),
            transcendentals=0,
        ),
        **small("decode_middle", 16),
    )(rest, *far, decoder)


def late_kernel(parts, tiles, first_ref, rest_ref, near, near_dec, out_ref, dense, stage, ids, sems):
    tokens, latents = dense.shape
    quarter, rows = tokens // 4, tokens // parts
    ids[...] = near_dec[latents:, :].astype(ids.dtype)
    expand(dense, ids, tiles, 0, [near])
    copies = []
    for number, lanes in enumerate(column_tiles(first_ref.shape[1])):
        total = jnp.dot(dense[...], near_dec[:latents, lanes], preferred_element_type=jnp.float32)
        stage[:quarter, lanes] = (total[:quarter] + first_ref[:, lanes]).astype(stage.dtype)
        stage[quarter:, lanes] = (total[quarter:] + rest_ref[:, lanes]).astype(stage.dtype)
        for held in range(parts):
            row = pl.multiple_of(held_tile(held * (tiles // parts), tiles, parts) * (tokens // tiles), rows)
            copies.append(
                pltpu.make_async_copy(
                    stage.at[held * rows : (held + 1) * rows, lanes],
                    out_ref.at[pl.ds(row, rows), lanes],
                    sems.at[number, held],
                )
            )
            copies[-1].start()
    for copy in copies:
        copy.wait()


def decode_late(partials, near, decoder, latents, parts):
    features = decoder.shape[1]
    tokens = near.shape[0] * near.shape[2]
    return pl.pallas_call(
        functools.partial(late_kernel, parts, near.shape[0]),
        out_shape=jax.ShapeDtypeStruct((tokens, features), jnp.bfloat16),
        in_specs=[VMEM] * 4,
        out_specs=ANY,
        scratch_shapes=[
            pltpu.VMEM((tokens, latents), jnp.bfloat16),
            pltpu.VMEM((tokens, features), jnp.bfloat16),
            pltpu.VMEM((decoder.shape[0] - latents, features), jnp.float32),
            pltpu.SemaphoreType.DMA((len(column_tiles(features)), parts)),
        ],
        cost_estimate=pl.CostEstimate(
            flops=2 * tokens * latents * features,
            bytes_accessed=2 * (latents * features + 3 * tokens * features),
            transcendentals=0,
        ),
        **small("decode_late", 16),
    )(*partials, near, decoder)


def shards(layer_input, enc_weight, enc_bias, dec_weight, block_lists, block_counts):
    parts = lax.axis_size("latent")
    x, encoder, decoder = layer_input[0], enc_weight[0], dec_weight[0]
    lists, counts = block_lists[0].T, block_counts[0]
    slots, tiles = lists.shape
    targets, latents, _ = decoder.shape
    if targets != 3 or parts < 2 or parts & (parts - 1) or tiles % 4:
        raise ValueError("mesh")

    with jax.named_scope("encoder_rows"):
        pieces = fetch_rows(encoder, parts)
        pieces, decoder = lax.optimization_barrier((pieces, decoder))
        weights = [pieces[0]] + [swapped(pieces[step], step) for step in interleaved(parts)]
        weights[1], lists = lax.optimization_barrier((weights[1], lists))
    with jax.named_scope("decoder_weights"):
        near_rows, far_rows, ids = fetch_decoders(lists, counts, decoder, encoder.shape[1], parts)
        near_decoder, far_decoder = passed_along(near_rows, 1), passed_along(far_rows, 2)
        near_decoder, far_decoder = lax.optimization_barrier((near_decoder, far_decoder))

    with jax.named_scope("encode"):
        quarter = tiles // 4
        (sent_a,) = encode([2 * quarter], ids, enc_bias, x, weights, slots, tiles, 64)
        arrived_a = swapped(sent_a, 1)
        starts = [3 * quarter, 0, quarter]
        sent_b, kept_a, kept_b = encode(starts, ids, enc_bias, x, weights, slots, tiles, 1)
        arrived_b = swapped(sent_b, 1)
        step = 2
        while step < parts:
            kept_a, sent_a = merge(kept_a, arrived_a)
            kept_b, sent_b = merge(kept_b, arrived_b)
            arrived_a = swapped(sent_a, step)
            arrived_a, sent_b = lax.optimization_barrier((arrived_a, sent_b))
            arrived_b = swapped(sent_b, step)
            step *= 2
        own_a, own_b = activate(kept_a, arrived_a), activate(kept_b, arrived_b)
    with jax.named_scope("spread"):
        late_a = swapped(own_a, 1)
        far_a = passed_along(own_a, 2)
        late_b = swapped(own_b, 1)
        joined = join(own_b, late_a)
        late_b, far_a = lax.optimization_barrier((late_b, far_a))
        own = [own_a, own_b, late_a, late_b]
        far = [far_a] + [passed_along(piece, 2) for piece in (joined, late_b)]
    with jax.named_scope("decode"):
        first, rest = decode_early(ids, own + far[:1], decoder, far_decoder, tiles)
        first, rest, far[2] = lax.optimization_barrier((first, rest, far[2]))
        near = across_cores(choose(own, far))
        rest = decode_middle(rest, far[1:], far_decoder, latents, tiles)
        return decode_late([first, rest], near, near_decoder, latents, parts)[None]


def solution(mesh):
    placed = (
        P("layer", None, "latent"),
        P("layer", None, "latent"),
        P("layer", "latent"),
        P("layer", None, None, "latent"),
        P("layer", None, None),
        P("layer", None),
    )
    return jax.shard_map(
        shards, mesh=mesh, in_specs=placed, out_specs=P("layer", None, "latent"), check_vma=False
    )
```

```python
import functools

import jax
import jax.numpy as jnp
from jax import lax
from jax.experimental import pallas as pl
from jax.experimental.pallas import tpu as pltpu
from jax.sharding import PartitionSpec as P

VMEM = pl.BlockSpec(memory_space=pltpu.VMEM)
SMEM = pl.BlockSpec(memory_space=pltpu.SMEM)
ANY = pl.BlockSpec(memory_space=pl.ANY)
HBM = pl.BlockSpec(memory_space=pltpu.HBM)


def swapped(value, step):
    count = lax.axis_size("latent")
    return lax.ppermute(value, "latent", [(i, i ^ step) for i in range(count)])


def interleaved(parts):
    across = list(range(parts // 2, parts))
    within = list(range(1, parts // 2))
    return [step for pair in zip(across, within + [None]) for step in pair if step]


def passed_along(value, steps):
    count = lax.axis_size("layer")
    return lax.ppermute(value, "layer", [(i, i + steps) for i in range(count - steps)])


def across_cores(value):
    count = lax.axis_size("layer")
    return lax.ppermute(value, "layer", [(i, i ^ 1) for i in range(count)])


def small(name, megabytes=8):
    return dict(compiler_params=pltpu.CompilerParams(vmem_limit_bytes=megabytes << 20), name=name)


def held_tile(position, tiles, parts):
    each = tiles // parts
    number, half = position // each, parts // 2
    parity = lax.bitwise_and(lax.axis_index("latent"), 1)
    return (2 * (number % half) + (parity if number < half else 1 - parity)) * each + position % each


def fetch_rows_kernel(encoder_ref, *piece_refs):
    depth = piece_refs[0].shape[0]
    for step, piece in enumerate(piece_refs):
        first = pl.multiple_of(lax.bitwise_xor(lax.axis_index("latent"), step) * depth, depth)
        piece[...] = encoder_ref[pl.ds(first, depth), :]


def fetch_rows(encoder, parts):
    depth = encoder.shape[0] // parts
    return pl.pallas_call(
        fetch_rows_kernel,
        out_shape=[jax.ShapeDtypeStruct((depth, encoder.shape[1]), encoder.dtype)] * parts,
        in_specs=[VMEM],
        out_specs=[VMEM] * parts,
        **small("fetch_rows"),
    )(encoder)


def id_place(slot, tiles, features, width):
    each = features // width
    return slot // each * tiles, slice(slot % each * width, (slot % each + 1) * width)


def fetch_decoders_kernel(parts, width, lists_ref, counts_ref, decoder_ref, *refs):
    out_refs, ids = refs[:-1], refs[-1]
    _, latents, features = decoder_ref.shape
    slots, tiles = lists_ref.shape
    ids[...] = jnp.zeros_like(ids)
    for slot in range(slots):
        first, lanes = id_place(slot, tiles, features, width)
        for position in range(tiles):
            tile = held_tile(position, tiles, parts)
            block = jnp.where(slot < counts_ref[tile], lists_ref[slot, tile], -1).astype(jnp.float32)
            ids[first + position : first + position + 1, lanes] = jnp.full((1, width), block, jnp.float32)
    for number, out_ref in enumerate(out_refs):
        out_ref[:latents, :] = decoder_ref[number + 1]
        out_ref[latents:, :] = ids[...].astype(out_ref.dtype)


def fetch_decoders(lists, counts, decoder, width, parts):
    targets, latents, features = decoder.shape
    slots, tiles = lists.shape
    rows = -(-slots // (features // width)) * tiles
    rows += -rows % 16
    shape = jax.ShapeDtypeStruct((latents + rows, features), decoder.dtype)
    return pl.pallas_call(
        functools.partial(fetch_decoders_kernel, parts, width),
        out_shape=[shape] * (targets - 1) + [jax.ShapeDtypeStruct((rows, features), jnp.float32)],
        in_specs=[SMEM, SMEM, VMEM],
        out_specs=[VMEM] * targets,
        **small("fetch_decoders", 16),
    )(lists, counts, decoder)


def encode_kernel(parts, starts, tiles, ids_ref, bias_ref, x_ref, *refs):
    weight_refs, out_refs, partial = refs[:parts], refs[parts:-1], refs[-1]
    width = bias_ref.shape[1]
    count, slots, rows, _ = out_refs[0].shape
    held = [[held_tile(start + position, tiles, parts) for position in range(count)] for start in starts]
    taken = [x_ref[pl.ds(pl.multiple_of(tile * rows, rows), rows), :] for group in held for tile in group]
    taken = jnp.concatenate(taken, axis=0)
    sources = [0] + interleaved(parts)
    wide = min(parts, 4)
    for first in range(0, parts, wide):
        stacked = jnp.concatenate([ref[...] for ref in weight_refs[first : first + wide]], axis=1)
        product = jnp.dot(taken, stacked, preferred_element_type=jnp.float32)
        for number in range(wide):
            block = product[:, number * width : (number + 1) * width]
            partial[sources[first + number]] = block if first + number else block + bias_ref[...]
    blocks = [lax.bitwise_xor(lax.axis_index("latent"), source).astype(jnp.float32) for source in range(parts)]
    row = 0
    for start, out_ref in zip(starts, out_refs):
        for position in range(count):
            for slot in range(slots):
                first, lanes = id_place(slot, tiles, ids_ref.shape[1], width)
                first += start + position
                wanted = ids_ref[first : first + 1, lanes]
                kept = jnp.zeros((rows, width), jnp.float32)
                for source in range(parts):
                    kept = kept + jnp.where(wanted == blocks[source], 1.0, 0.0) * partial[source, row : row + rows, :]
                out_ref[position, slot] = kept.astype(out_ref.dtype)
            row += rows


def encode(starts, ids, bias, x, weights, slots, tiles, weight):
    parts = len(weights)
    tokens, depth = x.shape
    width = bias.shape[1]
    shape = (tiles // 4, slots, tokens // tiles, width)
    dtypes = [jnp.float32 if start < tiles // 2 else jnp.bfloat16 for start in starts]
    taken = tokens // 4 * len(starts)
    return pl.pallas_call(
        functools.partial(encode_kernel, parts, starts, tiles),
        out_shape=[jax.ShapeDtypeStruct(shape, dtype) for dtype in dtypes],
        in_specs=[VMEM] * (3 + parts),
        out_specs=[VMEM] * len(starts),
        scratch_shapes=[pltpu.VMEM((parts, taken, width), jnp.float32)],
        cost_estimate=pl.CostEstimate(
            flops=weight * 2 * taken * depth * parts * width,
            bytes_accessed=2 * (tokens * depth + depth * parts * width),
            transcendentals=0,
        ),
        **small("encode", 16),
    )(ids, bias, x, *weights)


def merge_kernel(kept_ref, arrived_ref, total_ref, sent_ref):
    total = kept_ref[...] + arrived_ref[...].astype(jnp.float32)
    total_ref[...] = total
    sent_ref[...] = total.astype(sent_ref.dtype)


def merge(kept, arrived):
    return pl.pallas_call(
        merge_kernel,
        out_shape=[jax.ShapeDtypeStruct(kept.shape, kept.dtype), jax.ShapeDtypeStruct(kept.shape, arrived.dtype)],
        in_specs=[VMEM] * 2,
        out_specs=[VMEM] * 2,
        **small("merge"),
    )(kept, arrived)


def activate_kernel(kept_ref, arrived_ref, act_ref):
    preact = kept_ref[...] + arrived_ref[...].astype(jnp.float32)
    act_ref[...] = jnp.maximum(preact, 0.0).astype(act_ref.dtype)


def activate(kept, arrived):
    return pl.pallas_call(
        activate_kernel,
        out_shape=jax.ShapeDtypeStruct(kept.shape, arrived.dtype),
        in_specs=[VMEM] * 2,
        out_specs=VMEM,
        **small("activate"),
    )(kept, arrived)


def choose_kernel(*refs):
    sources, out_ref = refs[:-1], refs[-1]
    count = sources[0].shape[0]
    odd = lax.bitwise_and(lax.axis_index("layer"), 1)

    @pl.when(odd == 0)
    def _():
        for number in range(4):
            out_ref[number * count : (number + 1) * count] = sources[number][...]

    @pl.when(odd == 1)
    def _():
        out_ref[:count] = sources[4][...]
        out_ref[count : 3 * count] = sources[5][...]
        out_ref[3 * count :] = sources[6][...]


def choose(own, far):
    shape = own[0].shape
    return pl.pallas_call(
        choose_kernel,
        out_shape=jax.ShapeDtypeStruct((4 * shape[0],) + shape[1:], own[0].dtype),
        in_specs=[VMEM] * 7,
        out_specs=VMEM,
        **small("choose"),
    )(*own, *far)


def join_kernel(first_ref, second_ref, out_ref):
    count = first_ref.shape[0]
    out_ref[:count] = first_ref[...]
    out_ref[count:] = second_ref[...]


def join(first, second):
    return pl.pallas_call(
        join_kernel,
        out_shape=jax.ShapeDtypeStruct((2 * first.shape[0],) + first.shape[1:], first.dtype),
        in_specs=[VMEM] * 2,
        out_specs=VMEM,
        **small("join"),
    )(first, second)


def expand(dense, ids_ref, tiles, first, act_refs):
    row = 0
    for act_ref in act_refs:
        count, slots, rows, width = act_ref.shape
        for position in range(count):
            wanted = []
            for slot in range(slots):
                start, lanes = id_place(slot, tiles, ids_ref.shape[1], width)
                start += first + position
                wanted.append(ids_ref[start : start + 1, lanes])
            for block in range(dense.shape[1] // width):
                total = None
                for slot in range(slots):
                    chosen = jnp.where(wanted[slot] == block, 1.0, 0.0).astype(dense.dtype)
                    term = act_ref[position, slot] * chosen
                    total = term if total is None else total + term
                dense[row : row + rows, block * width : (block + 1) * width] = total
            row += rows
        first += count


def column_tiles(features):
    columns = 512 if features % 512 == 0 else features
    return [slice(first, first + columns) for first in range(0, features, columns)]


def early_kernel(tiles, ids_ref, *refs):
    own_refs, far_ref, (decoder_hbm, far_dec), refs = refs[:4], refs[4], refs[5:7], refs[7:]
    first_ref, rest_ref, own, other, own_dec, far_ids, sem = refs
    copy = pltpu.make_async_copy(decoder_hbm.at[0], own_dec, sem)
    copy.start()
    quarter, latents = other.shape
    far_ids[...] = far_dec[latents:, :].astype(far_ids.dtype)
    expand(own, ids_ref, tiles, 0, own_refs)
    expand(other, far_ids, tiles, 0, [far_ref])
    copy.wait()
    for lanes in column_tiles(first_ref.shape[1]):
        total = jnp.dot(own[...], own_dec[:, lanes], preferred_element_type=jnp.float32)
        rest_ref[:, lanes] = total[quarter:]
        first_ref[:, lanes] = total[:quarter] + jnp.dot(
            other[...], far_dec[:latents, lanes], preferred_element_type=jnp.float32
        )


def decode_early(ids, acts, decoder, far_decoder, tiles):
    _, latents, features = decoder.shape
    quarter = acts[0].shape[0] * acts[0].shape[2]
    return pl.pallas_call(
        functools.partial(early_kernel, tiles),
        out_shape=[jax.ShapeDtypeStruct((count * quarter, features), jnp.float32) for count in (1, 3)],
        in_specs=[VMEM] * 6 + [ANY, VMEM],
        out_specs=[VMEM] * 2,
        scratch_shapes=[
            pltpu.VMEM((4 * quarter, latents), jnp.bfloat16),
            pltpu.VMEM((quarter, latents), jnp.bfloat16),
            pltpu.VMEM((latents, features), jnp.bfloat16),
            pltpu.VMEM(ids.shape, jnp.float32),
            pltpu.SemaphoreType.DMA,
        ],
        cost_estimate=pl.CostEstimate(
            flops=10 * quarter * latents * features,
            bytes_accessed=2 * (2 * latents * features + 8 * quarter * features),
            transcendentals=0,
        ),
        **small("decode_early", 16),
    )(ids, *acts, decoder, far_decoder)


def middle_kernel(tiles, rest_ref, second, third, far_dec, total_ref, dense, ids):
    latents = dense.shape[1]
    ids[...] = far_dec[latents:, :].astype(ids.dtype)
    expand(dense, ids, tiles, third.shape[0], [second, third])
    for lanes in column_tiles(rest_ref.shape[1]):
        total_ref[:, lanes] = rest_ref[:, lanes] + jnp.dot(
            dense[...], far_dec[:latents, lanes], preferred_element_type=jnp.float32
        )


def decode_middle(rest, far, decoder, latents, tiles):
    rows, features = rest.shape
    return pl.pallas_call(
        functools.partial(middle_kernel, tiles),
        out_shape=jax.ShapeDtypeStruct(rest.shape, rest.dtype),
        in_specs=[VMEM] * 4,
        out_specs=VMEM,
        scratch_shapes=[
            pltpu.VMEM((rows, latents), jnp.bfloat16),
            pltpu.VMEM((decoder.shape[0] - latents, features), jnp.float32),
        ],
        cost_estimate=pl.CostEstimate(
            flops=2 * rows * latents * features,
            bytes_accessed=2 * (latents * features + 4 * rows * features),
            transcendentals=0,
        ),
        **small("decode_middle", 16),
    )(rest, *far, decoder)


def late_kernel(parts, tiles, first_ref, rest_ref, near, near_dec, out_ref, dense, stage, ids, sems):
    tokens, latents = dense.shape
    quarter, rows = tokens // 4, tokens // parts
    ids[...] = near_dec[latents:, :].astype(ids.dtype)
    expand(dense, ids, tiles, 0, [near])
    copies = []
    for number, lanes in enumerate(column_tiles(first_ref.shape[1])):
        total = jnp.dot(dense[...], near_dec[:latents, lanes], preferred_element_type=jnp.float32)
        stage[:quarter, lanes] = (total[:quarter] + first_ref[:, lanes]).astype(stage.dtype)
        stage[quarter:, lanes] = (total[quarter:] + rest_ref[:, lanes]).astype(stage.dtype)
        for held in range(parts):
            row = pl.multiple_of(held_tile(held * (tiles // parts), tiles, parts) * (tokens // tiles), rows)
            copies.append(
                pltpu.make_async_copy(
                    stage.at[held * rows : (held + 1) * rows, lanes],
                    out_ref.at[pl.ds(row, rows), lanes],
                    sems.at[number, held],
                )
            )
            copies[-1].start()
    for copy in copies:
        copy.wait()


def decode_late(partials, near, decoder, latents, parts):
    features = decoder.shape[1]
    tokens = near.shape[0] * near.shape[2]
    return pl.pallas_call(
        functools.partial(late_kernel, parts, near.shape[0]),
        out_shape=jax.ShapeDtypeStruct((tokens, features), jnp.bfloat16),
        in_specs=[VMEM] * 4,
        out_specs=ANY,
        scratch_shapes=[
            pltpu.VMEM((tokens, latents), jnp.bfloat16),
            pltpu.VMEM((tokens, features), jnp.bfloat16),
            pltpu.VMEM((decoder.shape[0] - latents, features), jnp.float32),
            pltpu.SemaphoreType.DMA((len(column_tiles(features)), parts)),
        ],
        cost_estimate=pl.CostEstimate(
            flops=2 * tokens * latents * features,
            bytes_accessed=2 * (latents * features + 3 * tokens * features),
            transcendentals=0,
        ),
        **small("decode_late", 16),
    )(*partials, near, decoder)


def shards(layer_input, enc_weight, enc_bias, dec_weight, block_lists, block_counts):
    parts = lax.axis_size("latent")
    x, encoder, decoder = layer_input[0], enc_weight[0], dec_weight[0]
    lists, counts = block_lists[0].T, block_counts[0]
    slots, tiles = lists.shape
    targets, latents, _ = decoder.shape
    if targets != 3 or parts < 2 or parts & (parts - 1) or tiles % 4:
        raise ValueError("mesh")

    with jax.named_scope("encoder_rows"):
        pieces = fetch_rows(encoder, parts)
        pieces, decoder = lax.optimization_barrier((pieces, decoder))
        weights = [pieces[0]] + [swapped(pieces[step], step) for step in interleaved(parts)]
    with jax.named_scope("decoder_weights"):
        near_rows, far_rows, ids = fetch_decoders(lists, counts, decoder, encoder.shape[1], parts)
        near_decoder, far_decoder = passed_along(near_rows, 1), passed_along(far_rows, 2)
        near_decoder, far_decoder = lax.optimization_barrier((near_decoder, far_decoder))

    with jax.named_scope("encode"):
        quarter = tiles // 4
        (sent_a,) = encode([2 * quarter], ids, enc_bias, x, weights, slots, tiles, 64)
        arrived_a = swapped(sent_a, 1)
        starts = [3 * quarter, 0, quarter]
        sent_b, kept_a, kept_b = encode(starts, ids, enc_bias, x, weights, slots, tiles, 1)
        arrived_b = swapped(sent_b, 1)
        step = 2
        while step < parts:
            kept_a, sent_a = merge(kept_a, arrived_a)
            kept_b, sent_b = merge(kept_b, arrived_b)
            arrived_a = swapped(sent_a, step)
            arrived_a, sent_b = lax.optimization_barrier((arrived_a, sent_b))
            arrived_b = swapped(sent_b, step)
            step *= 2
        own_a, own_b = activate(kept_a, arrived_a), activate(kept_b, arrived_b)
    with jax.named_scope("spread"):
        late_a = swapped(own_a, 1)
        far_a = passed_along(own_a, 2)
        late_b = swapped(own_b, 1)
        joined = join(own_b, late_a)
        late_b, far_a = lax.optimization_barrier((late_b, far_a))
        own = [own_a, own_b, late_a, late_b]
        far = [far_a] + [passed_along(piece, 2) for piece in (joined, late_b)]
    with jax.named_scope("decode"):
        first, rest = decode_early(ids, own + far[:1], decoder, far_decoder, tiles)
        first, rest, far[2] = lax.optimization_barrier((first, rest, far[2]))
        near = across_cores(choose(own, far))
        rest = decode_middle(rest, far[1:], far_decoder, latents, tiles)
        return decode_late([first, rest], near, near_decoder, latents, parts)[None]


def solution(mesh):
    placed = (
        P("layer", None, "latent"),
        P("layer", None, "latent"),
        P("layer", "latent"),
        P("layer", None, None, "latent"),
        P("layer", None, None),
        P("layer", None),
    )
    return jax.shard_map(
        shards, mesh=mesh, in_specs=placed, out_specs=P("layer", None, "latent"), check_vma=False
    )
```

```python
import functools

import jax
import jax.numpy as jnp
from jax import lax
from jax.experimental import pallas as pl
from jax.experimental.pallas import tpu as pltpu
from jax.sharding import PartitionSpec as P

VMEM = pl.BlockSpec(memory_space=pltpu.VMEM)
SMEM = pl.BlockSpec(memory_space=pltpu.SMEM)
ANY = pl.BlockSpec(memory_space=pl.ANY)
HBM = pl.BlockSpec(memory_space=pltpu.HBM)


def swapped(value, step):
    count = lax.axis_size("latent")
    return lax.ppermute(value, "latent", [(i, i ^ step) for i in range(count)])


def interleaved(parts):
    across = list(range(parts // 2, parts))
    within = list(range(1, parts // 2))
    return [step for pair in zip(across, within + [None]) for step in pair if step]


def passed_along(value, steps):
    count = lax.axis_size("layer")
    return lax.ppermute(value, "layer", [(i, i + steps) for i in range(count - steps)])


def across_cores(value):
    count = lax.axis_size("layer")
    return lax.ppermute(value, "layer", [(i, i ^ 1) for i in range(count)])


def small(name, megabytes=8):
    return dict(compiler_params=pltpu.CompilerParams(vmem_limit_bytes=megabytes << 20), name=name)


def held_tile(position, tiles, parts):
    each = tiles // parts
    number, half = position // each, parts // 2
    parity = lax.bitwise_and(lax.axis_index("latent"), 1)
    return (2 * (number % half) + (parity if number < half else 1 - parity)) * each + position % each


def fetch_rows_kernel(encoder_ref, *piece_refs):
    depth = piece_refs[0].shape[0]
    for step, piece in enumerate(piece_refs):
        first = pl.multiple_of(lax.bitwise_xor(lax.axis_index("latent"), step) * depth, depth)
        piece[...] = encoder_ref[pl.ds(first, depth), :]


def fetch_rows(encoder, parts):
    depth = encoder.shape[0] // parts
    return pl.pallas_call(
        fetch_rows_kernel,
        out_shape=[jax.ShapeDtypeStruct((depth, encoder.shape[1]), encoder.dtype)] * parts,
        in_specs=[VMEM],
        out_specs=[VMEM] * parts,
        **small("fetch_rows"),
    )(encoder)


def id_place(slot, tiles, features, width):
    each = features // width
    return slot // each * tiles, slice(slot % each * width, (slot % each + 1) * width)


def fetch_decoders_kernel(parts, width, lists_ref, counts_ref, decoder_ref, *refs):
    out_refs, ids = refs[:-1], refs[-1]
    _, latents, features = decoder_ref.shape
    slots, tiles = lists_ref.shape
    ids[...] = jnp.zeros_like(ids)
    for slot in range(slots):
        first, lanes = id_place(slot, tiles, features, width)
        for position in range(tiles):
            tile = held_tile(position, tiles, parts)
            block = jnp.where(slot < counts_ref[tile], lists_ref[slot, tile], -1).astype(jnp.float32)
            ids[first + position : first + position + 1, lanes] = jnp.full((1, width), block, jnp.float32)
    for number, out_ref in enumerate(out_refs):
        out_ref[:latents, :] = decoder_ref[number + 1]
        out_ref[latents:, :] = ids[...].astype(out_ref.dtype)


def fetch_decoders(lists, counts, decoder, width, parts):
    targets, latents, features = decoder.shape
    slots, tiles = lists.shape
    rows = -(-slots // (features // width)) * tiles
    rows += -rows % 16
    shape = jax.ShapeDtypeStruct((latents + rows, features), decoder.dtype)
    return pl.pallas_call(
        functools.partial(fetch_decoders_kernel, parts, width),
        out_shape=[shape] * (targets - 1) + [jax.ShapeDtypeStruct((rows, features), jnp.float32)],
        in_specs=[SMEM, SMEM, VMEM],
        out_specs=[VMEM] * targets,
        **small("fetch_decoders", 16),
    )(lists, counts, decoder)


def encode_kernel(parts, starts, tiles, ids_ref, bias_ref, x_ref, *refs):
    weight_refs, out_refs, partial = refs[:parts], refs[parts:-1], refs[-1]
    width = bias_ref.shape[1]
    count, slots, rows, _ = out_refs[0].shape
    held = [[held_tile(start + position, tiles, parts) for position in range(count)] for start in starts]
    taken = [x_ref[pl.ds(pl.multiple_of(tile * rows, rows), rows), :] for group in held for tile in group]
    taken = jnp.concatenate(taken, axis=0)
    sources = [0] + interleaved(parts)
    wide = min(parts, 4)
    for first in range(0, parts, wide):
        stacked = jnp.concatenate([ref[...] for ref in weight_refs[first : first + wide]], axis=1)
        product = jnp.dot(taken, stacked, preferred_element_type=jnp.float32)
        for number in range(wide):
            block = product[:, number * width : (number + 1) * width]
            partial[sources[first + number]] = block if first + number else block + bias_ref[...]
    blocks = [lax.bitwise_xor(lax.axis_index("latent"), source).astype(jnp.float32) for source in range(parts)]
    row = 0
    for start, out_ref in zip(starts, out_refs):
        for position in range(count):
            for slot in range(slots):
                first, lanes = id_place(slot, tiles, ids_ref.shape[1], width)
                first += start + position
                wanted = ids_ref[first : first + 1, lanes]
                kept = jnp.zeros((rows, width), jnp.float32)
                for source in range(parts):
                    kept = kept + jnp.where(wanted == blocks[source], 1.0, 0.0) * partial[source, row : row + rows, :]
                out_ref[position, slot] = kept.astype(out_ref.dtype)
            row += rows


def encode(starts, ids, bias, x, weights, slots, tiles, weight):
    parts = len(weights)
    tokens, depth = x.shape
    width = bias.shape[1]
    shape = (tiles // 4, slots, tokens // tiles, width)
    dtypes = [jnp.float32 if start < tiles // 2 else jnp.bfloat16 for start in starts]
    taken = tokens // 4 * len(starts)
    return pl.pallas_call(
        functools.partial(encode_kernel, parts, starts, tiles),
        out_shape=[jax.ShapeDtypeStruct(shape, dtype) for dtype in dtypes],
        in_specs=[VMEM] * (3 + parts),
        out_specs=[VMEM] * len(starts),
        scratch_shapes=[pltpu.VMEM((parts, taken, width), jnp.float32)],
        cost_estimate=pl.CostEstimate(
            flops=weight * 2 * taken * depth * parts * width,
            bytes_accessed=2 * (tokens * depth + depth * parts * width),
            transcendentals=0,
        ),
        **small("encode", 16),
    )(ids, bias, x, *weights)


def merge_kernel(kept_ref, arrived_ref, total_ref, sent_ref):
    total = kept_ref[...] + arrived_ref[...].astype(jnp.float32)
    total_ref[...] = total
    sent_ref[...] = total.astype(sent_ref.dtype)


def merge(kept, arrived):
    return pl.pallas_call(
        merge_kernel,
        out_shape=[jax.ShapeDtypeStruct(kept.shape, kept.dtype), jax.ShapeDtypeStruct(kept.shape, arrived.dtype)],
        in_specs=[VMEM] * 2,
        out_specs=[VMEM] * 2,
        **small("merge"),
    )(kept, arrived)


def activate_kernel(kept_ref, arrived_ref, act_ref):
    preact = kept_ref[...] + arrived_ref[...].astype(jnp.float32)
    act_ref[...] = jnp.maximum(preact, 0.0).astype(act_ref.dtype)


def activate(kept, arrived):
    return pl.pallas_call(
        activate_kernel,
        out_shape=jax.ShapeDtypeStruct(kept.shape, arrived.dtype),
        in_specs=[VMEM] * 2,
        out_specs=VMEM,
        **small("activate"),
    )(kept, arrived)


def choose_kernel(*refs):
    sources, out_ref = refs[:-1], refs[-1]
    count = sources[0].shape[0]
    odd = lax.bitwise_and(lax.axis_index("layer"), 1)

    @pl.when(odd == 0)
    def _():
        for number in range(4):
            out_ref[number * count : (number + 1) * count] = sources[number][...]

    @pl.when(odd == 1)
    def _():
        out_ref[:count] = sources[4][...]
        out_ref[count : 3 * count] = sources[5][...]
        out_ref[3 * count :] = sources[6][...]


def choose(own, far):
    shape = own[0].shape
    return pl.pallas_call(
        choose_kernel,
        out_shape=jax.ShapeDtypeStruct((4 * shape[0],) + shape[1:], own[0].dtype),
        in_specs=[VMEM] * 7,
        out_specs=VMEM,
        **small("choose"),
    )(*own, *far)


def join_kernel(first_ref, second_ref, out_ref):
    count = first_ref.shape[0]
    out_ref[:count] = first_ref[...]
    out_ref[count:] = second_ref[...]


def join(first, second):
    return pl.pallas_call(
        join_kernel,
        out_shape=jax.ShapeDtypeStruct((2 * first.shape[0],) + first.shape[1:], first.dtype),
        in_specs=[VMEM] * 2,
        out_specs=VMEM,
        **small("join"),
    )(first, second)


def expand(dense, ids_ref, tiles, first, act_refs):
    row = 0
    for act_ref in act_refs:
        count, slots, rows, width = act_ref.shape
        for position in range(count):
            wanted = []
            for slot in range(slots):
                start, lanes = id_place(slot, tiles, ids_ref.shape[1], width)
                start += first + position
                wanted.append(ids_ref[start : start + 1, lanes])
            for block in range(dense.shape[1] // width):
                total = None
                for slot in range(slots):
                    chosen = jnp.where(wanted[slot] == block, 1.0, 0.0).astype(dense.dtype)
                    term = act_ref[position, slot] * chosen
                    total = term if total is None else total + term
                dense[row : row + rows, block * width : (block + 1) * width] = total
            row += rows
        first += count


def column_tiles(features):
    columns = 512 if features % 512 == 0 else features
    return [slice(first, first + columns) for first in range(0, features, columns)]


def early_kernel(tiles, ids_ref, *refs):
    own_refs, far_ref, (decoder_hbm, far_dec), refs = refs[:4], refs[4], refs[5:7], refs[7:]
    first_ref, rest_ref, own, other, own_dec, far_ids, sem = refs
    copy = pltpu.make_async_copy(decoder_hbm.at[0], own_dec, sem)
    copy.start()
    quarter, latents = other.shape
    far_ids[...] = far_dec[latents:, :].astype(far_ids.dtype)
    expand(own, ids_ref, tiles, 0, own_refs)
    expand(other, far_ids, tiles, 0, [far_ref])
    copy.wait()
    for lanes in column_tiles(first_ref.shape[1]):
        total = jnp.dot(own[...], own_dec[:, lanes], preferred_element_type=jnp.float32)
        rest_ref[:, lanes] = total[quarter:]
        first_ref[:, lanes] = total[:quarter] + jnp.dot(
            other[...], far_dec[:latents, lanes], preferred_element_type=jnp.float32
        )


def decode_early(ids, acts, decoder, far_decoder, tiles):
    _, latents, features = decoder.shape
    quarter = acts[0].shape[0] * acts[0].shape[2]
    return pl.pallas_call(
        functools.partial(early_kernel, tiles),
        out_shape=[jax.ShapeDtypeStruct((count * quarter, features), jnp.float32) for count in (1, 3)],
        in_specs=[VMEM] * 6 + [ANY, VMEM],
        out_specs=[VMEM] * 2,
        scratch_shapes=[
            pltpu.VMEM((4 * quarter, latents), jnp.bfloat16),
            pltpu.VMEM((quarter, latents), jnp.bfloat16),
            pltpu.VMEM((latents, features), jnp.bfloat16),
            pltpu.VMEM(ids.shape, jnp.float32),
            pltpu.SemaphoreType.DMA,
        ],
        cost_estimate=pl.CostEstimate(
            flops=10 * quarter * latents * features,
            bytes_accessed=2 * (2 * latents * features + 8 * quarter * features),
            transcendentals=0,
        ),
        **small("decode_early", 16),
    )(ids, *acts, decoder, far_decoder)


def middle_kernel(tiles, rest_ref, second, third, far_dec, total_ref, dense, ids):
    latents = dense.shape[1]
    ids[...] = far_dec[latents:, :].astype(ids.dtype)
    expand(dense, ids, tiles, third.shape[0], [second, third])
    for lanes in column_tiles(rest_ref.shape[1]):
        total_ref[:, lanes] = rest_ref[:, lanes] + jnp.dot(
            dense[...], far_dec[:latents, lanes], preferred_element_type=jnp.float32
        )


def decode_middle(rest, far, decoder, latents, tiles):
    rows, features = rest.shape
    return pl.pallas_call(
        functools.partial(middle_kernel, tiles),
        out_shape=jax.ShapeDtypeStruct(rest.shape, rest.dtype),
        in_specs=[VMEM] * 4,
        out_specs=VMEM,
        scratch_shapes=[
            pltpu.VMEM((rows, latents), jnp.bfloat16),
            pltpu.VMEM((decoder.shape[0] - latents, features), jnp.float32),
        ],
        cost_estimate=pl.CostEstimate(
            flops=2 * rows * latents * features,
            bytes_accessed=2 * (latents * features + 4 * rows * features),
            transcendentals=0,
        ),
        **small("decode_middle", 16),
    )(rest, *far, decoder)


def late_kernel(parts, tiles, first_ref, rest_ref, near, near_dec, out_ref, dense, stage, ids, sems):
    tokens, latents = dense.shape
    quarter, rows = tokens // 4, tokens // parts
    ids[...] = near_dec[latents:, :].astype(ids.dtype)
    expand(dense, ids, tiles, 0, [near])
    copies = []
    for number, lanes in enumerate(column_tiles(first_ref.shape[1])):
        total = jnp.dot(dense[...], near_dec[:latents, lanes], preferred_element_type=jnp.float32)
        stage[:quarter, lanes] = (total[:quarter] + first_ref[:, lanes]).astype(stage.dtype)
        stage[quarter:, lanes] = (total[quarter:] + rest_ref[:, lanes]).astype(stage.dtype)
        for held in range(parts):
            row = pl.multiple_of(held_tile(held * (tiles // parts), tiles, parts) * (tokens // tiles), rows)
            copies.append(
                pltpu.make_async_copy(
                    stage.at[held * rows : (held + 1) * rows, lanes],
                    out_ref.at[pl.ds(row, rows), lanes],
                    sems.at[number, held],
                )
            )
            copies[-1].start()
    for copy in copies:
        copy.wait()


def decode_late(partials, near, decoder, latents, parts):
    features = decoder.shape[1]
    tokens = near.shape[0] * near.shape[2]
    return pl.pallas_call(
        functools.partial(late_kernel, parts, near.shape[0]),
        out_shape=jax.ShapeDtypeStruct((tokens, features), jnp.bfloat16),
        in_specs=[VMEM] * 4,
        out_specs=ANY,
        scratch_shapes=[
            pltpu.VMEM((tokens, latents), jnp.bfloat16),
            pltpu.VMEM((tokens, features), jnp.bfloat16),
            pltpu.VMEM((decoder.shape[0] - latents, features), jnp.float32),
            pltpu.SemaphoreType.DMA((len(column_tiles(features)), parts)),
        ],
        cost_estimate=pl.CostEstimate(
            flops=2 * tokens * latents * features,
            bytes_accessed=2 * (latents * features + 3 * tokens * features),
            transcendentals=0,
        ),
        **small("decode_late", 16),
    )(*partials, near, decoder)


def shards(layer_input, enc_weight, enc_bias, dec_weight, block_lists, block_counts):
    parts = lax.axis_size("latent")
    x, encoder, decoder = layer_input[0], enc_weight[0], dec_weight[0]
    lists, counts = block_lists[0].T, block_counts[0]
    slots, tiles = lists.shape
    targets, latents, _ = decoder.shape
    if targets != 3 or parts < 2 or parts & (parts - 1) or tiles % 4:
        raise ValueError("mesh")

    with jax.named_scope("encoder_rows"):
        pieces = fetch_rows(encoder, parts)
        pieces, decoder = lax.optimization_barrier((pieces, decoder))
        weights = [pieces[0]] + [swapped(pieces[step], step) for step in interleaved(parts)]
    with jax.named_scope("decoder_weights"):
        near_rows, far_rows, ids = fetch_decoders(lists, counts, decoder, encoder.shape[1], parts)
        far_decoder, near_decoder = passed_along(far_rows, 2), passed_along(near_rows, 1)
        far_decoder, near_decoder = lax.optimization_barrier((far_decoder, near_decoder))

    with jax.named_scope("encode"):
        quarter = tiles // 4
        (sent_a,) = encode([2 * quarter], ids, enc_bias, x, weights, slots, tiles, 64)
        arrived_a = swapped(sent_a, 1)
        starts = [3 * quarter, 0, quarter]
        sent_b, kept_a, kept_b = encode(starts, ids, enc_bias, x, weights, slots, tiles, 1)
        arrived_b = swapped(sent_b, 1)
        step = 2
        while step < parts:
            kept_a, sent_a = merge(kept_a, arrived_a)
            kept_b, sent_b = merge(kept_b, arrived_b)
            arrived_a = swapped(sent_a, step)
            arrived_a, sent_b = lax.optimization_barrier((arrived_a, sent_b))
            arrived_b = swapped(sent_b, step)
            step *= 2
        own_a, own_b = activate(kept_a, arrived_a), activate(kept_b, arrived_b)
    with jax.named_scope("spread"):
        late_a = swapped(own_a, 1)
        far_a = passed_along(own_a, 2)
        late_b = swapped(own_b, 1)
        joined = join(own_b, late_a)
        late_b, far_a = lax.optimization_barrier((late_b, far_a))
        own = [own_a, own_b, late_a, late_b]
        far = [far_a] + [passed_along(piece, 2) for piece in (joined, late_b)]
    with jax.named_scope("decode"):
        first, rest = decode_early(ids, own + far[:1], decoder, far_decoder, tiles)
        first, rest, far[2] = lax.optimization_barrier((first, rest, far[2]))
        near = across_cores(choose(own, far))
        rest = decode_middle(rest, far[1:], far_decoder, latents, tiles)
        return decode_late([first, rest], near, near_decoder, latents, parts)[None]


def solution(mesh):
    placed = (
        P("layer", None, "latent"),
        P("layer", None, "latent"),
        P("layer", "latent"),
        P("layer", None, None, "latent"),
        P("layer", None, None),
        P("layer", None),
    )
    return jax.shard_map(
        shards, mesh=mesh, in_specs=placed, out_specs=P("layer", None, "latent"), check_vma=False
    )
```
